32 devices in a mesh: dp: 8 (over z, y), tensor: 4 (over x, core).
Axes of the slice: x: 2, y: 2, z: 4, core: 2. Of those that a mesh axis runs over, the one named last changes fastest.
Arguments:
- embedded: bfloat16 [18912, 768], P('dp'), may hold values from -6 to 6
- attn_gain: bfloat16 [768], replicated, may hold values from 0.5 to 1.5
- attn_shift: bfloat16 [768], replicated, may hold values from -1 to 1
- qkv_weight: bfloat16 [3, 768, 768], P(None, None, 'tensor'), may hold values from -0.21875 to 0.21875
- qv_bias: bfloat16 [2, 768], P(None, 'tensor'), may hold values from -1 to 1
- out_weight: bfloat16 [768, 768], P('tensor'), may hold values from -1.25 to 1.25
- out_bias: bfloat16 [768], replicated, may hold values from -0.59765625 to 0.59765625
- moe_gain: bfloat16 [768], replicated, may hold values from 0.5 to 1.5
- moe_shift: bfloat16 [768], replicated, may hold values from -1 to 1
- router_weight: bfloat16 [768, 8], replicated, may hold values from -0.15625 to 0.15625
- up_weight: bfloat16 [8, 768, 3072], P(None, None, 'tensor'), may hold values from -0.21875 to 0.21875
- up_bias: bfloat16 [8, 3072], P(None, 'tensor'), may hold values from -0.59765625 to 0.59765625
- down_weight: bfloat16 [8, 3072, 768], P(None, 'tensor'), may hold values from -0.5 to 0.5
- down_bias: bfloat16 [8, 768], replicated, may hold values from -3 to 3
- routes: int32 [18912, 2], P('dp'), may hold values from 0 to 7, all different within a row; in each aligned block of 2364 rows (0 to 2363, 2364 to 4727, ...) at most 768 rows name the same one
- cotangent: bfloat16 [18912, 768], P('dp'), may hold values from -6 to 6
Outputs:
- layer_out: bfloat16 [18912, 768], P('dp')
- grad_embedded: float32 [18912, 768], P('dp')
- grad_attn_gain: float32 [768], replicated
- grad_attn_shift: float32 [768], replicated
- grad_qkv_weight: float32 [3, 768, 768], P(None, 'dp', 'tensor')
- grad_qv_bias: float32 [2, 768], P(None, 'tensor')
- grad_out_weight: float32 [768, 768], P('tensor', 'dp')
- grad_out_bias: float32 [768], replicated
- grad_moe_gain: float32 [768], replicated
- grad_moe_shift: float32 [768], replicated
- grad_router_weight: float32 [768, 8], replicated
- grad_up_weight: float32 [8, 768, 3072], P(None, 'dp', 'tensor')
- grad_up_bias: float32 [8, 3072], P(None, 'tensor')
- grad_down_weight: float32 [8, 3072, 768], P(None, 'tensor', 'dp')
- grad_down_bias: float32 [8, 768], replicated
The draws below stay inside these ranges and needn't reach their ends.
Inputs may be any that keep to these rules, and one draw needn't show every extreme that they name: `routes`: each token names 2 different experts; among the rows of one device no expert is named more than 768 times, and in every draw some expert is named exactly 768 times among some device's rows.
All inputs are finite; a program needn't handle non-finite values.
Results may differ from the reference program's by a relative error of at most 0.028.
Values may be sent and summed in bfloat16 or wider, within the bound.
No kernel may reach another device: no remote copies, remote signals or barrier semaphores. Data moves between devices by JAX's collectives and lax.ppermute only.
A program may use at most 256 MiB of HBM per device.

```python
import math
import jax
import jax.numpy as jnp
import numpy as np
from jax import lax

D = 768
HEADS = 12
FF = 3072
E = 8
TOP = 2
SEQ = 197
IMG_DEV = 12
HD = 64
TOK_DEV = 2364
TOKENS = 18912
CAP = 768
N_DP = 8
N_TENSOR = 4


def raised(values, rng, source, target, blocks, factor):
    def block_of(position):
        return (jnp.arange(values.shape[position]) // (values.shape[position] // blocks)).reshape((-1,) + (1,) * (values.ndim - 1 - position))

    near = jax.random.permutation(rng, blocks)[block_of(target)]
    far = (block_of(target) + blocks // 2) % blocks
    return jnp.where((block_of(source) == near) | (block_of(source) == far), factor * values, values)


def block_scale(own_key, dims, split, least, top_value):
    loudness, own = 1.0, jax.random.fold_in(own_key, 6)
    for dim, shards_of in split:
        steps = jnp.exp(jax.random.uniform(jax.random.fold_in(own, dim), (shards_of,), jnp.float32, least / len(split), top_value / len(split)))
        loudness = loudness * jnp.repeat(steps, dims[dim] // shards_of).reshape([-1 if axis == dim else 1 for axis in range(len(dims))])
    return loudness


def assign_block(stream_key, own, number, rows, count, top, most, slope):
    ranking = jax.random.permutation(stream_key, count)
    heavy_load, common = portions_of(count, rows * top, most, slope, True), portions_of(count, rows * top, most, slope, False)
    places = jnp.arange(count)

    def named(lengths, offset_by):
        used = int((lengths > 0).sum())
        fixed = max(1, used // 4)
        moved = fixed + (places - fixed + offset_by * (used - fixed)) % max(1, count - fixed)
        return jnp.zeros((count,), jnp.int32).at[ranking[jnp.where(places < fixed, places, moved)]].set(jnp.asarray(lengths, jnp.int32))

    lengths = jnp.where(number % 4 == 0, named(heavy_load, number // 4), named(common, number - number // 4 - 1))
    mixed = jax.random.permutation(jax.random.fold_in(own, 3), count)
    source_of, taker = mixed[0:count // 2 * 2:2], mixed[1:count // 2 * 2:2]
    room = jnp.minimum(lengths[source_of] - 1, most - lengths[taker]) // 2
    room = jnp.where((source_of == ranking[0]) | (taker == ranking[0]) | (lengths[taker] == 0), 0, jnp.maximum(room, 0))
    moved = jax.random.randint(jax.random.fold_in(own, 4), (count // 2,), 0, 1 << 20) % (room + 1)
    lengths = lengths.at[source_of].add(-moved).at[taker].add(moved)
    labels = jnp.searchsorted(jnp.cumsum(lengths), jnp.arange(rows * top), side="right").astype(jnp.int32)
    grid = labels.reshape(top, rows).T
    grid = grid[jax.random.permutation(jax.random.fold_in(own, 1), rows)]
    offset_by = jax.random.randint(jax.random.fold_in(own, 2), (rows, 1), 0, top)
    return jnp.take_along_axis(grid, (jnp.arange(top)[None, :] + offset_by) % top, axis=1)


def portions_of(count, total, bound, lean, full):
    loads = [(1 << 20) // math.isqrt(standing ** lean) + 1 for standing in range(1, count + 1)]
    largest = bound if full else min(bound, max(-(-total // count), total * loads[0] // sum(loads)))
    least = 1 if total - largest >= count - 1 else 0
    counts, rest = [largest] + [least] * (count - 1), total - largest - least * (count - 1)
    while rest > 0:
        movable = [i for i in range(1, count) if counts[i] < largest] or [i for i in range(1, count) if counts[i] < bound]
        whole, budget = sum([loads[i] for i in movable]), rest
        for i in movable:
            addition = min(bound - counts[i], max(1, budget * loads[i] // whole), rest)
            counts[i] = counts[i] + addition
            rest = rest - addition
    return np.array(counts)


def centred(own_key, extent, width, reach, pieces=(), kind=jnp.bfloat16):
    entries = width * jax.random.normal(own_key, extent, jnp.float32)
    if pieces:
        entries = entries * block_scale(own_key, extent, pieces, -0.22, 0.18)
    return jnp.clip(entries, -reach, reach).astype(kind)


def gaussian_with(key, dims, deviation, limit, shards, heavy, kind=jnp.bfloat16):
    entries = deviation * jax.random.normal(key, dims, jnp.float32)
    if shards:
        entries = entries * block_scale(key, dims, shards, -0.22, 0.18)
    return jnp.clip(raised(entries, jax.random.fold_in(key, 3), *heavy), -limit, limit).astype(kind)


def setup_inputs(seed: int = 0) -> dict:
    keys = jax.random.split(jax.random.key(seed), 17)
    embedded = centred(keys[0], (TOKENS, D), 1.0, 6.0, ((0, 8),))
    attn_gain = jnp.clip(1.0 + 0.1 * jax.random.normal(keys[1], (D,), jnp.float32), 0.5, 1.5).astype(jnp.bfloat16)
    attn_shift = centred(keys[2], (D,), 0.2, 1.0)
    qkv_weight = centred(keys[3], (3, D, D), D ** -0.5, 0.21875, ((2, 4),))
    qv_bias = centred(keys[4], (2, D), 0.2, 1.0, ((1, 4),))
    out_weight = centred(keys[5], (D, D), (D // 32) ** -0.5, 1.25, ((0, 4),))
    out_bias = centred(keys[6], (D,), 0.1, 0.59765625)
    moe_gain = jnp.clip(1.0 + 0.1 * jax.random.normal(keys[7], (D,), jnp.float32), 0.5, 1.5).astype(jnp.bfloat16)
    moe_shift = centred(keys[8], (D,), 0.2, 1.0)
    router_weight = centred(keys[9], (D, E), (2 * D) ** -0.5, 0.15625)
    up_weight = centred(keys[10], (E, D, FF), D ** -0.5, 0.21875, ((2, 4),))
    up_bias = centred(keys[11], (E, FF), 0.1, 0.59765625, ((1, 4),))
    down_weight = centred(keys[12], (E, FF, D), (FF // 24) ** -0.5, 0.5, ((1, 4),))
    down_bias = centred(keys[13], (E, D), 0.5, 3.0)
    routes_keys = jax.random.split(jax.random.fold_in(keys[14], 1), TOKENS // TOK_DEV)
    routes_turns = jax.random.permutation(jax.random.fold_in(keys[14], 3), TOKENS // TOK_DEV)
    routes = jax.vmap(lambda own, number: assign_block(jax.random.fold_in(keys[14], 2), own, number, TOK_DEV, E, TOP, CAP, 1))(routes_keys, routes_turns).reshape((TOKENS, TOP))
    cotangent = gaussian_with(keys[15], (TOKENS, D), 1.0, 6.0, ((0, 8),), (0, 1, 8, 2.0))
    return dict(embedded=embedded, attn_gain=attn_gain, attn_shift=attn_shift, qkv_weight=qkv_weight, qv_bias=qv_bias, out_weight=out_weight, out_bias=out_bias, moe_gain=moe_gain, moe_shift=moe_shift, router_weight=router_weight, up_weight=up_weight, up_bias=up_bias, down_weight=down_weight, down_bias=down_bias, routes=routes, cotangent=cotangent)


@jax.custom_vjp
def low(v):
    return lax.optimization_barrier(v.astype(jnp.bfloat16)).astype(jnp.float32)

@jax.custom_vjp
def low_back(v):
    return v

def low_keep(v):
    return (low(v), None)

def low_pass(kept, grad):
    return (grad,)

def back_keep(v):
    return (v, None)

def back_low(kept, grad):
    return (low(grad),)
low.defvjp(low_keep, low_pass)
low_back.defvjp(back_keep, back_low)
EPSILON = 1e-06

def matmul(left, right):
    return jnp.dot(left, right, precision=lax.Precision.HIGHEST, preferred_element_type=jnp.float32)

def layer_norm(inputs, gain_vec, shift_vec):
    row_mean = lax.optimization_barrier(jnp.mean(inputs, axis=-1, keepdims=True))
    centered = inputs - row_mean
    row_var = lax.optimization_barrier(jnp.mean(centered * centered, axis=-1, keepdims=True))
    return centered * lax.rsqrt(row_var + EPSILON) * gain_vec + shift_vec

def attention_group(group_rows, qkv_weight, qv_bias, out_weight, out_bias):
    head_width = D // N_TENSOR
    heads_each = HEADS // N_TENSOR
    head_shape = (IMG_DEV, SEQ, heads_each, HD)
    running = jnp.zeros(group_rows.shape, jnp.float32) + out_bias
    for shard_index in range(N_TENSOR):
        first_col = shard_index * head_width
        last_col = first_col + head_width
        copied = low_back(group_rows)
        queries = low_back(low(matmul(copied, qkv_weight[0][:, first_col:last_col]) + qv_bias[0, first_col:last_col]))
        key_rows = low_back(low(matmul(copied, qkv_weight[1][:, first_col:last_col])))
        value_rows = low_back(low(matmul(copied, qkv_weight[2][:, first_col:last_col]) + qv_bias[1, first_col:last_col]))
        scores = jnp.einsum('bqhd,bkhd->bhqk', queries.reshape(head_shape), key_rows.reshape(head_shape), precision=lax.Precision.HIGHEST) * HD ** (-0.5)
        scores = low_back(scores)
        attn_probs = jax.nn.softmax(scores, axis=-1)
        mixed_heads = jnp.einsum('bhqk,bkhd->bqhd', low(attn_probs), value_rows.reshape(head_shape), precision=lax.Precision.HIGHEST)
        mixed_heads = low_back(low(mixed_heads.reshape(TOK_DEV, head_width)))
        running = running + low(matmul(mixed_heads, out_weight[first_col:last_col, :]))
    return low_back(running)

def expert_part(copied, up_slice, up_bias_slice, down_slice, column):
    hidden_pre = low_back(matmul(copied, up_slice) + up_bias_slice)
    hidden = low(jax.nn.gelu(hidden_pre))
    return column * low_back(matmul(hidden, down_slice))

def forward(embedded, attn_gain, attn_shift, qkv_weight, qv_bias, out_weight, out_bias, moe_gain, moe_shift, router_weight, up_weight, up_bias, down_weight, down_bias, route_mask):
    normed = low(layer_norm(embedded, attn_gain, attn_shift))
    grouped = normed.reshape(N_DP, TOK_DEV, D)

    def one_group(group_rows):
        return attention_group(group_rows, qkv_weight, qv_bias, out_weight, out_bias)
    attn_out = lax.map(jax.checkpoint(one_group), grouped).reshape(TOKENS, D)
    middle = embedded + attn_out
    moe_normed = low(layer_norm(middle, moe_gain, moe_shift))
    logits = low_back(matmul(moe_normed, router_weight))
    gate_probs = jax.nn.softmax(logits, axis=-1)
    mixing = gate_probs * route_mask
    hidden_width = FF // N_TENSOR
    branch = matmul(mixing, down_bias)
    checked = jax.checkpoint(expert_part)
    for shard_index in range(N_TENSOR):
        first_col = shard_index * hidden_width
        last_col = first_col + hidden_width
        copied = low_back(moe_normed)
        partial_sum = jnp.zeros((TOKENS, D), jnp.float32)
        for expert in range(E):
            partial_sum = partial_sum + checked(copied, up_weight[expert][:, first_col:last_col], up_bias[expert, first_col:last_col], down_weight[expert][first_col:last_col, :], mixing[:, expert:expert + 1])
        branch = branch + low(partial_sum)
    return middle + low_back(branch)

def reference(embedded, attn_gain, attn_shift, qkv_weight, qv_bias, out_weight, out_bias, moe_gain, moe_shift, router_weight, up_weight, up_bias, down_weight, down_bias, routes, cotangent):
    float_args = [embedded, attn_gain, attn_shift, qkv_weight, qv_bias, out_weight, out_bias, moe_gain, moe_shift, router_weight, up_weight, up_bias, down_weight, down_bias]
    float_args = [item.astype(jnp.float32) for item in float_args]
    route_mask = lax.optimization_barrier(jnp.sum(jax.nn.one_hot(routes, E, dtype=jnp.float32), axis=1))

    def closed(*inputs):
        return forward(*inputs, route_mask)
    result, pullback = jax.vjp(closed, *float_args)
    gradients = pullback(cotangent.astype(jnp.float32))
    return (result.astype(jnp.bfloat16), gradients[0], gradients[1], gradients[2], gradients[3], gradients[4], gradients[5], gradients[6], gradients[7], gradients[8], gradients[9], gradients[10], gradients[11], gradients[12], gradients[13])
```

```python
import jax
import jax.numpy as jnp
from jax import lax
from jax.sharding import PartitionSpec as P

TOP = 2
SEQ = 197
HD = 64
CAP = 768


EPSILON = 1e-06
HIGHEST = lax.Precision.HIGHEST


def layer_norm(inputs, gain_vec, shift_vec):
    row_mean = jnp.mean(inputs, axis=-1, keepdims=True)
    centered = inputs - row_mean
    row_var = jnp.mean(centered * centered, axis=-1, keepdims=True)
    return centered * lax.rsqrt(row_var + EPSILON) * gain_vec + shift_vec


RING = (0, 2, 4, 6, 7, 5, 3, 1)


def pairs(count, bit):
    return [(i, i ^ bit) for i in range(count)]


def tensor_sum(part):
    if lax.axis_size("tensor") != 4:
        return lax.psum(part, "tensor").astype(jnp.float32)
    rows, cols = part.shape
    half = cols // 2
    core = lax.axis_index("tensor") % 2
    theirs = lax.dynamic_slice(part, (0, (1 - core) * half), (rows, half))
    mine = lax.dynamic_slice(part, (0, core * half), (rows, half))
    got = lax.ppermute(theirs, "tensor", pairs(4, 1))
    both = (mine.astype(jnp.float32) + got.astype(jnp.float32)).astype(jnp.bfloat16)
    far = lax.ppermute(both, "tensor", pairs(4, 2))
    total = (both.astype(jnp.float32) + far.astype(jnp.float32)).astype(jnp.bfloat16)
    other = lax.ppermute(total, "tensor", pairs(4, 1))
    low = jnp.where(core == 0, total, other)
    high = jnp.where(core == 0, other, total)
    return jnp.concatenate([low, high], axis=1).astype(jnp.float32)


def small_sum(values, axis):
    count = lax.axis_size(axis)
    if count not in (4, 8):
        return lax.psum(values, axis)
    bit = 1
    while bit < count:
        values = values + lax.ppermute(values, axis, pairs(count, bit))
        bit *= 2
    return values


def ring_scatter(values, way):
    count = lax.axis_size("dp")
    if count != 8:
        return lax.psum_scatter(values, "dp", scatter_dimension=1, tiled=True).astype(jnp.float32)
    chunk = values.shape[1] // count
    order = jnp.array(RING, jnp.int32)
    place = jnp.array([RING.index(i) for i in range(count)], jnp.int32)[lax.axis_index("dp")]
    path = [(RING[i], RING[(i + way) % count]) for i in range(count)]

    def local(step):
        owner = order[(place - way * (step + 1)) % count]
        start = (0, owner * chunk, 0)
        return lax.dynamic_slice(values, start, (values.shape[0], chunk, values.shape[2]))

    moving = local(0)
    for step in range(1, count):
        got = lax.ppermute(moving, "dp", path)
        total = got.astype(jnp.float32) + local(step).astype(jnp.float32)
        moving = total.astype(jnp.bfloat16) if step < count - 1 else total
    return moving


def on_device(
    embedded,
    attn_gain,
    attn_shift,
    qkv_weight,
    qv_bias,
    out_weight,
    out_bias,
    moe_gain,
    moe_shift,
    router_weight,
    up_weight,
    up_bias,
    down_weight,
    down_bias,
    routes,
    cotangent,
):
    tok_rows = embedded.shape[0]
    images = tok_rows // SEQ
    head_width = qkv_weight.shape[2]
    heads_here = head_width // HD
    expert_count = up_weight.shape[0]
    score_scale = HD ** (-0.5)
    embedded_f = embedded.astype(jnp.float32)
    attn_norm, attn_norm_back = jax.vjp(
        layer_norm, embedded_f, attn_gain.astype(jnp.float32), attn_shift.astype(jnp.float32)
    )
    normed = attn_norm.astype(jnp.bfloat16)
    bias_rows = jnp.stack([qv_bias[0], jnp.zeros_like(qv_bias[0]), qv_bias[1]]).astype(jnp.float32)
    projected = (
        jnp.einsum("td,cdh->cth", normed, qkv_weight, preferred_element_type=jnp.float32)
        + bias_rows[:, None, :]
    )
    projected = projected.astype(jnp.bfloat16)
    queries, key_rows, value_rows = projected.reshape(3, images, SEQ, heads_here, HD)
    scores = (
        jnp.einsum("bqhd,bkhd->bhqk", queries, key_rows, preferred_element_type=jnp.float32)
        * score_scale
    )
    top_score = jnp.max(scores, axis=-1, keepdims=True)
    log_total = top_score + jnp.log(jnp.sum(jnp.exp(scores - top_score), axis=-1, keepdims=True))
    probs_low = jnp.exp(scores - log_total).astype(jnp.bfloat16)
    mixed_heads = jnp.einsum(
        "bhqk,bkhd->bqhd", probs_low, value_rows, preferred_element_type=jnp.float32
    )
    mixed_low = mixed_heads.astype(jnp.bfloat16).reshape(tok_rows, head_width)
    attn_part = jnp.dot(mixed_low, out_weight, preferred_element_type=jnp.float32)
    attn_total = tensor_sum(attn_part.astype(jnp.bfloat16))
    middle = embedded_f + attn_total + out_bias.astype(jnp.float32)
    moe_norm, moe_norm_back = jax.vjp(
        layer_norm, middle, moe_gain.astype(jnp.float32), moe_shift.astype(jnp.float32)
    )
    moe_normed = moe_norm.astype(jnp.bfloat16)
    logits = jnp.dot(moe_normed, router_weight, preferred_element_type=jnp.float32)
    gate_probs = jax.nn.softmax(logits, axis=-1)
    choose = (
        routes[:, :, None] == jnp.arange(expert_count, dtype=jnp.int32)[None, None, :]
    ).astype(jnp.float32)
    mixing = gate_probs * jnp.sum(choose, axis=1)
    picked = jnp.sum(gate_probs[:, None, :] * choose, axis=-1)
    flat_expert = routes.reshape(-1)
    route_hot = choose.reshape(-1, expert_count).astype(jnp.int32)
    before = jnp.cumsum(route_hot, axis=0) - route_hot
    slot_index = jnp.sum(before * route_hot, axis=1)
    target = flat_expert * CAP + slot_index
    route_count = flat_expert.shape[0]
    route_of_slot = (
        jnp.full((expert_count * CAP,), route_count, jnp.int32)
        .at[target]
        .set(jnp.arange(route_count, dtype=jnp.int32))
    )
    token_of_slot = route_of_slot // TOP
    padded = jnp.concatenate(
        [moe_normed, jnp.zeros((1, moe_normed.shape[1]), jnp.bfloat16)], axis=0
    )
    buffers = padded[token_of_slot].reshape(expert_count, CAP, moe_normed.shape[1])
    pre_act = (
        jnp.einsum("ecd,edf->ecf", buffers, up_weight, preferred_element_type=jnp.float32)
        + up_bias.astype(jnp.float32)[:, None, :]
    )
    activated, gelu_back = jax.vjp(jax.nn.gelu, pre_act)
    activated_low = activated.astype(jnp.bfloat16)
    expert_out = jnp.einsum(
        "ecf,efd->ecd", activated_low, down_weight, preferred_element_type=jnp.float32
    )
    route_out = expert_out.reshape(expert_count * CAP, -1)[target].reshape(tok_rows, TOP, -1)
    moe_part = jnp.sum(picked[:, :, None] * route_out, axis=1)
    moe_total = tensor_sum(moe_part.astype(jnp.bfloat16))
    down_bias_f = down_bias.astype(jnp.float32)
    layer_out = middle + moe_total + jnp.dot(mixing, down_bias_f, precision=HIGHEST)
    upstream = cotangent.astype(jnp.float32)
    grad_down_bias = jnp.dot(mixing.T, upstream, precision=HIGHEST)
    bias_dot = jnp.dot(cotangent, down_bias.T, preferred_element_type=jnp.float32)
    route_dot_part = jnp.sum(route_out * upstream[:, None, :], axis=-1)
    route_dot = small_sum(route_dot_part, "tensor")
    grad_picked = route_dot + jnp.sum(bias_dot[:, None, :] * choose, axis=-1)
    grad_gates = jnp.sum(choose * grad_picked[:, :, None], axis=1)
    grad_logits = gate_probs * (
        grad_gates - jnp.sum(gate_probs * grad_gates, axis=-1, keepdims=True)
    )
    grad_logits_low = grad_logits.astype(jnp.bfloat16)
    grad_router = lax.dot_general(
        moe_normed, grad_logits_low, (((0,), (0,)), ((), ())), preferred_element_type=jnp.float32
    )
    router_back = lax.dot_general(
        grad_logits_low, router_weight, (((1,), (1,)), ((), ())), preferred_element_type=jnp.float32
    )
    route_grad = (
        (picked[:, :, None] * upstream[:, None, :]).astype(jnp.bfloat16).reshape(route_count, -1)
    )
    route_grad_pad = jnp.concatenate(
        [route_grad, jnp.zeros((1, route_grad.shape[1]), jnp.bfloat16)], axis=0
    )
    slot_grad = route_grad_pad[route_of_slot].reshape(expert_count, CAP, -1)
    grad_down = jnp.einsum(
        "ecf,ecd->edf", activated_low, slot_grad, preferred_element_type=jnp.float32
    )
    hidden_grad = jnp.einsum(
        "ecd,efd->ecf", slot_grad, down_weight, preferred_element_type=jnp.float32
    )
    pre_grad = gelu_back(hidden_grad)[0].astype(jnp.bfloat16)
    grad_up_bias = jnp.sum(pre_grad, axis=1, dtype=jnp.float32)
    grad_up = jnp.einsum("ecd,ecf->edf", buffers, pre_grad, preferred_element_type=jnp.float32)
    slot_back = jnp.einsum("ecf,edf->ecd", pre_grad, up_weight, preferred_element_type=jnp.float32)
    back_part = jnp.sum(
        slot_back.reshape(expert_count * CAP, -1)[target].reshape(tok_rows, TOP, -1), axis=1
    )
    back_total = tensor_sum(back_part.astype(jnp.bfloat16))
    normed2_grad = back_total + router_back
    middle_grad_ln, grad_moe_gain, grad_moe_shift = moe_norm_back(normed2_grad)
    middle_grad = upstream + middle_grad_ln
    attn_grad = middle_grad.astype(jnp.bfloat16)
    grad_out_bias = jnp.sum(attn_grad, axis=0, dtype=jnp.float32)
    grad_out = lax.dot_general(
        mixed_low, attn_grad, (((0,), (0,)), ((), ())), preferred_element_type=jnp.float32
    )
    mixed_grad = lax.dot_general(
        attn_grad, out_weight, (((1,), (1,)), ((), ())), preferred_element_type=jnp.float32
    )
    mixed_grad = mixed_grad.astype(jnp.bfloat16).reshape(images, SEQ, heads_here, HD)
    scores_again = (
        jnp.einsum("bqhd,bkhd->bhqk", queries, key_rows, preferred_element_type=jnp.float32)
        * score_scale
    )
    attn_probs = jnp.exp(scores_again - log_total)
    probs_again = attn_probs.astype(jnp.bfloat16)
    grad_values = jnp.einsum(
        "bhqk,bqhd->bkhd", probs_again, mixed_grad, preferred_element_type=jnp.float32
    )
    grad_probs = jnp.einsum(
        "bqhd,bkhd->bhqk", mixed_grad, value_rows, preferred_element_type=jnp.float32
    )
    row_dot = jnp.sum(attn_probs * grad_probs, axis=-1, keepdims=True)
    grad_scores = (attn_probs * (grad_probs - row_dot)).astype(jnp.bfloat16)
    grad_queries = (
        jnp.einsum("bhqk,bkhd->bqhd", grad_scores, key_rows, preferred_element_type=jnp.float32)
        * score_scale
    )
    grad_keys = (
        jnp.einsum("bhqk,bqhd->bkhd", grad_scores, queries, preferred_element_type=jnp.float32)
        * score_scale
    )
    grad_proj = (
        jnp.stack([grad_queries, grad_keys, grad_values])
        .astype(jnp.bfloat16)
        .reshape(3, tok_rows, head_width)
    )
    grad_qkv = jnp.einsum("td,cth->cdh", normed, grad_proj, preferred_element_type=jnp.float32)
    grad_qv_bias = jnp.sum(jnp.stack([grad_proj[0], grad_proj[2]]), axis=1, dtype=jnp.float32)
    normed_back = jnp.einsum(
        "cth,cdh->td", grad_proj, qkv_weight, preferred_element_type=jnp.float32
    )
    normed_grad = tensor_sum(normed_back.astype(jnp.bfloat16))
    embed_grad_ln, grad_attn_gain, grad_attn_shift = attn_norm_back(normed_grad)
    grad_embedded = middle_grad + embed_grad_ln
    width = embedded.shape[1]
    pieces = (
        grad_attn_gain[None],
        grad_attn_shift[None],
        grad_out_bias[None],
        grad_moe_gain[None],
        grad_moe_shift[None],
        jnp.pad(grad_qv_bias, ((0, 0), (0, width - head_width))),
        grad_router.T,
        grad_up_bias,
        grad_down_bias,
    )
    packed = small_sum(jnp.concatenate(pieces, axis=0), "dp")
    grad_attn_gain, grad_attn_shift, grad_out_bias, grad_moe_gain, grad_moe_shift = packed[:5]
    grad_qv_bias = packed[5:7, :head_width]
    grad_router = packed[7 : 7 + expert_count].T
    grad_up_bias = packed[7 + expert_count : 7 + 2 * expert_count]
    grad_down_bias = packed[7 + 2 * expert_count :]
    grad_up = ring_scatter(grad_up.astype(jnp.bfloat16), 1)
    grad_down = ring_scatter(grad_down.astype(jnp.bfloat16), -1).transpose(0, 2, 1)
    grad_qkv = ring_scatter(grad_qkv.astype(jnp.bfloat16), 1)
    grad_out = ring_scatter(grad_out.T[None].astype(jnp.bfloat16), -1)[0].T
    return (
        layer_out.astype(jnp.bfloat16),
        grad_embedded,
        grad_attn_gain,
        grad_attn_shift,
        grad_qkv,
        grad_qv_bias,
        grad_out,
        grad_out_bias,
        grad_moe_gain,
        grad_moe_shift,
        grad_router,
        grad_up,
        grad_up_bias,
        grad_down,
        grad_down_bias,
    )


def solution(mesh):
    return jax.shard_map(
        on_device,
        mesh=mesh,
        in_specs=(
            P("dp", None),
            P(),
            P(),
            P(None, None, "tensor"),
            P(None, "tensor"),
            P("tensor", None),
            P(),
            P(),
            P(),
            P(),
            P(None, None, "tensor"),
            P(None, "tensor"),
            P(None, "tensor", None),
            P(),
            P("dp", None),
            P("dp", None),
        ),
        out_specs=(
            P("dp", None),
            P("dp", None),
            P(),
            P(),
            P(None, "dp", "tensor"),
            P(None, "tensor"),
            P("tensor", "dp"),
            P(),
            P(),
            P(),
            P(),
            P(None, "dp", "tensor"),
            P(None, "tensor"),
            P(None, "tensor", "dp"),
            P(),
        ),
        check_vma=False,
    )
```

```python
import jax
import jax.numpy as jnp
from jax import lax
from jax.experimental import pallas as pl
from jax.experimental.pallas import tpu as pltpu
from jax.sharding import PartitionSpec as P

SEQ = 197
HD = 64


EPSILON = 1e-06
HIGHEST = lax.Precision.HIGHEST


def layer_norm(inputs, gain_vec, shift_vec):
    row_mean = jnp.mean(inputs, axis=-1, keepdims=True)
    centered = inputs - row_mean
    row_var = jnp.mean(centered * centered, axis=-1, keepdims=True)
    return centered * lax.rsqrt(row_var + EPSILON) * gain_vec + shift_vec


RING = (0, 2, 4, 6, 7, 5, 3, 1)


def pairs(count, bit):
    return [(i, i ^ bit) for i in range(count)]


def tensor_sum(part):
    if lax.axis_size("tensor") != 4:
        return lax.psum(part, "tensor").astype(jnp.float32)
    rows, cols = part.shape
    half = cols // 2
    core = lax.axis_index("tensor") % 2
    theirs = lax.dynamic_slice(part, (0, (1 - core) * half), (rows, half))
    mine = lax.dynamic_slice(part, (0, core * half), (rows, half))
    got = lax.ppermute(theirs, "tensor", pairs(4, 1))
    both = (mine.astype(jnp.float32) + got.astype(jnp.float32)).astype(jnp.bfloat16)
    far = lax.ppermute(both, "tensor", pairs(4, 2))
    total = (both.astype(jnp.float32) + far.astype(jnp.float32)).astype(jnp.bfloat16)
    other = lax.ppermute(total, "tensor", pairs(4, 1))
    low = jnp.where(core == 0, total, other)
    high = jnp.where(core == 0, other, total)
    return jnp.concatenate([low, high], axis=1).astype(jnp.float32)


def small_sum(values, axis):
    count = lax.axis_size(axis)
    if count not in (4, 8):
        return lax.psum(values, axis)
    bit = 1
    while bit < count:
        values = values + lax.ppermute(values, axis, pairs(count, bit))
        bit *= 2
    return values


def ring_scatter(values, way):
    count = lax.axis_size("dp")
    if count != 8:
        return lax.psum_scatter(values, "dp", scatter_dimension=1, tiled=True).astype(jnp.float32)
    chunk = values.shape[1] // count
    order = jnp.array(RING, jnp.int32)
    place = jnp.array([RING.index(i) for i in range(count)], jnp.int32)[lax.axis_index("dp")]
    path = [(RING[i], RING[(i + way) % count]) for i in range(count)]

    def local(step):
        owner = order[(place - way * (step + 1)) % count]
        start = (0, owner * chunk, 0)
        return lax.dynamic_slice(values, start, (values.shape[0], chunk, values.shape[2]))

    moving = local(0)
    for step in range(1, count):
        got = lax.ppermute(moving, "dp", path)
        total = got.astype(jnp.float32) + local(step).astype(jnp.float32)
        moving = total.astype(jnp.bfloat16) if step < count - 1 else total
    return moving


BLOCK = 512
GROUPS = 2
LOCAL = 1152
ROOM = 1024
TILE = 256
VMEM = 56 * 1024 * 1024


def route_plan(routes, expert_count):
    tokens = routes.shape[0]
    blocks = -(-tokens // BLOCK)
    padded = jnp.pad(routes.T, ((0, 0), (0, blocks * BLOCK - tokens)), constant_values=-1)
    experts = jnp.arange(expert_count, dtype=jnp.int32)[:, None]
    first = padded[0][None, :] == experts
    second = padded[1][None, :] == experts
    named = (first | second).reshape(expert_count * blocks, BLOCK)
    ahead = jnp.arange(BLOCK)[:, None] < jnp.arange(BLOCK)[None, :]
    rank = jnp.dot(
        named.astype(jnp.bfloat16), ahead.astype(jnp.bfloat16), preferred_element_type=jnp.float32
    )
    rank = rank.astype(jnp.int32).reshape(expert_count, blocks, BLOCK)
    chunks = (jnp.sum(named.astype(jnp.int32), axis=1).reshape(expert_count, blocks) + 15) // 16
    inside = jnp.cumsum(chunks, axis=0) - chunks
    offset = jnp.cumsum(chunks, axis=1) - chunks
    place = (rank + 16 * inside[:, :, None]).reshape(expert_count, blocks * BLOCK)
    target = jnp.stack(
        [jnp.sum(jnp.where(hot, place + 1, 0), axis=0) - 1 for hot in (first, second)]
    )
    tiles = (jnp.sum(chunks, axis=1) * 16 + TILE - 1) // TILE
    plan = jnp.concatenate([chunks.T.reshape(-1), inside.T.reshape(-1), offset.T.reshape(-1)])
    rows = target.reshape(2, blocks, BLOCK).transpose(1, 0, 2)
    return rows, target.T, plan, tiles


def spread(source, rows, plan, expert_count):
    blocks, cols = rows.shape[0], source.shape[1]

    def kernel(plan_ref, rows_ref, source_ref, out_ref, local):
        block = pl.program_id(0)

        @pl.when(block == 0)
        def _():
            out_ref[...] = jnp.zeros_like(out_ref)

        part = LOCAL // 3
        for i in range(3):
            slot = lax.broadcasted_iota(jnp.int32, (part, BLOCK), 0) + i * part
            hot = (slot == rows_ref[0, 0:1, :]) | (slot == rows_ref[0, 1:2, :])
            local[pl.ds(i * part, part), :] = jnp.dot(
                jnp.where(hot, 1.0, 0.0).astype(jnp.bfloat16),
                source_ref[...],
                preferred_element_type=jnp.float32,
            ).astype(jnp.bfloat16)
        for e in range(expert_count):
            at = block * expert_count + e
            size = blocks * expert_count
            begin, goal = plan_ref[size + at], plan_ref[2 * size + at]

            def move(j, carry):
                here = pl.ds(pl.multiple_of((begin + j) * 16, 16), 16)
                there = pl.ds(pl.multiple_of((goal + j) * 16, 16), 16)
                out_ref[e, there, :] = local[here, :]
                return carry

            lax.fori_loop(0, plan_ref[at], move, 0)

    return pl.pallas_call(
        kernel,
        grid_spec=pltpu.PrefetchScalarGridSpec(
            num_scalar_prefetch=1,
            grid=(blocks,),
            in_specs=[
                pl.BlockSpec((1, 2, BLOCK), lambda b, plan: (b, 0, 0)),
                pl.BlockSpec((BLOCK, cols), lambda b, plan: (b, 0)),
            ],
            out_specs=pl.BlockSpec((expert_count, ROOM, cols), lambda b, plan: (0, 0, 0)),
            scratch_shapes=[pltpu.VMEM((LOCAL, cols), jnp.bfloat16)],
        ),
        out_shape=jax.ShapeDtypeStruct((expert_count, ROOM, cols), jnp.bfloat16),
        compiler_params=pltpu.CompilerParams(vmem_limit_bytes=VMEM),
        cost_estimate=pl.CostEstimate(
            flops=2 * blocks * LOCAL * BLOCK * cols,
            bytes_accessed=2 * cols * (blocks * BLOCK + expert_count * ROOM),
            transcendentals=0,
        ),
        name="spread",
    )(plan, rows, source)


def collect(buffers, columns, plan, kept):
    each, room, cols = buffers[0].shape
    expert_count = each * len(buffers)
    blocks = columns.shape[0] // BLOCK
    extra = cols - kept

    def kernel(plan_ref, columns_ref, *refs):
        held, refs = refs[: len(buffers)], refs[len(buffers) :]
        out_ref, local = refs[0], refs[-1]
        block = pl.program_id(0)

        @pl.when(block == 0)
        def _():
            local[...] = jnp.zeros_like(local)

        for e in range(expert_count):
            at = block * expert_count + e
            size = blocks * expert_count
            begin, goal = plan_ref[size + at], plan_ref[2 * size + at]

            def move(j, carry):
                here = pl.ds(pl.multiple_of((begin + j) * 16, 16), 16)
                there = pl.ds(pl.multiple_of((goal + j) * 16, 16), 16)
                local[here, :] = held[e // each][e % each, there, :]
                return carry

            lax.fori_loop(0, plan_ref[at], move, 0)
        part = BLOCK // 2
        for i in range(2):
            rows = pl.ds(i * part, part)
            slot = lax.broadcasted_iota(jnp.int32, (part, LOCAL), 1)
            hot = (slot == columns_ref[rows, 0:1]) | (slot == columns_ref[rows, 1:2])
            total = jnp.dot(
                jnp.where(hot, 1.0, 0.0).astype(jnp.bfloat16),
                local[...],
                preferred_element_type=jnp.float32,
            )
            out_ref[rows, :] = total[:, :kept].astype(jnp.bfloat16)
            if extra:
                refs[1][rows, :] = total[:, kept:]

    out_specs = [pl.BlockSpec((BLOCK, kept), lambda b, plan: (b, 0))]
    out_shape = [jax.ShapeDtypeStruct((blocks * BLOCK, kept), jnp.bfloat16)]
    if extra:
        out_specs.append(pl.BlockSpec((BLOCK, extra), lambda b, plan: (b, 0)))
        out_shape.append(jax.ShapeDtypeStruct((blocks * BLOCK, extra), jnp.float32))
    return pl.pallas_call(
        kernel,
        grid_spec=pltpu.PrefetchScalarGridSpec(
            num_scalar_prefetch=1,
            grid=(blocks,),
            in_specs=[
                pl.BlockSpec((BLOCK, 2), lambda b, plan: (b, 0)),
            ]
            + [pl.BlockSpec((each, room, cols), lambda b, plan: (0, 0, 0))] * len(buffers),
            out_specs=out_specs,
            scratch_shapes=[pltpu.VMEM((LOCAL, cols), jnp.bfloat16)],
        ),
        out_shape=out_shape,
        compiler_params=pltpu.CompilerParams(vmem_limit_bytes=VMEM),
        cost_estimate=pl.CostEstimate(
            flops=2 * blocks * LOCAL * BLOCK * cols,
            bytes_accessed=2 * cols * (blocks * BLOCK + expert_count * room),
            transcendentals=0,
        ),
        name="collect",
    )(plan, columns, *buffers)


GELU_A = 0.7978845608028654
GELU_B = 0.044715


def expert_pass(inputs, grads, up_weight, up_bias, down_weight, tiles, first, count):
    expert_count, room, cols = inputs.shape
    width, hidden = up_weight.shape[1:]

    def kernel(
        tiles_ref, x_ref, g_ref, up_ref, bias_ref, down_ref,
        y_ref, dx_ref, dup_ref, ddown_ref, dbias_ref, mixed, dpre,
    ):
        step = pl.program_id(0)
        expert = step + first

        @pl.when(step == 0)
        def _():
            mixed[...] = jnp.zeros_like(mixed)
            dpre[...] = jnp.zeros_like(dpre)

        dbias_ref[...] = jnp.zeros_like(dbias_ref)
        lane = lax.broadcasted_iota(jnp.int32, (TILE, cols - width), 1)

        def tile(r, carry):
            rows = pl.ds(pl.multiple_of(r * TILE, TILE), TILE)
            x = x_ref[0, rows, :width]
            g = g_ref[0, rows, :]
            gates = x_ref[0, rows, width:].astype(jnp.float32)
            own = (lane == expert) | (lane == expert + expert_count)
            mix = jnp.sum(jnp.where(own, gates, 0.0), axis=1, keepdims=True)
            pre = jnp.dot(x, up_ref[0], preferred_element_type=jnp.float32)
            pre = pre + bias_ref[0].astype(jnp.float32)
            back = lax.dot_general(
                g, down_ref[0], (((1,), (1,)), ((), ())), preferred_element_type=jnp.float32
            )
            square = pre * pre
            bend = jnp.tanh(pre * (GELU_A + GELU_A * GELU_B * square))
            upper = 0.5 + 0.5 * bend
            act = pre * upper
            slope = upper + 0.5 * pre * (1.0 - bend * bend) * (
                GELU_A + 3.0 * GELU_A * GELU_B * square
            )
            dot = jnp.sum(act * back, axis=1, keepdims=True)
            act_low = (mix * act).astype(jnp.bfloat16)
            down = (mix * back * slope).astype(jnp.bfloat16)
            mixed[rows, :] = act_low
            dpre[rows, :] = down
            dbias_ref[0] += jnp.sum(down.astype(jnp.float32), axis=0, keepdims=True)
            y_ref[0, rows, :] = jnp.dot(
                act_low, down_ref[0], preferred_element_type=jnp.float32
            ).astype(jnp.bfloat16)
            dx_ref[0, rows, :width] = lax.dot_general(
                down, up_ref[0], (((1,), (1,)), ((), ())), preferred_element_type=jnp.float32
            ).astype(jnp.bfloat16)
            high = dot.astype(jnp.bfloat16).astype(jnp.float32)
            dx_ref[0, rows, width:] = jnp.where(
                lane == expert, high, jnp.where(lane == expert + expert_count, dot - high, 0.0)
            ).astype(jnp.bfloat16)
            return carry

        lax.fori_loop(0, tiles_ref[expert], tile, 0)

        def weights(depth):
            rows = pl.ds(0, depth)
            for i in range(width // TILE):
                part = pl.ds(i * TILE, TILE)
                dup_ref[0, part, :] = lax.dot_general(
                    x_ref[0, rows, part], dpre[rows, :], (((0,), (0,)), ((), ())),
                    preferred_element_type=jnp.float32,
                ).astype(jnp.bfloat16)
                ddown_ref[0, part, :] = lax.dot_general(
                    g_ref[0, rows, part], mixed[rows, :], (((0,), (0,)), ((), ())),
                    preferred_element_type=jnp.float32,
                ).astype(jnp.bfloat16)

        pl.when(tiles_ref[expert] <= 3)(lambda: weights(3 * TILE))
        pl.when(tiles_ref[expert] > 3)(lambda: weights(room))

    def whole(*dims):
        return pl.BlockSpec((1, *dims), lambda e, tiles: (e + first, 0, 0))

    def own(*dims):
        return pl.BlockSpec((1, *dims), lambda e, tiles: (e, 0, 0))

    shapes = [
        ((room, width), jnp.bfloat16),
        ((room, cols), jnp.bfloat16),
        ((width, hidden), jnp.bfloat16),
        ((width, hidden), jnp.bfloat16),
        ((1, hidden), jnp.float32),
    ]
    return pl.pallas_call(
        kernel,
        grid_spec=pltpu.PrefetchScalarGridSpec(
            num_scalar_prefetch=1,
            grid=(count,),
            in_specs=[
                whole(room, cols),
                whole(room, width),
                whole(width, hidden),
                whole(1, hidden),
                whole(hidden, width),
            ],
            out_specs=[own(*dims) for dims, _ in shapes],
            scratch_shapes=[pltpu.VMEM((room, hidden), jnp.bfloat16)] * 2,
        ),
        out_shape=[jax.ShapeDtypeStruct((count, *dims), kind) for dims, kind in shapes],
        compiler_params=pltpu.CompilerParams(vmem_limit_bytes=VMEM),
        cost_estimate=pl.CostEstimate(
            flops=count * 12 * 768 * width * hidden,
            bytes_accessed=count * (4 * room * (cols + width) + 8 * width * hidden),
            transcendentals=count * 768 * hidden,
        ),
        name="experts",
    )(tiles, inputs, grads, up_weight, up_bias[:, None, :], down_weight)


def on_device(
    embedded,
    attn_gain,
    attn_shift,
    qkv_weight,
    qv_bias,
    out_weight,
    out_bias,
    moe_gain,
    moe_shift,
    router_weight,
    up_weight,
    up_bias,
    down_weight,
    down_bias,
    routes,
    cotangent,
):
    tok_rows = embedded.shape[0]
    images = tok_rows // SEQ
    head_width = qkv_weight.shape[2]
    heads_here = head_width // HD
    expert_count = up_weight.shape[0]
    score_scale = HD ** (-0.5)
    embedded_f = embedded.astype(jnp.float32)
    attn_norm, attn_norm_back = jax.vjp(
        layer_norm, embedded_f, attn_gain.astype(jnp.float32), attn_shift.astype(jnp.float32)
    )
    normed = attn_norm.astype(jnp.bfloat16)
    bias_rows = jnp.stack([qv_bias[0], jnp.zeros_like(qv_bias[0]), qv_bias[1]]).astype(jnp.float32)
    projected = (
        jnp.einsum("td,cdh->cth", normed, qkv_weight, preferred_element_type=jnp.float32)
        + bias_rows[:, None, :]
    )
    projected = projected.astype(jnp.bfloat16)
    queries, key_rows, value_rows = projected.reshape(3, images, SEQ, heads_here, HD)
    scores = (
        jnp.einsum("bqhd,bkhd->bhqk", queries, key_rows, preferred_element_type=jnp.float32)
        * score_scale
    )
    top_score = jnp.max(scores, axis=-1, keepdims=True)
    log_total = top_score + jnp.log(jnp.sum(jnp.exp(scores - top_score), axis=-1, keepdims=True))
    probs_low = jnp.exp(scores - log_total).astype(jnp.bfloat16)
    mixed_heads = jnp.einsum(
        "bhqk,bkhd->bqhd", probs_low, value_rows, preferred_element_type=jnp.float32
    )
    mixed_low = mixed_heads.astype(jnp.bfloat16).reshape(tok_rows, head_width)
    attn_part = jnp.dot(mixed_low, out_weight, preferred_element_type=jnp.float32)
    attn_total = tensor_sum(attn_part.astype(jnp.bfloat16))
    middle = embedded_f + attn_total + out_bias.astype(jnp.float32)
    moe_norm, moe_norm_back = jax.vjp(
        layer_norm, middle, moe_gain.astype(jnp.float32), moe_shift.astype(jnp.float32)
    )
    moe_normed = moe_norm.astype(jnp.bfloat16)
    logits = jnp.dot(moe_normed, router_weight, preferred_element_type=jnp.float32)
    gate_probs = jax.nn.softmax(logits, axis=-1)
    experts = jnp.arange(expert_count, dtype=jnp.int32)[None, :]
    mask = ((routes[:, :1] == experts) | (routes[:, 1:] == experts)).astype(jnp.float32)
    mixing = gate_probs * mask
    rows, columns, plan, tiles = route_plan(routes, expert_count)
    blank = rows.shape[0] * BLOCK - tok_rows
    grad_buffers = spread(jnp.pad(cotangent, ((0, blank), (0, 0))), rows, plan, expert_count)
    mix_high = mixing.astype(jnp.bfloat16)
    mix_low = (mixing - mix_high.astype(jnp.float32)).astype(jnp.bfloat16)
    wide = jnp.concatenate([moe_normed, mix_high, mix_low], axis=1)
    wide = jnp.pad(wide, ((0, blank), (0, 128 - 2 * expert_count)))
    buffers = spread(wide, rows, plan, expert_count)
    group = expert_count // GROUPS
    outs = []
    for i in range(GROUPS):
        outs.append(
            expert_pass(
                buffers, grad_buffers, up_weight, up_bias, down_weight, tiles, i * group, group
            )
        )
    y_buffers, back_buffers, up_parts, down_parts, bias_parts = zip(*outs)
    back_part, dots = collect(back_buffers, columns, plan, moe_normed.shape[1])
    back_part = back_part[:tok_rows]
    (moe_part,) = collect(y_buffers, columns, plan, moe_normed.shape[1])
    moe_part = moe_part[:tok_rows]
    grad_up_bias = jnp.concatenate(bias_parts)[:, 0]
    moe_total = tensor_sum(moe_part)
    down_bias_f = down_bias.astype(jnp.float32)
    layer_out = middle + moe_total + jnp.dot(mixing, down_bias_f, precision=HIGHEST)
    upstream = cotangent.astype(jnp.float32)
    grad_down_bias = jnp.dot(mixing.T, upstream, precision=HIGHEST)
    bias_dot = jnp.dot(cotangent, down_bias.T, preferred_element_type=jnp.float32)
    dots = dots[:tok_rows, : 2 * expert_count].T
    route_dot = small_sum(dots[:expert_count] + dots[expert_count:], "tensor").T
    grad_gates = route_dot + bias_dot * mask
    grad_logits = gate_probs * (
        grad_gates - jnp.sum(gate_probs * grad_gates, axis=-1, keepdims=True)
    )
    grad_logits_low = grad_logits.astype(jnp.bfloat16)
    grad_router = lax.dot_general(
        moe_normed, grad_logits_low, (((0,), (0,)), ((), ())), preferred_element_type=jnp.float32
    )
    router_back = lax.dot_general(
        grad_logits_low, router_weight, (((1,), (1,)), ((), ())), preferred_element_type=jnp.float32
    )
    back_total = tensor_sum(back_part)
    normed2_grad = back_total + router_back
    middle_grad_ln, grad_moe_gain, grad_moe_shift = moe_norm_back(normed2_grad)
    middle_grad = upstream + middle_grad_ln
    attn_grad = middle_grad.astype(jnp.bfloat16)
    grad_out_bias = jnp.sum(attn_grad, axis=0, dtype=jnp.float32)
    grad_out = lax.dot_general(
        mixed_low, attn_grad, (((0,), (0,)), ((), ())), preferred_element_type=jnp.float32
    )
    mixed_grad = lax.dot_general(
        attn_grad, out_weight, (((1,), (1,)), ((), ())), preferred_element_type=jnp.float32
    )
    mixed_grad = mixed_grad.astype(jnp.bfloat16).reshape(images, SEQ, heads_here, HD)
    scores_again = (
        jnp.einsum("bqhd,bkhd->bhqk", queries, key_rows, preferred_element_type=jnp.float32)
        * score_scale
    )
    attn_probs = jnp.exp(scores_again - log_total)
    probs_again = attn_probs.astype(jnp.bfloat16)
    grad_values = jnp.einsum(
        "bhqk,bqhd->bkhd", probs_again, mixed_grad, preferred_element_type=jnp.float32
    )
    grad_probs = jnp.einsum(
        "bqhd,bkhd->bhqk", mixed_grad, value_rows, preferred_element_type=jnp.float32
    )
    row_dot = jnp.sum(attn_probs * grad_probs, axis=-1, keepdims=True)
    grad_scores = (attn_probs * (grad_probs - row_dot)).astype(jnp.bfloat16)
    grad_queries = (
        jnp.einsum("bhqk,bkhd->bqhd", grad_scores, key_rows, preferred_element_type=jnp.float32)
        * score_scale
    )
    grad_keys = (
        jnp.einsum("bhqk,bqhd->bkhd", grad_scores, queries, preferred_element_type=jnp.float32)
        * score_scale
    )
    grad_proj = (
        jnp.stack([grad_queries, grad_keys, grad_values])
        .astype(jnp.bfloat16)
        .reshape(3, tok_rows, head_width)
    )
    grad_qkv = jnp.einsum("td,cth->cdh", normed, grad_proj, preferred_element_type=jnp.float32)
    grad_qv_bias = jnp.sum(jnp.stack([grad_proj[0], grad_proj[2]]), axis=1, dtype=jnp.float32)
    normed_back = jnp.einsum(
        "cth,cdh->td", grad_proj, qkv_weight, preferred_element_type=jnp.float32
    )
    normed_grad = tensor_sum(normed_back.astype(jnp.bfloat16))
    embed_grad_ln = attn_norm_back(normed_grad)[0]
    _, grad_attn_gain, grad_attn_shift = attn_norm_back(normed_back)
    norm_parts = small_sum(jnp.stack([grad_attn_gain, grad_attn_shift]), "tensor")
    grad_embedded = middle_grad + embed_grad_ln
    width = embedded.shape[1]
    pieces = (
        norm_parts,
        grad_out_bias[None],
        grad_moe_gain[None],
        grad_moe_shift[None],
        jnp.pad(grad_qv_bias, ((0, 0), (0, width - head_width))),
        grad_router.T,
        grad_up_bias,
        grad_down_bias,
    )
    packed = small_sum(jnp.concatenate(pieces, axis=0), "dp")
    grad_attn_gain, grad_attn_shift, grad_out_bias, grad_moe_gain, grad_moe_shift = packed[:5]
    grad_qv_bias = packed[5:7, :head_width]
    grad_router = packed[7 : 7 + expert_count].T
    grad_up_bias = packed[7 + expert_count : 7 + 2 * expert_count]
    grad_down_bias = packed[7 + 2 * expert_count :]
    grad_up = jnp.concatenate([ring_scatter(part, 1) for part in up_parts])
    grad_down = jnp.concatenate([ring_scatter(part, -1) for part in down_parts])
    grad_down = grad_down.transpose(0, 2, 1)
    grad_qkv = ring_scatter(grad_qkv.astype(jnp.bfloat16), 1)
    grad_out = ring_scatter(grad_out.T[None].astype(jnp.bfloat16), -1)[0].T
    return (
        layer_out.astype(jnp.bfloat16),
        grad_embedded,
        grad_attn_gain,
        grad_attn_shift,
        grad_qkv,
        grad_qv_bias,
        grad_out,
        grad_out_bias,
        grad_moe_gain,
        grad_moe_shift,
        grad_router,
        grad_up,
        grad_up_bias,
        grad_down,
        grad_down_bias,
    )


def solution(mesh):
    return jax.shard_map(
        on_device,
        mesh=mesh,
        in_specs=(
            P("dp", None),
            P(),
            P(),
            P(None, None, "tensor"),
            P(None, "tensor"),
            P("tensor", None),
            P(),
            P(),
            P(),
            P(),
            P(None, None, "tensor"),
            P(None, "tensor"),
            P(None, "tensor", None),
            P(),
            P("dp", None),
            P("dp", None),
        ),
        out_specs=(
            P("dp", None),
            P("dp", None),
            P(),
            P(),
            P(None, "dp", "tensor"),
            P(None, "tensor"),
            P("tensor", "dp"),
            P(),
            P(),
            P(),
            P(),
            P(None, "dp", "tensor"),
            P(None, "tensor"),
            P(None, "tensor", "dp"),
            P(),
        ),
        check_vma=False,
    )
```

```python
import jax
import jax.numpy as jnp
from jax import lax
from jax.experimental import pallas as pl
from jax.experimental.pallas import tpu as pltpu
from jax.sharding import PartitionSpec as P

SEQ = 197
HD = 64
EPSILON = 1e-06
RING = (0, 2, 4, 6, 7, 5, 3, 1)


def pairs(count, bit):
    return [(i, i ^ bit) for i in range(count)]


def small_sum(values, axis):
    count = lax.axis_size(axis)
    if count not in (4, 8):
        return lax.psum(values, axis)
    bit = 1
    while bit < count:
        values = values + lax.ppermute(values, axis, pairs(count, bit))
        bit *= 2
    return values


ROWS = 208
PAIR = 2
BLOCK = 416
GROUPS = 2
LOCAL = 960
ROOM = 1024
TILE = 256
VMEM = 56 * 1024 * 1024


def route_plan(routes, expert_count):
    tokens = routes.shape[0]
    blocks = -(-tokens // BLOCK)
    padded = jnp.pad(routes.T, ((0, 0), (0, blocks * BLOCK - tokens)), constant_values=-1)
    experts = jnp.arange(expert_count, dtype=jnp.int32)[:, None]
    first = padded[0][None, :] == experts
    second = padded[1][None, :] == experts
    named = (first | second).reshape(expert_count * blocks, BLOCK)
    ahead = jnp.arange(BLOCK)[:, None] < jnp.arange(BLOCK)[None, :]
    rank = jnp.dot(
        named.astype(jnp.bfloat16), ahead.astype(jnp.bfloat16), preferred_element_type=jnp.float32
    )
    rank = rank.astype(jnp.int32).reshape(expert_count, blocks, BLOCK)
    chunks = (jnp.sum(named.astype(jnp.int32), axis=1).reshape(expert_count, blocks) + 15) // 16
    inside = jnp.cumsum(chunks, axis=0) - chunks
    offset = jnp.cumsum(chunks, axis=1) - chunks
    place = (rank + 16 * inside[:, :, None]).reshape(expert_count, blocks * BLOCK)
    target = jnp.stack(
        [jnp.sum(jnp.where(hot, place + 1, 0), axis=0) - 1 for hot in (first, second)]
    )
    tiles = (jnp.sum(chunks, axis=1) * 16 + TILE - 1) // TILE
    plan = jnp.concatenate([chunks.T.reshape(-1), inside.T.reshape(-1), offset.T.reshape(-1)])
    rows = target.reshape(2, blocks, BLOCK).transpose(1, 0, 2)
    return rows, target.T, plan, tiles


def spread(source, rows, plan, expert_count):
    blocks, cols = rows.shape[0], source.shape[1]

    def kernel(plan_ref, rows_ref, source_ref, out_ref, local):
        block = pl.program_id(0)

        @pl.when(block == 0)
        def _():
            out_ref[...] = jnp.zeros_like(out_ref)

        part = LOCAL // 3
        for i in range(3):
            slot = lax.broadcasted_iota(jnp.int32, (part, BLOCK), 0) + i * part
            hot = (slot == rows_ref[0, 0:1, :]) | (slot == rows_ref[0, 1:2, :])
            local[pl.ds(i * part, part), :] = jnp.dot(
                jnp.where(hot, 1.0, 0.0).astype(jnp.bfloat16),
                source_ref[...],
                preferred_element_type=jnp.float32,
            ).astype(jnp.bfloat16)
        for e in range(expert_count):
            at = block * expert_count + e
            size = blocks * expert_count
            begin, goal = plan_ref[size + at], plan_ref[2 * size + at]

            def move(j, carry):
                here = pl.ds(pl.multiple_of((begin + j) * 16, 16), 16)
                there = pl.ds(pl.multiple_of((goal + j) * 16, 16), 16)
                out_ref[e, there, :] = local[here, :]
                return carry

            lax.fori_loop(0, plan_ref[at], move, 0)

    return pl.pallas_call(
        kernel,
        grid_spec=pltpu.PrefetchScalarGridSpec(
            num_scalar_prefetch=1,
            grid=(blocks,),
            in_specs=[
                pl.BlockSpec((1, 2, BLOCK), lambda b, plan: (b, 0, 0)),
                pl.BlockSpec((BLOCK, cols), lambda b, plan: (b, 0)),
            ],
            out_specs=pl.BlockSpec((expert_count, ROOM, cols), lambda b, plan: (0, 0, 0)),
            scratch_shapes=[pltpu.VMEM((LOCAL, cols), jnp.bfloat16)],
        ),
        out_shape=jax.ShapeDtypeStruct((expert_count, ROOM, cols), jnp.bfloat16),
        compiler_params=pltpu.CompilerParams(vmem_limit_bytes=VMEM),
        cost_estimate=pl.CostEstimate(
            flops=2 * blocks * LOCAL * BLOCK * cols,
            bytes_accessed=2 * cols * (blocks * BLOCK + expert_count * ROOM),
            transcendentals=0,
        ),
        name="spread",
    )(plan, rows, source)


def gated_spread(source, rows, plan, chosen, router, expert_count, extra):
    blocks, cols = rows.shape[0], source.shape[1]
    both = cols + extra

    def kernel(
        plan_ref, rows_ref, source_ref, chosen_ref, router_ref, out_ref, gate_ref, pair_ref, local
    ):
        block = pl.program_id(0)

        @pl.when(block == 0)
        def _():
            out_ref[...] = jnp.zeros_like(out_ref)

        logits = jnp.dot(source_ref[...], router_ref[...], preferred_element_type=jnp.float32)
        lane = lax.broadcasted_iota(jnp.int32, logits.shape, 1)
        first, second = lane < expert_count, lane < 2 * expert_count
        expert = jnp.where(first, lane, lane - expert_count)
        top = jnp.max(jnp.where(first, logits, -jnp.inf), axis=-1, keepdims=True)
        raised = jnp.where(second, jnp.exp(logits - top), 0.0)
        gate = raised / jnp.sum(jnp.where(first, raised, 0.0), axis=-1, keepdims=True)
        named = (expert == chosen_ref[:, 0:1]) | (expert == chosen_ref[:, 1:2])
        mixing = jnp.where(named & second, gate, 0.0)
        high = mixing.astype(jnp.bfloat16).astype(jnp.float32)
        pair = jnp.where(first, high, mixing - high).astype(jnp.bfloat16)
        gate_ref[...] = gate
        pair_ref[...] = pair
        part = LOCAL // 3
        for i in range(3):
            slot = lax.broadcasted_iota(jnp.int32, (part, BLOCK), 0) + i * part
            hot = (slot == rows_ref[0, 0:1, :]) | (slot == rows_ref[0, 1:2, :])
            hot = jnp.where(hot, 1.0, 0.0).astype(jnp.bfloat16)
            for begin, end, value in ((0, cols, source_ref[...]), (cols, both, pair)):
                local[pl.ds(i * part, part), begin:end] = jnp.dot(
                    hot, value, preferred_element_type=jnp.float32
                ).astype(jnp.bfloat16)
        for e in range(expert_count):
            at = block * expert_count + e
            size = blocks * expert_count
            begin, goal = plan_ref[size + at], plan_ref[2 * size + at]

            def move(j, carry):
                here = pl.ds(pl.multiple_of((begin + j) * 16, 16), 16)
                there = pl.ds(pl.multiple_of((goal + j) * 16, 16), 16)
                out_ref[e, there, :] = local[here, :]
                return carry

            lax.fori_loop(0, plan_ref[at], move, 0)

    return pl.pallas_call(
        kernel,
        grid_spec=pltpu.PrefetchScalarGridSpec(
            num_scalar_prefetch=1,
            grid=(blocks,),
            in_specs=[
                pl.BlockSpec((1, 2, BLOCK), lambda b, plan: (b, 0, 0)),
                pl.BlockSpec((BLOCK, cols), lambda b, plan: (b, 0)),
                pl.BlockSpec((BLOCK, 2), lambda b, plan: (b, 0)),
                pl.BlockSpec(router.shape, lambda b, plan: (0, 0)),
            ],
            out_specs=[
                pl.BlockSpec((expert_count, ROOM, both), lambda b, plan: (0, 0, 0)),
                pl.BlockSpec((BLOCK, extra), lambda b, plan: (b, 0)),
                pl.BlockSpec((BLOCK, extra), lambda b, plan: (b, 0)),
            ],
            scratch_shapes=[pltpu.VMEM((LOCAL, both), jnp.bfloat16)],
        ),
        out_shape=[
            jax.ShapeDtypeStruct((expert_count, ROOM, both), jnp.bfloat16),
            jax.ShapeDtypeStruct((blocks * BLOCK, extra), jnp.float32),
            jax.ShapeDtypeStruct((blocks * BLOCK, extra), jnp.bfloat16),
        ],
        compiler_params=pltpu.CompilerParams(vmem_limit_bytes=VMEM),
        cost_estimate=pl.CostEstimate(
            flops=2 * blocks * LOCAL * BLOCK * cols,
            bytes_accessed=2 * cols * (blocks * BLOCK + expert_count * ROOM),
            transcendentals=0,
        ),
        name="gated_spread",
    )(plan, rows, source, chosen, router)


def collect(buffers, columns, plan, kept, after):
    each, room, cols = buffers[0].shape
    expert_count = each * len(buffers)
    blocks = columns.shape[0] // BLOCK
    extra = cols - kept

    def kernel(plan_ref, columns_ref, *refs):
        held, refs = refs[: len(buffers)], refs[len(buffers) + len(after) :]
        out_ref, local = refs[0], refs[-1]
        block = pl.program_id(0)

        @pl.when(block == 0)
        def _():
            local[...] = jnp.zeros_like(local)

        for e in range(expert_count):
            at = block * expert_count + e
            size = blocks * expert_count
            begin, goal = plan_ref[size + at], plan_ref[2 * size + at]

            def move(j, carry):
                here = pl.ds(pl.multiple_of((begin + j) * 16, 16), 16)
                there = pl.ds(pl.multiple_of((goal + j) * 16, 16), 16)
                local[here, :] = held[e // each][e % each, there, :]
                return carry

            lax.fori_loop(0, plan_ref[at], move, 0)
        part = BLOCK // 2
        for i in range(2):
            rows = pl.ds(i * part, part)
            slot = lax.broadcasted_iota(jnp.int32, (part, LOCAL), 1)
            hot = (slot == columns_ref[rows, 0:1]) | (slot == columns_ref[rows, 1:2])
            total = jnp.dot(
                jnp.where(hot, 1.0, 0.0).astype(jnp.bfloat16),
                local[...],
                preferred_element_type=jnp.float32,
            )
            out_ref[rows, :] = total[:, :kept].astype(jnp.bfloat16)
            if extra:
                refs[1][rows, :] = total[:, kept:]

    out_specs = [pl.BlockSpec((BLOCK, kept), lambda b, plan: (b, 0))]
    out_shape = [jax.ShapeDtypeStruct((blocks * BLOCK, kept), jnp.bfloat16)]
    if extra:
        out_specs.append(pl.BlockSpec((BLOCK, extra), lambda b, plan: (b, 0)))
        out_shape.append(jax.ShapeDtypeStruct((blocks * BLOCK, extra), jnp.float32))
    return pl.pallas_call(
        kernel,
        grid_spec=pltpu.PrefetchScalarGridSpec(
            num_scalar_prefetch=1,
            grid=(blocks,),
            in_specs=[
                pl.BlockSpec((BLOCK, 2), lambda b, plan: (b, 0)),
            ]
            + [pl.BlockSpec((each, room, cols), lambda b, plan: (0, 0, 0))] * len(buffers)
            + [pl.BlockSpec(memory_space=pl.ANY)] * len(after),
            out_specs=out_specs,
            scratch_shapes=[pltpu.VMEM((LOCAL, cols), jnp.bfloat16)],
        ),
        out_shape=out_shape,
        compiler_params=pltpu.CompilerParams(vmem_limit_bytes=VMEM),
        cost_estimate=pl.CostEstimate(
            flops=2 * blocks * LOCAL * BLOCK * cols,
            bytes_accessed=2 * cols * (blocks * BLOCK + expert_count * room),
            transcendentals=0,
        ),
        name="collect",
    )(plan, columns, *buffers, *after)


GELU_A = 0.7978845608028654
GELU_B = 0.044715


def expert_pass(inputs, grads, up_weight, up_bias, down_weight, tiles, first, count, after):
    expert_count, room, cols = inputs.shape
    width, hidden = up_weight.shape[1:]

    def kernel(
        tiles_ref, x_ref, g_ref, up_ref, bias_ref, down_ref, *refs
    ):
        y_ref, dx_ref, dup_ref, ddown_ref, dbias_ref, mixed, dpre = refs[len(after) :]
        step = pl.program_id(0)
        expert = step + first

        @pl.when(step == 0)
        def _():
            mixed[...] = jnp.zeros_like(mixed)
            dpre[...] = jnp.zeros_like(dpre)

        dbias_ref[...] = jnp.zeros_like(dbias_ref)
        lane = lax.broadcasted_iota(jnp.int32, (TILE, cols - width), 1)

        def tile(r, carry):
            rows = pl.ds(pl.multiple_of(r * TILE, TILE), TILE)
            x = x_ref[0, rows, :width]
            g = g_ref[0, rows, :]
            gates = x_ref[0, rows, width:].astype(jnp.float32)
            own = (lane == expert) | (lane == expert + expert_count)
            mix = jnp.sum(jnp.where(own, gates, 0.0), axis=1, keepdims=True)
            pre = jnp.dot(x, up_ref[0], preferred_element_type=jnp.float32)
            pre = pre + bias_ref[0].astype(jnp.float32)
            back = lax.dot_general(
                g, down_ref[0], (((1,), (1,)), ((), ())), preferred_element_type=jnp.float32
            )
            square = pre * pre
            bend = jnp.tanh(pre * (GELU_A + GELU_A * GELU_B * square))
            upper = 0.5 + 0.5 * bend
            act = pre * upper
            slope = upper + 0.5 * pre * (1.0 - bend * bend) * (
                GELU_A + 3.0 * GELU_A * GELU_B * square
            )
            dot = jnp.sum(act * back, axis=1, keepdims=True)
            act_low = (mix * act).astype(jnp.bfloat16)
            down = (mix * back * slope).astype(jnp.bfloat16)
            mixed[rows, :] = act_low
            dpre[rows, :] = down
            dbias_ref[0] += jnp.sum(down.astype(jnp.float32), axis=0, keepdims=True)
            y_ref[0, rows, :] = jnp.dot(
                act_low, down_ref[0], preferred_element_type=jnp.float32
            ).astype(jnp.bfloat16)
            dx_ref[0, rows, :width] = lax.dot_general(
                down, up_ref[0], (((1,), (1,)), ((), ())), preferred_element_type=jnp.float32
            ).astype(jnp.bfloat16)
            high = dot.astype(jnp.bfloat16).astype(jnp.float32)
            dx_ref[0, rows, width:] = jnp.where(
                lane == expert, high, jnp.where(lane == expert + expert_count, dot - high, 0.0)
            ).astype(jnp.bfloat16)
            return carry

        lax.fori_loop(0, tiles_ref[expert], tile, 0)

        def weights(depth):
            rows = pl.ds(0, depth)
            for i in range(width // TILE):
                part = pl.ds(i * TILE, TILE)
                dup_ref[0, part, :] = lax.dot_general(
                    x_ref[0, rows, part], dpre[rows, :], (((0,), (0,)), ((), ())),
                    preferred_element_type=jnp.float32,
                ).astype(jnp.bfloat16)
                ddown_ref[0, part, :] = lax.dot_general(
                    g_ref[0, rows, part], mixed[rows, :], (((0,), (0,)), ((), ())),
                    preferred_element_type=jnp.float32,
                ).astype(jnp.bfloat16)

        pl.when(tiles_ref[expert] <= 3)(lambda: weights(3 * TILE))
        pl.when(tiles_ref[expert] > 3)(lambda: weights(room))

    def whole(*dims):
        return pl.BlockSpec((1, *dims), lambda e, tiles: (e + first, 0, 0))

    def own(*dims):
        return pl.BlockSpec((1, *dims), lambda e, tiles: (e, 0, 0))

    shapes = [
        ((room, width), jnp.bfloat16),
        ((room, cols), jnp.bfloat16),
        ((width, hidden), jnp.bfloat16),
        ((width, hidden), jnp.bfloat16),
        ((1, hidden), jnp.float32),
    ]
    return pl.pallas_call(
        kernel,
        grid_spec=pltpu.PrefetchScalarGridSpec(
            num_scalar_prefetch=1,
            grid=(count,),
            in_specs=[
                whole(room, cols),
                whole(room, width),
                whole(width, hidden),
                whole(1, hidden),
                whole(hidden, width),
            ]
            + [pl.BlockSpec(memory_space=pl.ANY)] * len(after),
            out_specs=[own(*dims) for dims, _ in shapes],
            scratch_shapes=[pltpu.VMEM((room, hidden), jnp.bfloat16)] * 2,
        ),
        out_shape=[jax.ShapeDtypeStruct((count, *dims), kind) for dims, kind in shapes],
        compiler_params=pltpu.CompilerParams(vmem_limit_bytes=VMEM),
        cost_estimate=pl.CostEstimate(
            flops=count * 12 * 768 * width * hidden,
            bytes_accessed=count * (4 * room * (cols + width) + 8 * width * hidden),
            transcendentals=count * 768 * hidden,
        ),
        name="experts",
    )(tiles, inputs, grads, up_weight, up_bias[:, None, :], down_weight, *after)


def call(kernel, name, grid, ins, outs, after=(), scratch=(), flops=0, traffic=0, each=1, turn=None):
    turn = jnp.zeros((1,), jnp.int32) if turn is None else turn

    def spec(shape, split):
        zeros = (0,) * (len(shape) - 1)
        if split == "turned":
            return pl.BlockSpec((each, *shape[1:]), lambda i, t: ((i + t[0]) % grid, *zeros))
        if split:
            return pl.BlockSpec((each, *shape[1:]), lambda i, t: (i, *zeros))
        return pl.BlockSpec(tuple(shape), lambda i, t: (0, *zeros))

    count, late = len(ins), len(after)

    def body(turn_ref, *refs):
        kernel(*refs[:count], *refs[count + late :])

    return pl.pallas_call(
        body,
        grid_spec=pltpu.PrefetchScalarGridSpec(
            num_scalar_prefetch=1,
            grid=(grid,),
            in_specs=[spec(a.shape, split) for a, split in ins]
            + [pl.BlockSpec(memory_space=pl.ANY)] * late,
            out_specs=[spec(a.shape, split) for a, split in outs],
            scratch_shapes=list(scratch),
        ),
        out_shape=[a for a, _ in outs],
        compiler_params=pltpu.CompilerParams(vmem_limit_bytes=VMEM),
        cost_estimate=pl.CostEstimate(flops=flops, bytes_accessed=traffic, transcendentals=0),
        name=name,
    )(turn, *[a for a, _ in ins], *after)


def shape_of(dims, kind):
    return jax.ShapeDtypeStruct(tuple(dims), kind)


def normal(x):
    centered = x - jnp.mean(x, axis=-1, keepdims=True)
    spread_of = lax.rsqrt(jnp.mean(centered * centered, axis=-1, keepdims=True) + EPSILON)
    return centered * spread_of, spread_of


def contract(left, right, left_dim, right_dim):
    return lax.dot_general(
        left, right, (((left_dim,), (right_dim,)), ((), ())), preferred_element_type=jnp.float32
    )


def head_masks(width):
    lane = lax.broadcasted_iota(jnp.int32, (1, width), 1)
    return [(lane >= h * HD) & (lane < (h + 1) * HD) for h in range(width // HD)]


def head_probs(q, k, mask):
    own = jnp.where(mask, q, jnp.zeros_like(q)) * jnp.bfloat16(HD ** (-0.5))
    scores = contract(own, k, 1, 1)
    column = lax.broadcasted_iota(jnp.int32, scores.shape, 1)
    scores = jnp.where(column < SEQ, scores, -1e30)
    raised = jnp.exp(scores - jnp.max(scores, axis=-1, keepdims=True))
    return raised / jnp.sum(raised, axis=-1, keepdims=True)


def attention_forward(x, turn, gain, shift, weight, bias, out_weight):
    images, seq, width = x.shape
    rows, inner = ROWS, weight.shape[2]

    def kernel(
        x_ref, gain_ref, shift_ref, w_ref, b_ref, wo_ref,
        part_ref, pad_ref, n_ref, q_ref, k_ref, v_ref, o_ref, held,
    ):
        held[...] = jnp.zeros_like(held)
        for i in range(PAIR):
            held[i, :seq, :] = x_ref[i].astype(jnp.float32)
        for i in range(PAIR):
            value = held[i]
            pad_ref[i] = value.astype(jnp.bfloat16)
            n = (normal(value)[0] * gain_ref[...] + shift_ref[...]).astype(jnp.bfloat16)
            n_ref[i] = n
            q, k, v = [
                (
                    jnp.dot(n, w_ref[j], preferred_element_type=jnp.float32) + b_ref[j : j + 1, :]
                ).astype(jnp.bfloat16)
                for j in range(3)
            ]
            q_ref[i], k_ref[i], v_ref[i] = q, k, v
            mixed = jnp.zeros((rows, inner), jnp.float32)
            for mask in head_masks(inner):
                probs = head_probs(q, k, mask).astype(jnp.bfloat16)
                head = jnp.dot(probs, v, preferred_element_type=jnp.float32)
                mixed = jnp.where(mask, head, mixed)
            mixed = mixed.astype(jnp.bfloat16)
            o_ref[i] = mixed
            part_ref[i] = jnp.dot(mixed, wo_ref[...], preferred_element_type=jnp.float32).astype(
                jnp.bfloat16
            )

    wide = shape_of((images, rows, width), jnp.bfloat16)
    slim = shape_of((images, rows, inner), jnp.bfloat16)
    return call(
        kernel, "attention_forward", images // PAIR,
        [(x, "turned"), (gain, False), (shift, False), (weight, False), (bias, False), (out_weight, False)],
        [(wide, True)] * 3 + [(slim, True)] * 4,
        scratch=[pltpu.VMEM((PAIR, rows, width), jnp.float32)], each=PAIR, turn=turn,
        flops=images * rows * width * inner * 8, traffic=images * rows * (width * 8 + inner * 8),
    )


def attention_backward(da, x, n, q, k, v, o, weight, out_weight, after):
    images, rows, width = x.shape
    inner = weight.shape[2]

    def kernel(
        da_ref, x_ref, n_ref, q_ref, k_ref, v_ref, o_ref, w_ref, wo_ref,
        back_ref, dw_ref, dwo_ref, dbias_ref, sums_ref,
    ):
        @pl.when(pl.program_id(0) == 0)
        def _():
            dw_ref[...] = jnp.zeros_like(dw_ref)
            dwo_ref[...] = jnp.zeros_like(dwo_ref)
            dbias_ref[...] = jnp.zeros_like(dbias_ref)
            sums_ref[...] = jnp.zeros_like(sums_ref)

        for i in range(PAIR):
            da, q, k, v = da_ref[i], q_ref[i], k_ref[i], v_ref[i]
            do = contract(da, wo_ref[...], 1, 1).astype(jnp.bfloat16)
            dq = dk = dv = jnp.zeros((rows, inner), jnp.float32)
            for mask in head_masks(inner):
                probs = head_probs(q, k, mask)
                dv = jnp.where(mask, contract(probs.astype(jnp.bfloat16), do, 0, 0), dv)
                dp = contract(jnp.where(mask, do, jnp.zeros_like(do)), v, 1, 1)
                ds = probs * (dp - jnp.sum(probs * dp, axis=-1, keepdims=True))
                ds = ds.astype(jnp.bfloat16)
                dq = jnp.where(mask, jnp.dot(ds, k, preferred_element_type=jnp.float32), dq)
                dk = jnp.where(mask, contract(ds, q, 0, 0), dk)
            scale = HD ** (-0.5)
            grads = [(dq * scale).astype(jnp.bfloat16), (dk * scale).astype(jnp.bfloat16), dv.astype(jnp.bfloat16)]
            n = n_ref[i]
            back = jnp.zeros((rows, width), jnp.float32)
            for j in range(3):
                dw_ref[j] += contract(n, grads[j], 0, 0)
                back += contract(grads[j], w_ref[j], 1, 1)
            dwo_ref[0] += contract(da, o_ref[i], 0, 0)
            back_ref[i] = back.astype(jnp.bfloat16)
            dbias_ref[0:1, :] += jnp.sum(grads[0].astype(jnp.float32), axis=0, keepdims=True)
            dbias_ref[1:2, :] += jnp.sum(grads[2].astype(jnp.float32), axis=0, keepdims=True)
            unit, _ = normal(x_ref[i].astype(jnp.float32))
            sums_ref[0:1, :] += jnp.sum(back * unit, axis=0, keepdims=True)
            sums_ref[1:2, :] += jnp.sum(back, axis=0, keepdims=True)
            sums_ref[2:3, :] += jnp.sum(da.astype(jnp.float32), axis=0, keepdims=True)

    return call(
        kernel, "attention_backward", images // PAIR,
        [(a, True) for a in (da, x, n, q, k, v, o)] + [(weight, False), (out_weight, False)],
        [
            (shape_of((images, rows, width), jnp.bfloat16), True),
            (shape_of((3, width, inner), jnp.float32), False),
            (shape_of((1, width, inner), jnp.float32), False),
            (shape_of((2, inner), jnp.float32), False),
            (shape_of((3, width), jnp.float32), False),
        ],
        after=after, each=PAIR, flops=images * rows * width * inner * 18,
        traffic=images * rows * (width * 8 + inner * 8),
    )


def middle_norm(near, far, x, out_bias, gain, shift, after):
    def kernel(near_ref, far_ref, x_ref, bias_ref, gain_ref, shift_ref, middle_ref, n_ref):
        total = near_ref[0].astype(jnp.float32) + far_ref[0].astype(jnp.float32)
        middle = x_ref[0].astype(jnp.float32) + total + bias_ref[...]
        middle_ref[0] = middle
        n_ref[0] = (normal(middle)[0] * gain_ref[...] + shift_ref[...]).astype(jnp.bfloat16)

    return call(
        kernel, "middle_norm", near.shape[0],
        [(near, True), (far, True), (x, True), (out_bias, False), (gain, False), (shift, False)],
        [(shape_of(near.shape, jnp.float32), True), (shape_of(near.shape, jnp.bfloat16), True)],
        after=after, traffic=12 * near.size,
    )


def norm_back(dn, unit, spread_of, gain):
    dz = dn * gain
    mean = jnp.mean(dz, axis=-1, keepdims=True)
    return spread_of * (dz - mean - unit * jnp.mean(dz * unit, axis=-1, keepdims=True))


def middle_back(near, far, dots, gates, chosen, pair, n, router_weight, down_bias, middle, upstream, gain, after):
    count, wide = down_bias.shape[0], pair.shape[2]

    def kernel(
        near_ref, far_ref, dots_ref, gates_ref, chosen_ref, pair_ref, n_ref, router_ref, bias_ref,
        middle_ref, g_ref, gain_ref, grad_ref, da_ref, sums_ref, drouter_ref, dbias_ref,
    ):
        @pl.when(pl.program_id(0) == 0)
        def _():
            sums_ref[...] = jnp.zeros_like(sums_ref)
            drouter_ref[...] = jnp.zeros_like(drouter_ref)
            dbias_ref[...] = jnp.zeros_like(dbias_ref)

        g = g_ref[0]
        lane = lax.broadcasted_iota(jnp.int32, (g.shape[0], count), 1)
        named = (lane == chosen_ref[0, :, 0:1]) | (lane == chosen_ref[0, :, 1:2])
        dmix = dots_ref[0] + jnp.where(named, contract(g, bias_ref[...], 1, 1), 0.0)
        gate = gates_ref[0, :, :count]
        dlogits = gate * (dmix - jnp.sum(gate * dmix, axis=-1, keepdims=True))
        dlogits = dlogits.astype(jnp.bfloat16)
        drouter_ref[...] += contract(dlogits, n_ref[0], 0, 0)
        dbias_ref[...] += contract(pair_ref[0], g, 0, 0)
        dn = near_ref[0].astype(jnp.float32) + far_ref[0].astype(jnp.float32)
        dn = dn + contract(dlogits, router_ref[...], 1, 1)
        unit, spread_of = normal(middle_ref[0])
        grad = g.astype(jnp.float32) + norm_back(dn, unit, spread_of, gain_ref[...])
        grad_ref[0] = grad
        da_ref[0] = grad.astype(jnp.bfloat16)
        sums_ref[0:1, :] += jnp.sum(dn * unit, axis=0, keepdims=True)
        sums_ref[1:2, :] += jnp.sum(dn, axis=0, keepdims=True)

    width = middle.shape[2]
    return call(
        kernel, "middle_back", middle.shape[0],
        [(a, True) for a in (near, far, dots, gates, chosen, pair, n)]
        + [(router_weight, False), (down_bias, False), (middle, True), (upstream, True), (gain, False)],
        [
            (shape_of(middle.shape, jnp.float32), True),
            (shape_of(middle.shape, jnp.bfloat16), True),
            (shape_of((2, width), jnp.float32), False),
            (shape_of((count, width), jnp.float32), False),
            (shape_of((wide, width), jnp.float32), False),
        ],
        after=after, traffic=18 * middle.size,
    )


def finish(near, far, middle, pair, down_bias, after):
    def kernel(near_ref, far_ref, middle_ref, pair_ref, bias_ref, out_ref):
        total = near_ref[0].astype(jnp.float32) + far_ref[0].astype(jnp.float32)
        total = total + jnp.dot(pair_ref[0], bias_ref[...], preferred_element_type=jnp.float32)
        out_ref[0] = (middle_ref[0] + total).astype(jnp.bfloat16)

    return call(
        kernel, "finish", middle.shape[0],
        [(near, True), (far, True), (middle, True), (pair, True), (down_bias, False)],
        [(shape_of(middle.shape, jnp.bfloat16), True)],
        after=after, traffic=10 * middle.size,
    )[0]


def input_back(own, other, x, own_grad, other_grad, gain, turn, after):
    images, _, width = x.shape
    half = images // 2

    def kernel(turn_ref, own_ref, other_ref, x_ref, own_grad_ref, other_grad_ref, gain_ref, *refs):
        out_ref = refs[-1]
        step = pl.program_id(0)
        place = (step + turn_ref[0]) % images
        mine = step < half
        dn = jnp.where(mine, own_ref[0], other_ref[0]).astype(jnp.float32)
        unit, spread_of = normal(x_ref[0].astype(jnp.float32))
        grad = jnp.where(mine, own_grad_ref[0], other_grad_ref[0])
        grad = grad + norm_back(dn, unit, spread_of, gain_ref[...])
        for j in range(images):

            @pl.when(place == j)
            def _():
                out_ref[j * SEQ : (j + 1) * SEQ, :] = grad[:SEQ]

    def low(shape):
        return pl.BlockSpec((1, *shape[1:]), lambda i, t: (jnp.minimum(i, half - 1), 0, 0))

    def high(shape):
        return pl.BlockSpec((1, *shape[1:]), lambda i, t: (jnp.maximum(i - half, 0), 0, 0))

    return pl.pallas_call(
        kernel,
        grid_spec=pltpu.PrefetchScalarGridSpec(
            num_scalar_prefetch=1,
            grid=(images,),
            in_specs=[
                low(own.shape),
                high(other.shape),
                pl.BlockSpec((1, *x.shape[1:]), lambda i, t: (i, 0, 0)),
                low(own_grad.shape),
                high(other_grad.shape),
                pl.BlockSpec(gain.shape, lambda i, t: (0, 0)),
            ]
            + [pl.BlockSpec(memory_space=pl.ANY)] * len(after),
            out_specs=pl.BlockSpec((images * SEQ, width), lambda i, t: (0, 0)),
        ),
        out_shape=jax.ShapeDtypeStruct((images * SEQ, width), jnp.float32),
        compiler_params=pltpu.CompilerParams(vmem_limit_bytes=VMEM),
        cost_estimate=pl.CostEstimate(flops=0, bytes_accessed=14 * x.size, transcendentals=0),
        name="input_back",
    )(turn, own, other, x, own_grad, other_grad, gain, *after)


def to_core(value):
    return lax.ppermute(value, "tensor", pairs(lax.axis_size("tensor"), 1))


def across(value):
    return lax.ppermute(value, "tensor", pairs(lax.axis_size("tensor"), 2))


def core_sum(part, zero):
    half = part.shape[0] // 2
    got = to_core(part[half:])
    return (part[:half].astype(jnp.float32) + got.astype(jnp.float32) + zero).astype(jnp.bfloat16)


def zero_of(value):
    return value[(0,) * value.ndim].astype(jnp.float32) * 0.0


class Ring:
    def __init__(self, values, way):
        self.values, self.way, self.step, self.count = values, way, 0, lax.axis_size("dp")
        self.ring = self.count == len(RING)
        self.moving = self.local(0) if self.ring else values.astype(jnp.bfloat16)

    def local(self, step):
        count = self.count
        chunk = self.values.shape[1] // count
        order = jnp.array(RING, jnp.int32)
        place = jnp.array([RING.index(i) for i in range(count)], jnp.int32)
        owner = order[(place[lax.axis_index("dp")] - self.way * (step + 1)) % count]
        size = (self.values.shape[0], chunk, self.values.shape[2])
        return lax.dynamic_slice(self.values, (0, owner * chunk, 0), size).astype(jnp.bfloat16)

    def hop(self, zero):
        if not self.ring or self.step == self.count - 1:
            return
        path = [(RING[i], RING[(i + self.way) % self.count]) for i in range(self.count)]
        got = lax.ppermute(self.moving, "dp", path)
        self.step += 1
        total = got.astype(jnp.float32) + self.local(self.step).astype(jnp.float32) + zero
        self.moving = total.astype(jnp.bfloat16) if self.step < self.count - 1 else total

    def result(self):
        if not self.ring:
            return lax.psum_scatter(self.moving, "dp", scatter_dimension=1, tiled=True).astype(jnp.float32)
        while self.step < self.count - 1:
            self.hop(0.0)
        return self.moving


def halving_scatter(values):
    if lax.axis_size("dp") != 8:
        return lax.psum_scatter(values.astype(jnp.bfloat16), "dp", scatter_dimension=1, tiled=True).astype(jnp.float32)
    index = lax.axis_index("dp")
    many, rows, cols = values.shape
    values = values.reshape(many, 2, 2, 2, rows // 8, cols)
    for bit, axis in ((0, 3), (1, 2), (2, 1)):
        mine = (index >> bit) % 2
        keep = lax.dynamic_index_in_dim(values, mine, axis, keepdims=True)
        give = lax.dynamic_index_in_dim(values, 1 - mine, axis, keepdims=True)
        got = lax.ppermute(give.astype(jnp.bfloat16), "dp", pairs(8, 1 << bit))
        values = keep.astype(jnp.float32) + got.astype(jnp.float32)
    return values.reshape(many, rows // 8, cols)


def on_device(
    embedded,
    attn_gain,
    attn_shift,
    qkv_weight,
    qv_bias,
    out_weight,
    out_bias,
    moe_gain,
    moe_shift,
    router_weight,
    up_weight,
    up_bias,
    down_weight,
    down_bias,
    routes,
    cotangent,
):
    tok_rows, width = embedded.shape
    images = tok_rows // SEQ
    half = images // 2
    head_width = qkv_weight.shape[2]
    expert_count = up_weight.shape[0]
    core = lax.axis_index("tensor") % 2
    f32 = jnp.float32

    def own_first(value, fill):
        value = value.reshape(images, SEQ, value.shape[1])
        value = jnp.pad(value, ((0, 0), (0, ROWS - SEQ), (0, 0)), constant_values=fill)
        return jnp.where(core == 0, value, jnp.roll(value, half, axis=0))

    def in_order(own, other):
        low = jnp.where(core == 0, own, other)
        high = jnp.where(core == 0, other, own)
        return jnp.concatenate([low, high])[:, :SEQ].reshape(tok_rows, width)

    def row(value):
        return value.astype(f32)[None]

    def imaged(value):
        return value.reshape(images, ROWS, value.shape[1])

    turn = (half * core).astype(jnp.int32)[None]
    bias_rows = jnp.stack([qv_bias[0], jnp.zeros_like(qv_bias[0]), qv_bias[1]]).astype(f32)
    part, x, normed, queries, keys, values, mixed = attention_forward(
        embedded.reshape(images, SEQ, width), turn // PAIR, row(attn_gain), row(attn_shift),
        qkv_weight, bias_rows, out_weight,
    )
    near = core_sum(part, 0.0)
    far = across(near)

    chosen = own_first(routes, -1).reshape(images * ROWS, 2)
    rows, columns, plan, tiles = route_plan(chosen, expert_count)
    upstream = own_first(cotangent, 0)
    grad_buffers = spread(upstream.reshape(images * ROWS, width), rows, plan, expert_count)

    middle, own_normed = middle_norm(
        near, far, x, row(out_bias), row(moe_gain), row(moe_shift), (grad_buffers,)
    )
    moe_normed = jnp.concatenate([own_normed, to_core(own_normed)]).reshape(images * ROWS, width)
    extra = 128
    router_twice = jnp.pad(
        jnp.concatenate([router_weight, router_weight], axis=1),
        ((0, 0), (0, extra - 2 * expert_count)),
    )
    bias_twice = jnp.pad(
        jnp.concatenate([down_bias, down_bias]), ((0, extra - 2 * expert_count), (0, 0))
    )
    buffers, gates, mix_pair = gated_spread(
        moe_normed, rows, plan, chosen, router_twice, expert_count, extra
    )
    gates, mix_pair, chosen = imaged(gates), imaged(mix_pair), imaged(chosen)
    group = expert_count // GROUPS

    def experts_of(i, after):
        return expert_pass(
            buffers, grad_buffers, up_weight, up_bias, down_weight, tiles, i * group, group, after
        )

    def tokens(*some):
        return tuple(ring.moving for ring in some)

    def hops(value, *some):
        for ring in some:
            ring.hop(zero_of(value))

    y_first, back_first, up_grad, down_grad, bias_first = experts_of(0, ())
    first = (Ring(up_grad, 1), Ring(down_grad, -1))
    y_second, back_second, up_grad, down_grad, bias_second = experts_of(1, tokens(*first))
    hops(bias_second, *first)
    back_part, dots = collect((back_first, back_second), columns, plan, width, tokens(*first))
    second = (Ring(up_grad, 1), Ring(down_grad, -1))
    back_near = core_sum(imaged(back_part), 0.0)
    back_far = across(back_near)
    dots = dots[:, : 2 * expert_count].T
    dots = dots[:expert_count] + dots[expert_count:]
    own_rows = half * ROWS
    dots = dots[:, :own_rows] + to_core(dots[:, own_rows:])
    dots = (dots + across(dots)).T.reshape(half, ROWS, expert_count)
    hops(back_near, *first)
    (moe_part,) = collect(
        (y_first, y_second), columns, plan, width, (back_near, *tokens(*first, *second))
    )
    hops(moe_part, *second)
    hops(second[1].moving, *first)
    hops(first[1].moving, *second)
    middle_grad, own_da, moe_sums, router_sums, bias_sums = middle_back(
        back_near, back_far, dots, gates, chosen, mix_pair, imaged(moe_normed), router_weight,
        down_bias, middle, upstream, row(moe_gain), tokens(*second),
    )
    da = jnp.concatenate([own_da, to_core(own_da)])
    y_near = core_sum(imaged(moe_part), zero_of(own_da))
    y_far = across(y_near)
    other_grad = to_core(middle_grad)
    hops(own_da, *first)
    normed_back, grad_qkv, grad_out, grad_qv_bias, sums = attention_backward(
        da, x, normed, queries, keys, values, mixed, qkv_weight, out_weight, tokens(*first)
    )
    last_near = core_sum(normed_back, 0.0)
    last_far = across(last_near)
    hops(normed_back, *second)
    hops(last_near, *first)
    own_out = finish(y_near, y_far, middle, mix_pair, bias_twice, (last_near,))
    layer_out = in_order(own_out, to_core(own_out))
    router_bias = [router_sums, bias_sums[:expert_count] + bias_sums[expert_count : 2 * expert_count]]
    tensor_parts = jnp.concatenate([sums[:2]] + [0.5 * part for part in (moe_sums, *router_bias)])
    packed = jnp.concatenate(
        [
            small_sum(tensor_parts, "tensor"),
            sums[2:],
            jnp.pad(grad_qv_bias, ((0, 0), (0, width - head_width))),
            bias_first[:, 0],
            bias_second[:, 0],
        ]
    )
    packed = small_sum(packed, "dp")
    slim = halving_scatter(jnp.concatenate([grad_qkv, grad_out]))
    up_first, down_first, up_second, down_second = [ring.result() for ring in first + second]
    last = (last_near.astype(f32) + last_far.astype(f32)).astype(jnp.bfloat16)
    grad_embedded = input_back(
        last, to_core(last), x, middle_grad, other_grad, row(attn_gain), turn,
        (layer_out, packed, slim),
    )
    base = 4 + 2 * expert_count
    return (
        layer_out,
        grad_embedded,
        packed[0],
        packed[1],
        slim[:3],
        packed[base + 1 : base + 3, :head_width],
        slim[3].T,
        packed[base],
        packed[2],
        packed[3],
        packed[4 : 4 + expert_count].T,
        jnp.concatenate([up_first, up_second]),
        packed[base + 3 :],
        jnp.concatenate([down_first, down_second]).transpose(0, 2, 1),
        packed[4 + expert_count : base],
    )


def solution(mesh):
    return jax.shard_map(
        on_device,
        mesh=mesh,
        in_specs=(
            P("dp", None),
            P(),
            P(),
            P(None, None, "tensor"),
            P(None, "tensor"),
            P("tensor", None),
            P(),
            P(),
            P(),
            P(),
            P(None, None, "tensor"),
            P(None, "tensor"),
            P(None, "tensor", None),
            P(),
            P("dp", None),
            P("dp", None),
        ),
        out_specs=(
            P("dp", None),
            P("dp", None),
            P(),
            P(),
            P(None, "dp", "tensor"),
            P(None, "tensor"),
            P("tensor", "dp"),
            P(),
            P(),
            P(),
            P(),
            P(None, "dp", "tensor"),
            P(None, "tensor"),
            P(None, "tensor", "dp"),
            P(),
        ),
        check_vma=False,
    )
```

```python
import jax
import jax.numpy as jnp
from jax import lax
from jax.experimental import pallas as pl
from jax.experimental.pallas import tpu as pltpu
from jax.sharding import PartitionSpec as P

SEQ = 197
HD = 64
EPSILON = 1e-06
RING = (0, 2, 4, 6, 7, 5, 3, 1)


def pairs(count, bit):
    return [(i, i ^ bit) for i in range(count)]


def small_sum(values, axis):
    count = lax.axis_size(axis)
    if count not in (4, 8):
        return lax.psum(values, axis)
    bit = 1
    while bit < count:
        values = values + lax.ppermute(values, axis, pairs(count, bit))
        bit *= 2
    return values


ROWS = 208
PAIR = 2
BLOCK = 416
GROUPS = 2
LOCAL = 960
ROOM = 1024
TILE = 256
VMEM = 56 * 1024 * 1024


def cost(us):
    return pl.CostEstimate(flops=int(us * 1.1e9), bytes_accessed=0, transcendentals=0)


def route_plan(routes, expert_count):
    tokens = routes.shape[0]
    blocks = -(-tokens // BLOCK)
    padded = jnp.pad(routes.T, ((0, 0), (0, blocks * BLOCK - tokens)), constant_values=-1)
    experts = jnp.arange(expert_count, dtype=jnp.int32)[:, None]
    first = padded[0][None, :] == experts
    second = padded[1][None, :] == experts
    named = (first | second).reshape(expert_count * blocks, BLOCK)
    ahead = jnp.arange(BLOCK)[:, None] < jnp.arange(BLOCK)[None, :]
    rank = jnp.dot(
        named.astype(jnp.bfloat16), ahead.astype(jnp.bfloat16), preferred_element_type=jnp.float32
    )
    rank = rank.astype(jnp.int32).reshape(expert_count, blocks, BLOCK)
    chunks = (jnp.sum(named.astype(jnp.int32), axis=1).reshape(expert_count, blocks) + 15) // 16
    inside = jnp.cumsum(chunks, axis=0) - chunks
    offset = jnp.cumsum(chunks, axis=1) - chunks
    place = (rank + 16 * inside[:, :, None]).reshape(expert_count, blocks * BLOCK)
    target = jnp.stack(
        [jnp.sum(jnp.where(hot, place + 1, 0), axis=0) - 1 for hot in (first, second)]
    )
    tiles = (jnp.sum(chunks, axis=1) * 16 + TILE - 1) // TILE
    plan = jnp.concatenate([chunks.T.reshape(-1), inside.T.reshape(-1), offset.T.reshape(-1)])
    rows = target.reshape(2, blocks, BLOCK).transpose(1, 0, 2)
    return rows, target.T, plan, tiles


def spread(source, rows, plan, expert_count):
    blocks, cols = rows.shape[0], source.shape[1]

    def kernel(plan_ref, rows_ref, source_ref, out_ref, local):
        block = pl.program_id(0)

        @pl.when(block == 0)
        def _():
            out_ref[...] = jnp.zeros_like(out_ref)

        part = LOCAL // 3
        for i in range(3):
            slot = lax.broadcasted_iota(jnp.int32, (part, BLOCK), 0) + i * part
            hot = (slot == rows_ref[0, 0:1, :]) | (slot == rows_ref[0, 1:2, :])
            local[pl.ds(i * part, part), :] = jnp.dot(
                jnp.where(hot, 1.0, 0.0).astype(jnp.bfloat16),
                source_ref[...],
                preferred_element_type=jnp.float32,
            ).astype(jnp.bfloat16)
        for e in range(expert_count):
            at = block * expert_count + e
            size = blocks * expert_count
            begin, goal = plan_ref[size + at], plan_ref[2 * size + at]

            def move(j, carry):
                here = pl.ds(pl.multiple_of((begin + j) * 16, 16), 16)
                there = pl.ds(pl.multiple_of((goal + j) * 16, 16), 16)
                out_ref[e, there, :] = local[here, :]
                return carry

            lax.fori_loop(0, plan_ref[at], move, 0)

    return pl.pallas_call(
        kernel,
        grid_spec=pltpu.PrefetchScalarGridSpec(
            num_scalar_prefetch=1,
            grid=(blocks,),
            in_specs=[
                pl.BlockSpec((1, 2, BLOCK), lambda b, plan: (b, 0, 0)),
                pl.BlockSpec((BLOCK, cols), lambda b, plan: (b, 0)),
            ],
            out_specs=pl.BlockSpec((expert_count, ROOM, cols), lambda b, plan: (0, 0, 0)),
            scratch_shapes=[pltpu.VMEM((LOCAL, cols), jnp.bfloat16)],
        ),
        out_shape=jax.ShapeDtypeStruct((expert_count, ROOM, cols), jnp.bfloat16),
        compiler_params=pltpu.CompilerParams(vmem_limit_bytes=VMEM),
        cost_estimate=cost(15),
        name="spread",
    )(plan, rows, source)


def gated_spread(source, rows, plan, chosen, router, expert_count, extra):
    blocks, cols = rows.shape[0], source.shape[1]
    both = cols + extra

    def kernel(
        plan_ref, rows_ref, source_ref, chosen_ref, router_ref, out_ref, gate_ref, pair_ref, local
    ):
        block = pl.program_id(0)

        @pl.when(block == 0)
        def _():
            out_ref[...] = jnp.zeros_like(out_ref)

        logits = jnp.dot(source_ref[...], router_ref[...], preferred_element_type=jnp.float32)
        lane = lax.broadcasted_iota(jnp.int32, logits.shape, 1)
        first, second = lane < expert_count, lane < 2 * expert_count
        expert = jnp.where(first, lane, lane - expert_count)
        top = jnp.max(jnp.where(first, logits, -jnp.inf), axis=-1, keepdims=True)
        raised = jnp.where(second, jnp.exp(logits - top), 0.0)
        gate = raised / jnp.sum(jnp.where(first, raised, 0.0), axis=-1, keepdims=True)
        named = (expert == chosen_ref[:, 0:1]) | (expert == chosen_ref[:, 1:2])
        mixing = jnp.where(named & second, gate, 0.0)
        high = mixing.astype(jnp.bfloat16).astype(jnp.float32)
        pair = jnp.where(first, high, mixing - high).astype(jnp.bfloat16)
        gate_ref[...] = gate
        pair_ref[...] = pair
        part = LOCAL // 3
        for i in range(3):
            slot = lax.broadcasted_iota(jnp.int32, (part, BLOCK), 0) + i * part
            hot = (slot == rows_ref[0, 0:1, :]) | (slot == rows_ref[0, 1:2, :])
            hot = jnp.where(hot, 1.0, 0.0).astype(jnp.bfloat16)
            for begin, end, value in ((0, cols, source_ref[...]), (cols, both, pair)):
                local[pl.ds(i * part, part), begin:end] = jnp.dot(
                    hot, value, preferred_element_type=jnp.float32
                ).astype(jnp.bfloat16)
        for e in range(expert_count):
            at = block * expert_count + e
            size = blocks * expert_count
            begin, goal = plan_ref[size + at], plan_ref[2 * size + at]

            def move(j, carry):
                here = pl.ds(pl.multiple_of((begin + j) * 16, 16), 16)
                there = pl.ds(pl.multiple_of((goal + j) * 16, 16), 16)
                out_ref[e, there, :] = local[here, :]
                return carry

            lax.fori_loop(0, plan_ref[at], move, 0)

    return pl.pallas_call(
        kernel,
        grid_spec=pltpu.PrefetchScalarGridSpec(
            num_scalar_prefetch=1,
            grid=(blocks,),
            in_specs=[
                pl.BlockSpec((1, 2, BLOCK), lambda b, plan: (b, 0, 0)),
                pl.BlockSpec((BLOCK, cols), lambda b, plan: (b, 0)),
                pl.BlockSpec((BLOCK, 2), lambda b, plan: (b, 0)),
                pl.BlockSpec(router.shape, lambda b, plan: (0, 0)),
            ],
            out_specs=[
                pl.BlockSpec((expert_count, ROOM, both), lambda b, plan: (0, 0, 0)),
                pl.BlockSpec((BLOCK, extra), lambda b, plan: (b, 0)),
                pl.BlockSpec((BLOCK, extra), lambda b, plan: (b, 0)),
            ],
            scratch_shapes=[pltpu.VMEM((LOCAL, both), jnp.bfloat16)],
        ),
        out_shape=[
            jax.ShapeDtypeStruct((expert_count, ROOM, both), jnp.bfloat16),
            jax.ShapeDtypeStruct((blocks * BLOCK, extra), jnp.float32),
            jax.ShapeDtypeStruct((blocks * BLOCK, extra), jnp.bfloat16),
        ],
        compiler_params=pltpu.CompilerParams(vmem_limit_bytes=VMEM),
        cost_estimate=cost(20),
        name="gated_spread",
    )(plan, rows, source, chosen, router)


def collect(buffers, columns, plan, kept, after):
    each, room, cols = buffers[0].shape
    expert_count = each * len(buffers)
    blocks = columns.shape[0] // BLOCK
    extra = cols - kept

    def kernel(plan_ref, columns_ref, *refs):
        held, refs = refs[: len(buffers)], refs[len(buffers) + len(after) :]
        out_ref, local = refs[0], refs[-1]
        block = pl.program_id(0)

        @pl.when(block == 0)
        def _():
            local[...] = jnp.zeros_like(local)

        for e in range(expert_count):
            at = block * expert_count + e
            size = blocks * expert_count
            begin, goal = plan_ref[size + at], plan_ref[2 * size + at]

            def move(j, carry):
                here = pl.ds(pl.multiple_of((begin + j) * 16, 16), 16)
                there = pl.ds(pl.multiple_of((goal + j) * 16, 16), 16)
                local[here, :] = held[e // each][e % each, there, :]
                return carry

            lax.fori_loop(0, plan_ref[at], move, 0)
        part = BLOCK // 2
        for i in range(2):
            rows = pl.ds(i * part, part)
            slot = lax.broadcasted_iota(jnp.int32, (part, LOCAL), 1)
            hot = (slot == columns_ref[rows, 0:1]) | (slot == columns_ref[rows, 1:2])
            total = jnp.dot(
                jnp.where(hot, 1.0, 0.0).astype(jnp.bfloat16),
                local[...],
                preferred_element_type=jnp.float32,
            )
            out_ref[rows, :] = total[:, :kept].astype(jnp.bfloat16)
            if extra:
                refs[1][rows, :] = total[:, kept:]

    out_specs = [pl.BlockSpec((BLOCK, kept), lambda b, plan: (b, 0))]
    out_shape = [jax.ShapeDtypeStruct((blocks * BLOCK, kept), jnp.bfloat16)]
    if extra:
        out_specs.append(pl.BlockSpec((BLOCK, extra), lambda b, plan: (b, 0)))
        out_shape.append(jax.ShapeDtypeStruct((blocks * BLOCK, extra), jnp.float32))
    return pl.pallas_call(
        kernel,
        grid_spec=pltpu.PrefetchScalarGridSpec(
            num_scalar_prefetch=1,
            grid=(blocks,),
            in_specs=[
                pl.BlockSpec((BLOCK, 2), lambda b, plan: (b, 0)),
            ]
            + [pl.BlockSpec((each, room, cols), lambda b, plan: (0, 0, 0))] * len(buffers)
            + [pl.BlockSpec(memory_space=pl.ANY)] * len(after),
            out_specs=out_specs,
            scratch_shapes=[pltpu.VMEM((LOCAL, cols), jnp.bfloat16)],
        ),
        out_shape=out_shape,
        compiler_params=pltpu.CompilerParams(vmem_limit_bytes=VMEM),
        cost_estimate=cost(16),
        name="collect",
    )(plan, columns, *buffers, *after)


GELU_A = 0.7978845608028654
GELU_B = 0.044715


def expert_pass(inputs, grads, up_weight, up_bias, down_weight, tiles, first, count, after):
    expert_count, room, cols = inputs.shape
    width, hidden = up_weight.shape[1:]

    def kernel(
        tiles_ref, x_ref, g_ref, up_ref, bias_ref, down_ref, *refs
    ):
        y_ref, dx_ref, dup_ref, ddown_ref, dbias_ref, mixed, dpre = refs[len(after) :]
        step = pl.program_id(0)
        expert = step + first

        @pl.when(step == 0)
        def _():
            mixed[...] = jnp.zeros_like(mixed)
            dpre[...] = jnp.zeros_like(dpre)

        dbias_ref[...] = jnp.zeros_like(dbias_ref)
        lane = lax.broadcasted_iota(jnp.int32, (TILE, cols - width), 1)

        def tile(r, carry):
            rows = pl.ds(pl.multiple_of(r * TILE, TILE), TILE)
            x = x_ref[0, rows, :width]
            g = g_ref[0, rows, :]
            gates = x_ref[0, rows, width:].astype(jnp.float32)
            own = (lane == expert) | (lane == expert + expert_count)
            mix = jnp.sum(jnp.where(own, gates, 0.0), axis=1, keepdims=True)
            pre = jnp.dot(x, up_ref[0], preferred_element_type=jnp.float32)
            pre = pre + bias_ref[0].astype(jnp.float32)
            back = lax.dot_general(
                g, down_ref[0], (((1,), (1,)), ((), ())), preferred_element_type=jnp.float32
            )
            square = pre * pre
            bend = jnp.tanh(pre * (GELU_A + GELU_A * GELU_B * square))
            upper = 0.5 + 0.5 * bend
            act = pre * upper
            slope = upper + 0.5 * pre * (1.0 - bend * bend) * (
                GELU_A + 3.0 * GELU_A * GELU_B * square
            )
            dot = jnp.sum(act * back, axis=1, keepdims=True)
            act_low = (mix * act).astype(jnp.bfloat16)
            down = (mix * back * slope).astype(jnp.bfloat16)
            mixed[rows, :] = act_low
            dpre[rows, :] = down
            dbias_ref[0] += jnp.sum(down.astype(jnp.float32), axis=0, keepdims=True)
            y_ref[0, rows, :] = jnp.dot(
                act_low, down_ref[0], preferred_element_type=jnp.float32
            ).astype(jnp.bfloat16)
            dx_ref[0, rows, :width] = lax.dot_general(
                down, up_ref[0], (((1,), (1,)), ((), ())), preferred_element_type=jnp.float32
            ).astype(jnp.bfloat16)
            high = dot.astype(jnp.bfloat16).astype(jnp.float32)
            dx_ref[0, rows, width:] = jnp.where(
                lane == expert, high, jnp.where(lane == expert + expert_count, dot - high, 0.0)
            ).astype(jnp.bfloat16)
            return carry

        lax.fori_loop(0, tiles_ref[expert], tile, 0)

        def weights(depth):
            rows = pl.ds(0, depth)
            for i in range(width // TILE):
                part = pl.ds(i * TILE, TILE)
                dup_ref[0, part, :] = lax.dot_general(
                    x_ref[0, rows, part], dpre[rows, :], (((0,), (0,)), ((), ())),
                    preferred_element_type=jnp.float32,
                ).astype(jnp.bfloat16)
                ddown_ref[0, part, :] = lax.dot_general(
                    g_ref[0, rows, part], mixed[rows, :], (((0,), (0,)), ((), ())),
                    preferred_element_type=jnp.float32,
                ).astype(jnp.bfloat16)

        pl.when(tiles_ref[expert] <= 3)(lambda: weights(3 * TILE))
        pl.when(tiles_ref[expert] > 3)(lambda: weights(room))

    def whole(*dims):
        return pl.BlockSpec((1, *dims), lambda e, tiles: (e + first, 0, 0))

    def own(*dims):
        return pl.BlockSpec((1, *dims), lambda e, tiles: (e, 0, 0))

    shapes = [
        ((room, width), jnp.bfloat16),
        ((room, cols), jnp.bfloat16),
        ((width, hidden), jnp.bfloat16),
        ((width, hidden), jnp.bfloat16),
        ((1, hidden), jnp.float32),
    ]
    return pl.pallas_call(
        kernel,
        grid_spec=pltpu.PrefetchScalarGridSpec(
            num_scalar_prefetch=1,
            grid=(count,),
            in_specs=[
                whole(room, cols),
                whole(room, width),
                whole(width, hidden),
                whole(1, hidden),
                whole(hidden, width),
            ]
            + [pl.BlockSpec(memory_space=pl.ANY)] * len(after),
            out_specs=[own(*dims) for dims, _ in shapes],
            scratch_shapes=[pltpu.VMEM((room, hidden), jnp.bfloat16)] * 2,
        ),
        out_shape=[jax.ShapeDtypeStruct((count, *dims), kind) for dims, kind in shapes],
        compiler_params=pltpu.CompilerParams(vmem_limit_bytes=VMEM),
        cost_estimate=pl.CostEstimate(
            flops=count * 12 * 768 * width * hidden,
            bytes_accessed=count * (4 * room * (cols + width) + 8 * width * hidden),
            transcendentals=count * 768 * hidden,
        ),
        name="experts",
    )(tiles, inputs, grads, up_weight, up_bias[:, None, :], down_weight, *after)


def call(kernel, name, grid, ins, outs, after=(), scratch=(), us=5, each=1, turn=None):
    turn = jnp.zeros((1,), jnp.int32) if turn is None else turn

    def spec(shape, split):
        zeros = (0,) * (len(shape) - 1)
        if split == "turned":
            return pl.BlockSpec((each, *shape[1:]), lambda i, t: ((i + t[0]) % grid, *zeros))
        if split:
            return pl.BlockSpec((each, *shape[1:]), lambda i, t: (i, *zeros))
        return pl.BlockSpec(tuple(shape), lambda i, t: (0, *zeros))

    count, late = len(ins), len(after)

    def body(turn_ref, *refs):
        kernel(*refs[:count], *refs[count + late :])

    return pl.pallas_call(
        body,
        grid_spec=pltpu.PrefetchScalarGridSpec(
            num_scalar_prefetch=1,
            grid=(grid,),
            in_specs=[spec(a.shape, split) for a, split in ins]
            + [pl.BlockSpec(memory_space=pl.ANY)] * late,
            out_specs=[spec(a.shape, split) for a, split in outs],
            scratch_shapes=list(scratch),
        ),
        out_shape=[a for a, _ in outs],
        compiler_params=pltpu.CompilerParams(vmem_limit_bytes=VMEM),
        cost_estimate=cost(us),
        name=name,
    )(turn, *[a for a, _ in ins], *after)


def shape_of(dims, kind):
    return jax.ShapeDtypeStruct(tuple(dims), kind)


def normal(x):
    centered = x - jnp.mean(x, axis=-1, keepdims=True)
    spread_of = lax.rsqrt(jnp.mean(centered * centered, axis=-1, keepdims=True) + EPSILON)
    return centered * spread_of, spread_of


def contract(left, right, left_dim, right_dim):
    return lax.dot_general(
        left, right, (((left_dim,), (right_dim,)), ((), ())), preferred_element_type=jnp.float32
    )


def head_masks(width):
    lane = lax.broadcasted_iota(jnp.int32, (1, width), 1)
    return [(lane >= h * HD) & (lane < (h + 1) * HD) for h in range(width // HD)]


def head_probs(q, k, mask):
    own = jnp.where(mask, q, jnp.zeros_like(q)) * jnp.bfloat16(HD ** (-0.5))
    scores = contract(own, k, 1, 1)
    column = lax.broadcasted_iota(jnp.int32, scores.shape, 1)
    scores = jnp.where(column < SEQ, scores, -1e30)
    raised = jnp.exp(scores - jnp.max(scores, axis=-1, keepdims=True))
    return raised * (1.0 / jnp.sum(raised, axis=-1, keepdims=True))


def attention_forward(x, turn, gain, shift, weight, bias, out_weight):
    images, seq, width = x.shape
    rows, inner = ROWS, weight.shape[2]

    def kernel(
        x_ref, gain_ref, shift_ref, w_ref, b_ref, wo_ref,
        part_ref, pad_ref, n_ref, q_ref, k_ref, v_ref, o_ref, held,
    ):
        held[...] = jnp.zeros_like(held)
        for i in range(PAIR):
            held[i, :seq, :] = x_ref[i].astype(jnp.float32)
        value = held[...].reshape(PAIR * rows, width)
        pad_ref[...] = value.astype(jnp.bfloat16).reshape(PAIR, rows, width)
        n = (normal(value)[0] * gain_ref[...] + shift_ref[...]).astype(jnp.bfloat16)
        n_ref[...] = n.reshape(PAIR, rows, width)
        for j, ref in enumerate((q_ref, k_ref, v_ref)):
            made = jnp.dot(n, w_ref[j], preferred_element_type=jnp.float32) + b_ref[j : j + 1, :]
            ref[...] = made.astype(jnp.bfloat16).reshape(PAIR, rows, inner)
        for i in range(PAIR):
            q, k, v = q_ref[i], k_ref[i], v_ref[i]
            mixed = jnp.zeros((rows, inner), jnp.float32)
            for mask in head_masks(inner):
                probs = head_probs(q, k, mask).astype(jnp.bfloat16)
                head = jnp.dot(probs, v, preferred_element_type=jnp.float32)
                mixed = jnp.where(mask, head, mixed)
            o_ref[i] = mixed.astype(jnp.bfloat16)
        mixed = o_ref[...].reshape(PAIR * rows, inner)
        part = jnp.dot(mixed, wo_ref[...], preferred_element_type=jnp.float32)
        part_ref[...] = part.astype(jnp.bfloat16).reshape(PAIR, rows, width)

    wide = shape_of((images, rows, width), jnp.bfloat16)
    slim = shape_of((images, rows, inner), jnp.bfloat16)
    return call(
        kernel, "attention_forward", images // PAIR,
        [(x, "turned"), (gain, False), (shift, False), (weight, False), (bias, False), (out_weight, False)],
        [(wide, True)] * 3 + [(slim, True)] * 4,
        scratch=[pltpu.VMEM((PAIR, rows, width), jnp.float32)], each=PAIR, turn=turn,
        us=20,
    )


def attention_backward(da, x, n, q, k, v, o, weight, out_weight, after):
    images, rows, width = x.shape
    inner = weight.shape[2]

    def kernel(
        da_ref, x_ref, n_ref, q_ref, k_ref, v_ref, o_ref, w_ref, wo_ref,
        back_ref, dw_ref, dwo_ref, dbias_ref, sums_ref, held,
    ):
        @pl.when(pl.program_id(0) == 0)
        def _():
            dw_ref[...] = jnp.zeros_like(dw_ref)
            dwo_ref[...] = jnp.zeros_like(dwo_ref)
            dbias_ref[...] = jnp.zeros_like(dbias_ref)
            sums_ref[...] = jnp.zeros_like(sums_ref)

        joined = PAIR * rows
        da = da_ref[...].reshape(joined, width)
        do_all = contract(da, wo_ref[...], 1, 1).astype(jnp.bfloat16).reshape(PAIR, rows, inner)
        scale = HD ** (-0.5)
        for i in range(PAIR):
            q, k, v, do = q_ref[i], k_ref[i], v_ref[i], do_all[i]
            dq = dk = dv = jnp.zeros((rows, inner), jnp.float32)
            for mask in head_masks(inner):
                probs = head_probs(q, k, mask)
                dv = jnp.where(mask, contract(probs.astype(jnp.bfloat16), do, 0, 0), dv)
                dp = contract(jnp.where(mask, do, jnp.zeros_like(do)), v, 1, 1)
                ds = probs * (dp - jnp.sum(probs * dp, axis=-1, keepdims=True))
                ds = ds.astype(jnp.bfloat16)
                dq = jnp.where(mask, jnp.dot(ds, k, preferred_element_type=jnp.float32), dq)
                dk = jnp.where(mask, contract(ds, q, 0, 0), dk)
            held[0, i] = (dq * scale).astype(jnp.bfloat16)
            held[1, i] = (dk * scale).astype(jnp.bfloat16)
            held[2, i] = dv.astype(jnp.bfloat16)
        n = n_ref[...].reshape(joined, width)
        back = jnp.zeros((joined, width), jnp.float32)
        for j in range(3):
            grad = held[j].reshape(joined, inner)
            dw_ref[j] += contract(n, grad, 0, 0)
            back += contract(grad, w_ref[j], 1, 1)
            if j != 1:
                dbias_ref[j // 2 : j // 2 + 1, :] += jnp.sum(
                    grad.astype(jnp.float32), axis=0, keepdims=True
                )
        dwo_ref[0] += contract(da, o_ref[...].reshape(joined, inner), 0, 0)
        back_ref[...] = back.astype(jnp.bfloat16).reshape(PAIR, rows, width)
        unit, _ = normal(x_ref[...].reshape(joined, width).astype(jnp.float32))
        sums_ref[0:1, :] += jnp.sum(back * unit, axis=0, keepdims=True)
        sums_ref[1:2, :] += jnp.sum(back, axis=0, keepdims=True)
        sums_ref[2:3, :] += jnp.sum(da.astype(jnp.float32), axis=0, keepdims=True)

    return call(
        kernel, "attention_backward", images // PAIR,
        [(a, True) for a in (da, x, n, q, k, v, o)] + [(weight, False), (out_weight, False)],
        [
            (shape_of((images, rows, width), jnp.bfloat16), True),
            (shape_of((3, width, inner), jnp.float32), False),
            (shape_of((1, width, inner), jnp.float32), False),
            (shape_of((2, inner), jnp.float32), False),
            (shape_of((3, width), jnp.float32), False),
        ],
        after=after, each=PAIR, us=30,
        scratch=[pltpu.VMEM((3, PAIR, rows, inner), jnp.bfloat16)],
    )


def middle_norm(near, far, x, out_bias, gain, shift, after):
    def kernel(near_ref, far_ref, x_ref, bias_ref, gain_ref, shift_ref, middle_ref, n_ref):
        total = near_ref[0].astype(jnp.float32) + far_ref[0].astype(jnp.float32)
        middle = x_ref[0].astype(jnp.float32) + total + bias_ref[...]
        middle_ref[0] = middle
        n_ref[0] = (normal(middle)[0] * gain_ref[...] + shift_ref[...]).astype(jnp.bfloat16)

    return call(
        kernel, "middle_norm", near.shape[0],
        [(near, True), (far, True), (x, True), (out_bias, False), (gain, False), (shift, False)],
        [(shape_of(near.shape, jnp.float32), True), (shape_of(near.shape, jnp.bfloat16), True)],
        after=after, us=8,
    )


def norm_back(dn, unit, spread_of, gain):
    dz = dn * gain
    mean = jnp.mean(dz, axis=-1, keepdims=True)
    return spread_of * (dz - mean - unit * jnp.mean(dz * unit, axis=-1, keepdims=True))


def middle_back(near, far, dots, gates, chosen, pair, n, router_weight, down_bias, middle, upstream, gain, after):
    count, wide = down_bias.shape[0], pair.shape[2]

    def kernel(
        near_ref, far_ref, dots_ref, gates_ref, chosen_ref, pair_ref, n_ref, router_ref, bias_ref,
        middle_ref, g_ref, gain_ref, grad_ref, da_ref, sums_ref, drouter_ref, dbias_ref,
    ):
        @pl.when(pl.program_id(0) == 0)
        def _():
            sums_ref[...] = jnp.zeros_like(sums_ref)
            drouter_ref[...] = jnp.zeros_like(drouter_ref)
            dbias_ref[...] = jnp.zeros_like(dbias_ref)

        g = g_ref[0]
        lane = lax.broadcasted_iota(jnp.int32, (g.shape[0], count), 1)
        named = (lane == chosen_ref[0, :, 0:1]) | (lane == chosen_ref[0, :, 1:2])
        dmix = dots_ref[0] + jnp.where(named, contract(g, bias_ref[...], 1, 1), 0.0)
        gate = gates_ref[0, :, :count]
        dlogits = gate * (dmix - jnp.sum(gate * dmix, axis=-1, keepdims=True))
        dlogits = dlogits.astype(jnp.bfloat16)
        drouter_ref[...] += contract(dlogits, n_ref[0], 0, 0)
        dbias_ref[...] += contract(pair_ref[0], g, 0, 0)
        dn = near_ref[0].astype(jnp.float32) + far_ref[0].astype(jnp.float32)
        dn = dn + contract(dlogits, router_ref[...], 1, 1)
        unit, spread_of = normal(middle_ref[0])
        grad = g.astype(jnp.float32) + norm_back(dn, unit, spread_of, gain_ref[...])
        grad_ref[0] = grad
        da_ref[0] = grad.astype(jnp.bfloat16)
        sums_ref[0:1, :] += jnp.sum(dn * unit, axis=0, keepdims=True)
        sums_ref[1:2, :] += jnp.sum(dn, axis=0, keepdims=True)

    width = middle.shape[2]
    return call(
        kernel, "middle_back", middle.shape[0],
        [(a, True) for a in (near, far, dots, gates, chosen, pair, n)]
        + [(router_weight, False), (down_bias, False), (middle, True), (upstream, True), (gain, False)],
        [
            (shape_of(middle.shape, jnp.float32), True),
            (shape_of(middle.shape, jnp.bfloat16), True),
            (shape_of((2, width), jnp.float32), False),
            (shape_of((count, width), jnp.float32), False),
            (shape_of((wide, width), jnp.float32), False),
        ],
        after=after, us=8,
    )


def finish(near, far, middle, pair, down_bias, after):
    def kernel(near_ref, far_ref, middle_ref, pair_ref, bias_ref, out_ref):
        total = near_ref[0].astype(jnp.float32) + far_ref[0].astype(jnp.float32)
        total = total + jnp.dot(pair_ref[0], bias_ref[...], preferred_element_type=jnp.float32)
        out_ref[0] = (middle_ref[0] + total).astype(jnp.bfloat16)

    return call(
        kernel, "finish", middle.shape[0],
        [(near, True), (far, True), (middle, True), (pair, True), (down_bias, False)],
        [(shape_of(middle.shape, jnp.bfloat16), True)],
        after=after, us=8,
    )[0]


def input_back(own, other, x, own_grad, other_grad, gain, turn, after):
    images, _, width = x.shape
    half = images // 2

    def kernel(turn_ref, own_ref, other_ref, x_ref, own_grad_ref, other_grad_ref, gain_ref, *refs):
        out_ref = refs[-1]
        step = pl.program_id(0)
        place = (step + turn_ref[0]) % images
        mine = step < half
        dn = jnp.where(mine, own_ref[0], other_ref[0]).astype(jnp.float32)
        unit, spread_of = normal(x_ref[0].astype(jnp.float32))
        grad = jnp.where(mine, own_grad_ref[0], other_grad_ref[0])
        grad = grad + norm_back(dn, unit, spread_of, gain_ref[...])
        for j in range(images):

            @pl.when(place == j)
            def _():
                out_ref[j * SEQ : (j + 1) * SEQ, :] = grad[:SEQ]

    def low(shape):
        return pl.BlockSpec((1, *shape[1:]), lambda i, t: (jnp.minimum(i, half - 1), 0, 0))

    def high(shape):
        return pl.BlockSpec((1, *shape[1:]), lambda i, t: (jnp.maximum(i - half, 0), 0, 0))

    return pl.pallas_call(
        kernel,
        grid_spec=pltpu.PrefetchScalarGridSpec(
            num_scalar_prefetch=1,
            grid=(images,),
            in_specs=[
                low(own.shape),
                high(other.shape),
                pl.BlockSpec((1, *x.shape[1:]), lambda i, t: (i, 0, 0)),
                low(own_grad.shape),
                high(other_grad.shape),
                pl.BlockSpec(gain.shape, lambda i, t: (0, 0)),
            ]
            + [pl.BlockSpec(memory_space=pl.ANY)] * len(after),
            out_specs=pl.BlockSpec((images * SEQ, width), lambda i, t: (0, 0)),
        ),
        out_shape=jax.ShapeDtypeStruct((images * SEQ, width), jnp.float32),
        compiler_params=pltpu.CompilerParams(vmem_limit_bytes=VMEM),
        cost_estimate=cost(15),
        name="input_back",
    )(turn, own, other, x, own_grad, other_grad, gain, *after)


def to_core(value):
    return lax.ppermute(value, "tensor", pairs(lax.axis_size("tensor"), 1))


def across(value):
    return lax.ppermute(value, "tensor", pairs(lax.axis_size("tensor"), 2))


def core_sum(part, zero):
    half = part.shape[0] // 2
    got = to_core(part[half:])
    return (part[:half].astype(jnp.float32) + got.astype(jnp.float32) + zero).astype(jnp.bfloat16)


def zero_of(value):
    return value[(0,) * value.ndim].astype(jnp.float32) * 0.0


def ring_owner(way, step):
    index = lax.axis_index("dp")
    place = jnp.where(index % 2 == 0, index // 2, 7 - index // 2)
    place = (place - way * (step + 1)) % 8
    return jnp.where(place < 4, 2 * place, 15 - 2 * place).astype(jnp.int32)


def ring_hop(value, way):
    path = [(RING[i], RING[(i + way) % len(RING)]) for i in range(len(RING))]
    return lax.ppermute(value, "dp", path)


def ring_add(got, sources, steps, kinds, after):
    groups, came = len(sources), got[0].shape[0]
    many, total, cols = sources[0][0].shape
    rows, part = total // 8, 2
    owners = jnp.stack([ring_owner(way, step) for step in steps for way in (1, -1)])
    joint = all(kind == kinds[0] for kind in kinds)

    def kernel(owners_ref, *refs):
        held, locals_, outs = refs[:2], refs[2 : 2 + 2 * groups], refs[2 + 2 * groups + len(after) :]
        for g in range(groups):
            for d in range(2):
                value = locals_[2 * g + d][...]
                if g < came:
                    value = value.astype(jnp.float32) + held[d][g].astype(jnp.float32)
                if joint:
                    outs[d][g] = value.astype(kinds[g])
                else:
                    outs[2 * g + d][0] = value.astype(kinds[g])

    def source(slot):
        return pl.BlockSpec((part, rows, cols), lambda i, own: (i, own[slot], 0))

    def stack(count):
        return pl.BlockSpec((count, part, rows, cols), lambda i, own: (0, i, 0, 0))

    if joint:
        outs = [((groups, many, rows, cols), kinds[0])] * 2
    else:
        outs = [((1, many, rows, cols), kind) for kind in kinds for _ in range(2)]
    return pl.pallas_call(
        kernel,
        grid_spec=pltpu.PrefetchScalarGridSpec(
            num_scalar_prefetch=1,
            grid=(many // part,),
            in_specs=[stack(came)] * 2
            + [source(i) for i in range(2 * groups)]
            + [pl.BlockSpec(memory_space=pl.ANY)] * len(after),
            out_specs=[stack(dims[0]) for dims, _ in outs],
        ),
        out_shape=[jax.ShapeDtypeStruct(dims, kind) for dims, kind in outs],
        compiler_params=pltpu.CompilerParams(vmem_limit_bytes=VMEM),
        cost_estimate=cost(5),
        name="ring_add",
    )(owners, *got, *[piece for pair in sources for piece in pair], *after)


def halving_scatter(values):
    if lax.axis_size("dp") != 8:
        return lax.psum_scatter(values.astype(jnp.bfloat16), "dp", scatter_dimension=1, tiled=True).astype(jnp.float32)
    index = lax.axis_index("dp")
    many, rows, cols = values.shape
    values = values.reshape(many, 2, 2, 2, rows // 8, cols)
    for bit, axis in ((0, 3), (1, 2), (2, 1)):
        mine = (index >> bit) % 2
        keep = lax.dynamic_index_in_dim(values, mine, axis, keepdims=True)
        give = lax.dynamic_index_in_dim(values, 1 - mine, axis, keepdims=True)
        got = lax.ppermute(give.astype(jnp.bfloat16), "dp", pairs(8, 1 << bit))
        values = keep.astype(jnp.float32) + got.astype(jnp.float32)
    return values.reshape(many, rows // 8, cols)


def on_device(
    embedded,
    attn_gain,
    attn_shift,
    qkv_weight,
    qv_bias,
    out_weight,
    out_bias,
    moe_gain,
    moe_shift,
    router_weight,
    up_weight,
    up_bias,
    down_weight,
    down_bias,
    routes,
    cotangent,
):
    tok_rows, width = embedded.shape
    images = tok_rows // SEQ
    half = images // 2
    head_width = qkv_weight.shape[2]
    expert_count = up_weight.shape[0]
    core = lax.axis_index("tensor") % 2
    f32 = jnp.float32

    def own_first(value, fill):
        value = value.reshape(images, SEQ, value.shape[1])
        value = jnp.pad(value, ((0, 0), (0, ROWS - SEQ), (0, 0)), constant_values=fill)
        return jnp.where(core == 0, value, jnp.roll(value, half, axis=0))

    def in_order(own, other):
        low = jnp.where(core == 0, own, other)
        high = jnp.where(core == 0, other, own)
        return jnp.concatenate([low, high])[:, :SEQ].reshape(tok_rows, width)

    def row(value):
        return value.astype(f32)[None]

    def imaged(value):
        return value.reshape(images, ROWS, value.shape[1])

    turn = (half * core).astype(jnp.int32)[None]
    bias_rows = jnp.stack([qv_bias[0], jnp.zeros_like(qv_bias[0]), qv_bias[1]]).astype(f32)
    part, x, normed, queries, keys, values, mixed = attention_forward(
        embedded.reshape(images, SEQ, width), turn // PAIR, row(attn_gain), row(attn_shift),
        qkv_weight, bias_rows, out_weight,
    )
    near = core_sum(part, 0.0)
    far = across(near)

    chosen = own_first(routes, -1).reshape(images * ROWS, 2)
    rows, columns, plan, tiles = route_plan(chosen, expert_count)
    upstream = own_first(cotangent, 0)
    grad_buffers = spread(upstream.reshape(images * ROWS, width), rows, plan, expert_count)

    middle, own_normed = middle_norm(
        near, far, x, row(out_bias), row(moe_gain), row(moe_shift), (grad_buffers,)
    )
    moe_normed = jnp.concatenate([own_normed, to_core(own_normed)]).reshape(images * ROWS, width)
    extra = 128
    router_twice = jnp.pad(
        jnp.concatenate([router_weight, router_weight], axis=1),
        ((0, 0), (0, extra - 2 * expert_count)),
    )
    bias_twice = jnp.pad(
        jnp.concatenate([down_bias, down_bias]), ((0, extra - 2 * expert_count), (0, 0))
    )
    buffers, gates, mix_pair = gated_spread(
        moe_normed, rows, plan, chosen, router_twice, expert_count, extra
    )
    gates, mix_pair, chosen = imaged(gates), imaged(mix_pair), imaged(chosen)
    group = expert_count // GROUPS

    def experts_of(i, after):
        return expert_pass(
            buffers, grad_buffers, up_weight, up_bias, down_weight, tiles, i * group, group, after
        )

    ringed = lax.axis_size("dp") == len(RING)
    low = jnp.bfloat16
    y_first, back_first, *first, bias_first = experts_of(0, ())
    moving = ()
    if ringed:
        rows_each = width // 8
        moving = [
            lax.dynamic_slice_in_dim(grad, ring_owner(way, 0) * rows_each, rows_each, 1)[None]
            for grad, way in zip(first, (1, -1))
        ]
    y_second, back_second, *second, bias_second = experts_of(1, tuple(moving))

    def round_trip(step, kinds, *after):
        if not ringed:
            return ()
        got = [ring_hop(value, way) for value, way in zip(moving, (1, -1))]
        if step < 8:
            return ring_add(got, [first, second], [step, step - 1], kinds, after)
        return ring_add(got, [second], [step - 1], kinds, after)

    moving = round_trip(1, [low, low])
    back_part, dots = collect((back_first, back_second), columns, plan, width, tuple(moving))
    back_near = core_sum(imaged(back_part), 0.0)
    back_far = across(back_near)
    dots = dots[:, : 2 * expert_count].T
    dots = dots[:expert_count] + dots[expert_count:]
    own_rows = half * ROWS
    dots = dots[:, :own_rows] + to_core(dots[:, own_rows:])
    dots = (dots + across(dots)).T.reshape(half, ROWS, expert_count)
    moving = round_trip(2, [low, low], back_near)
    (moe_part,) = collect((y_first, y_second), columns, plan, width, (back_near, *moving))
    moving = round_trip(3, [low, low], moe_part)
    middle_grad, own_da, moe_sums, router_sums, bias_sums = middle_back(
        back_near, back_far, dots, gates, chosen, mix_pair, imaged(moe_normed), router_weight,
        down_bias, middle, upstream, row(moe_gain), tuple(moving),
    )
    da = jnp.concatenate([own_da, to_core(own_da)])
    y_near = core_sum(imaged(moe_part), zero_of(own_da))
    y_far = across(y_near)
    other_grad = to_core(middle_grad)
    moving = round_trip(4, [low, low], own_da)
    normed_back, grad_qkv, grad_out, grad_qv_bias, sums = attention_backward(
        da, x, normed, queries, keys, values, mixed, qkv_weight, out_weight, (y_near, *moving)
    )
    last_near = core_sum(normed_back, 0.0)
    last_far = across(last_near)
    moving = round_trip(5, [low, low], last_near)
    near_zero = zero_of(last_near)
    own_out = finish(y_near, y_far, middle, mix_pair, bias_twice, (last_near,))
    layer_out = in_order(own_out, to_core(own_out))
    router_bias = [router_sums, bias_sums[:expert_count] + bias_sums[expert_count : 2 * expert_count]]
    tensor_parts = jnp.concatenate([sums[:2]] + [0.5 * part for part in (moe_sums, *router_bias)])
    packed = jnp.concatenate(
        [
            small_sum(tensor_parts + near_zero, "tensor"),
            sums[2:],
            jnp.pad(grad_qv_bias, ((0, 0), (0, width - head_width))),
            bias_first[:, 0],
            bias_second[:, 0],
        ]
    )
    packed = small_sum(packed, "dp")
    slim = halving_scatter(jnp.concatenate([grad_qkv, grad_out]) + near_zero)
    if ringed:
        moving = round_trip(6, [low, low])
        up_first, down_first, *moving = round_trip(7, [f32, low])
        up_second, down_second = round_trip(8, [f32])
    else:
        up_first, down_first, up_second, down_second = [
            lax.psum_scatter(grad, "dp", scatter_dimension=1, tiled=True).astype(f32)[None]
            for grad in (*first, *second)
        ]
    grad_up = jnp.concatenate([up_first[0], up_second[0]])
    grad_down = jnp.concatenate([down_first[0], down_second[0]]).transpose(0, 2, 1)
    last = (last_near.astype(f32) + last_far.astype(f32)).astype(jnp.bfloat16)
    grad_embedded = input_back(
        last, to_core(last), x, middle_grad, other_grad, row(attn_gain), turn,
        (layer_out, packed, slim),
    )
    base = 4 + 2 * expert_count
    return (
        layer_out,
        grad_embedded,
        packed[0],
        packed[1],
        slim[:3],
        packed[base + 1 : base + 3, :head_width],
        slim[3].T,
        packed[base],
        packed[2],
        packed[3],
        packed[4 : 4 + expert_count].T,
        grad_up,
        packed[base + 3 :],
        grad_down,
        packed[4 + expert_count : base],
    )


def solution(mesh):
    return jax.shard_map(
        on_device,
        mesh=mesh,
        in_specs=(
            P("dp", None),
            P(),
            P(),
            P(None, None, "tensor"),
            P(None, "tensor"),
            P("tensor", None),
            P(),
            P(),
            P(),
            P(),
            P(None, None, "tensor"),
            P(None, "tensor"),
            P(None, "tensor", None),
            P(),
            P("dp", None),
            P("dp", None),
        ),
        out_specs=(
            P("dp", None),
            P("dp", None),
            P(),
            P(),
            P(None, "dp", "tensor"),
            P(None, "tensor"),
            P("tensor", "dp"),
            P(),
            P(),
            P(),
            P(),
            P(None, "dp", "tensor"),
            P(None, "tensor"),
            P(None, "tensor", "dp"),
            P(),
        ),
        check_vma=False,
    )
```

```python
import jax
import jax.numpy as jnp
from jax import lax
from jax.experimental import pallas as pl
from jax.experimental.pallas import tpu as pltpu
from jax.sharding import PartitionSpec as P

SEQ = 197
HD = 64
EPSILON = 1e-06
RING = (0, 2, 4, 6, 7, 5, 3, 1)


def pairs(count, bit):
    return [(i, i ^ bit) for i in range(count)]


def small_sum(values, axis):
    count = lax.axis_size(axis)
    if count not in (4, 8):
        return lax.psum(values, axis)
    bit = 1
    while bit < count:
        values = values + lax.ppermute(values, axis, pairs(count, bit))
        bit *= 2
    return values


ROWS = 208
PAIR = 2
TRIO = 3
BLOCK = 416
GROUPS = 2
LOCAL = 960
ROOM = 1024
TILE = 256
VMEM = 56 * 1024 * 1024


def cost(us):
    return pl.CostEstimate(flops=int(us * 1.1e9), bytes_accessed=0, transcendentals=0)


def route_plan(routes, expert_count):
    tokens = routes.shape[0]
    blocks = -(-tokens // BLOCK)
    padded = jnp.pad(routes.T, ((0, 0), (0, blocks * BLOCK - tokens)), constant_values=-1)
    experts = jnp.arange(expert_count, dtype=jnp.int32)[:, None]
    first = padded[0][None, :] == experts
    second = padded[1][None, :] == experts
    named = (first | second).reshape(expert_count * blocks, BLOCK)
    ahead = jnp.arange(BLOCK)[:, None] < jnp.arange(BLOCK)[None, :]
    rank = jnp.dot(
        named.astype(jnp.bfloat16), ahead.astype(jnp.bfloat16), preferred_element_type=jnp.float32
    )
    rank = rank.astype(jnp.int32).reshape(expert_count, blocks, BLOCK)
    chunks = (jnp.sum(named.astype(jnp.int32), axis=1).reshape(expert_count, blocks) + 15) // 16
    inside = jnp.cumsum(chunks, axis=0) - chunks
    offset = jnp.cumsum(chunks, axis=1) - chunks
    place = (rank + 16 * inside[:, :, None]).reshape(expert_count, blocks * BLOCK)
    target = jnp.stack(
        [jnp.sum(jnp.where(hot, place + 1, 0), axis=0) - 1 for hot in (first, second)]
    )
    tiles = (jnp.sum(chunks, axis=1) * 16 + TILE - 1) // TILE
    plan = jnp.concatenate([chunks.T.reshape(-1), inside.T.reshape(-1), offset.T.reshape(-1)])
    rows = target.reshape(2, blocks, BLOCK).transpose(1, 0, 2)
    return rows, target.T, plan, tiles


def spread(source, rows, plan, expert_count):
    blocks, cols = rows.shape[0], source.shape[1]

    def kernel(plan_ref, rows_ref, source_ref, out_ref, local):
        block = pl.program_id(0)

        @pl.when(block == 0)
        def _():
            out_ref[...] = jnp.zeros_like(out_ref)

        part = LOCAL // 3
        for i in range(3):
            slot = lax.broadcasted_iota(jnp.int32, (part, BLOCK), 0) + i * part
            hot = (slot == rows_ref[0, 0:1, :]) | (slot == rows_ref[0, 1:2, :])
            local[pl.ds(i * part, part), :] = jnp.dot(
                jnp.where(hot, 1.0, 0.0).astype(jnp.bfloat16),
                source_ref[...],
                preferred_element_type=jnp.float32,
            ).astype(jnp.bfloat16)
        for e in range(expert_count):
            at = block * expert_count + e
            size = blocks * expert_count
            begin, goal = plan_ref[size + at], plan_ref[2 * size + at]

            def move(j, carry):
                here = pl.ds(pl.multiple_of((begin + j) * 16, 16), 16)
                there = pl.ds(pl.multiple_of((goal + j) * 16, 16), 16)
                out_ref[e, there, :] = local[here, :]
                return carry

            lax.fori_loop(0, plan_ref[at], move, 0)

    return pl.pallas_call(
        kernel,
        grid_spec=pltpu.PrefetchScalarGridSpec(
            num_scalar_prefetch=1,
            grid=(blocks,),
            in_specs=[
                pl.BlockSpec((1, 2, BLOCK), lambda b, plan: (b, 0, 0)),
                pl.BlockSpec((BLOCK, cols), lambda b, plan: (b, 0)),
            ],
            out_specs=pl.BlockSpec((expert_count, ROOM, cols), lambda b, plan: (0, 0, 0)),
            scratch_shapes=[pltpu.VMEM((LOCAL, cols), jnp.bfloat16)],
        ),
        out_shape=jax.ShapeDtypeStruct((expert_count, ROOM, cols), jnp.bfloat16),
        compiler_params=pltpu.CompilerParams(vmem_limit_bytes=VMEM),
        cost_estimate=cost(15),
        name="spread",
    )(plan, rows, source)


def gated_spread(source, rows, plan, chosen, router, expert_count, extra):
    blocks, cols = rows.shape[0], source.shape[1]
    both = cols + extra

    def kernel(
        plan_ref, rows_ref, source_ref, chosen_ref, router_ref, out_ref, gate_ref, pair_ref, local
    ):
        block = pl.program_id(0)

        @pl.when(block == 0)
        def _():
            out_ref[...] = jnp.zeros_like(out_ref)

        logits = jnp.dot(source_ref[...], router_ref[...], preferred_element_type=jnp.float32)
        lane = lax.broadcasted_iota(jnp.int32, logits.shape, 1)
        first, second = lane < expert_count, lane < 2 * expert_count
        expert = jnp.where(first, lane, lane - expert_count)
        top = jnp.max(jnp.where(first, logits, -jnp.inf), axis=-1, keepdims=True)
        raised = jnp.where(second, jnp.exp(logits - top), 0.0)
        gate = raised / jnp.sum(jnp.where(first, raised, 0.0), axis=-1, keepdims=True)
        named = (expert == chosen_ref[:, 0:1]) | (expert == chosen_ref[:, 1:2])
        mixing = jnp.where(named & second, gate, 0.0)
        high = mixing.astype(jnp.bfloat16).astype(jnp.float32)
        pair = jnp.where(first, high, mixing - high).astype(jnp.bfloat16)
        gate_ref[...] = gate
        pair_ref[...] = pair
        part = LOCAL // 3
        for i in range(3):
            slot = lax.broadcasted_iota(jnp.int32, (part, BLOCK), 0) + i * part
            hot = (slot == rows_ref[0, 0:1, :]) | (slot == rows_ref[0, 1:2, :])
            hot = jnp.where(hot, 1.0, 0.0).astype(jnp.bfloat16)
            for begin, end, value in ((0, cols, source_ref[...]), (cols, both, pair)):
                local[pl.ds(i * part, part), begin:end] = jnp.dot(
                    hot, value, preferred_element_type=jnp.float32
                ).astype(jnp.bfloat16)
        for e in range(expert_count):
            at = block * expert_count + e
            size = blocks * expert_count
            begin, goal = plan_ref[size + at], plan_ref[2 * size + at]

            def move(j, carry):
                here = pl.ds(pl.multiple_of((begin + j) * 16, 16), 16)
                there = pl.ds(pl.multiple_of((goal + j) * 16, 16), 16)
                out_ref[e, there, :] = local[here, :]
                return carry

            lax.fori_loop(0, plan_ref[at], move, 0)

    return pl.pallas_call(
        kernel,
        grid_spec=pltpu.PrefetchScalarGridSpec(
            num_scalar_prefetch=1,
            grid=(blocks,),
            in_specs=[
                pl.BlockSpec((1, 2, BLOCK), lambda b, plan: (b, 0, 0)),
                pl.BlockSpec((BLOCK, cols), lambda b, plan: (b, 0)),
                pl.BlockSpec((BLOCK, 2), lambda b, plan: (b, 0)),
                pl.BlockSpec(router.shape, lambda b, plan: (0, 0)),
            ],
            out_specs=[
                pl.BlockSpec((expert_count, ROOM, both), lambda b, plan: (0, 0, 0)),
                pl.BlockSpec((BLOCK, extra), lambda b, plan: (b, 0)),
                pl.BlockSpec((BLOCK, extra), lambda b, plan: (b, 0)),
            ],
            scratch_shapes=[pltpu.VMEM((LOCAL, both), jnp.bfloat16)],
        ),
        out_shape=[
            jax.ShapeDtypeStruct((expert_count, ROOM, both), jnp.bfloat16),
            jax.ShapeDtypeStruct((blocks * BLOCK, extra), jnp.float32),
            jax.ShapeDtypeStruct((blocks * BLOCK, extra), jnp.bfloat16),
        ],
        compiler_params=pltpu.CompilerParams(vmem_limit_bytes=VMEM),
        cost_estimate=cost(20),
        name="gated_spread",
    )(plan, rows, source, chosen, router)


def collect(buffers, columns, plan, kept, after):
    each, room, cols = buffers[0].shape
    expert_count = each * len(buffers)
    blocks = columns.shape[0] // BLOCK
    extra = cols - kept

    def kernel(plan_ref, columns_ref, *refs):
        held, refs = refs[: len(buffers)], refs[len(buffers) + len(after) :]
        out_ref, local = refs[0], refs[-1]
        block = pl.program_id(0)

        @pl.when(block == 0)
        def _():
            local[...] = jnp.zeros_like(local)

        for e in range(expert_count):
            at = block * expert_count + e
            size = blocks * expert_count
            begin, goal = plan_ref[size + at], plan_ref[2 * size + at]

            def move(j, carry):
                here = pl.ds(pl.multiple_of((begin + j) * 16, 16), 16)
                there = pl.ds(pl.multiple_of((goal + j) * 16, 16), 16)
                local[here, :] = held[e // each][e % each, there, :]
                return carry

            lax.fori_loop(0, plan_ref[at], move, 0)
        part = BLOCK // 2
        for i in range(2):
            rows = pl.ds(i * part, part)
            slot = lax.broadcasted_iota(jnp.int32, (part, LOCAL), 1)
            hot = (slot == columns_ref[rows, 0:1]) | (slot == columns_ref[rows, 1:2])
            total = jnp.dot(
                jnp.where(hot, 1.0, 0.0).astype(jnp.bfloat16),
                local[...],
                preferred_element_type=jnp.float32,
            )
            out_ref[rows, :] = total[:, :kept].astype(jnp.bfloat16)
            if extra:
                refs[1][rows, :] = total[:, kept:]

    out_specs = [pl.BlockSpec((BLOCK, kept), lambda b, plan: (b, 0))]
    out_shape = [jax.ShapeDtypeStruct((blocks * BLOCK, kept), jnp.bfloat16)]
    if extra:
        out_specs.append(pl.BlockSpec((BLOCK, extra), lambda b, plan: (b, 0)))
        out_shape.append(jax.ShapeDtypeStruct((blocks * BLOCK, extra), jnp.float32))
    return pl.pallas_call(
        kernel,
        grid_spec=pltpu.PrefetchScalarGridSpec(
            num_scalar_prefetch=1,
            grid=(blocks,),
            in_specs=[
                pl.BlockSpec((BLOCK, 2), lambda b, plan: (b, 0)),
            ]
            + [pl.BlockSpec((each, room, cols), lambda b, plan: (0, 0, 0))] * len(buffers)
            + [pl.BlockSpec(memory_space=pl.ANY)] * len(after),
            out_specs=out_specs,
            scratch_shapes=[pltpu.VMEM((LOCAL, cols), jnp.bfloat16)],
        ),
        out_shape=out_shape,
        compiler_params=pltpu.CompilerParams(vmem_limit_bytes=VMEM),
        cost_estimate=cost(16),
        name="collect",
    )(plan, columns, *buffers, *after)


GELU_A = 0.7978845608028654
GELU_B = 0.044715


def expert_pass(inputs, grads, up_weight, up_bias, down_weight, tiles, first, count, after):
    expert_count, room, cols = inputs.shape
    width, hidden = up_weight.shape[1:]

    def kernel(
        tiles_ref, x_ref, g_ref, up_ref, bias_ref, down_ref, *refs
    ):
        y_ref, dx_ref, dup_ref, ddown_ref, dbias_ref, mixed, dpre = refs[len(after) :]
        step = pl.program_id(0)
        expert = step + first

        @pl.when(step == 0)
        def _():
            mixed[...] = jnp.zeros_like(mixed)
            dpre[...] = jnp.zeros_like(dpre)

        dbias_ref[...] = jnp.zeros_like(dbias_ref)
        lane = lax.broadcasted_iota(jnp.int32, (TILE, cols - width), 1)

        def tile(r, carry):
            rows = pl.ds(pl.multiple_of(r * TILE, TILE), TILE)
            x = x_ref[0, rows, :width]
            g = g_ref[0, rows, :]
            gates = x_ref[0, rows, width:].astype(jnp.float32)
            own = (lane == expert) | (lane == expert + expert_count)
            mix = jnp.sum(jnp.where(own, gates, 0.0), axis=1, keepdims=True)
            pre = jnp.dot(x, up_ref[0], preferred_element_type=jnp.float32)
            pre = pre + bias_ref[0].astype(jnp.float32)
            back = lax.dot_general(
                g, down_ref[0], (((1,), (1,)), ((), ())), preferred_element_type=jnp.float32
            )
            square = pre * pre
            bend = jnp.tanh(pre * (GELU_A + GELU_A * GELU_B * square))
            upper = 0.5 + 0.5 * bend
            act = pre * upper
            slope = upper + 0.5 * pre * (1.0 - bend * bend) * (
                GELU_A + 3.0 * GELU_A * GELU_B * square
            )
            dot = jnp.sum(act * back, axis=1, keepdims=True)
            act_low = (mix * act).astype(jnp.bfloat16)
            down = (mix * back * slope).astype(jnp.bfloat16)
            mixed[rows, :] = act_low
            dpre[rows, :] = down
            dbias_ref[0] += jnp.sum(down.astype(jnp.float32), axis=0, keepdims=True)
            y_ref[0, rows, :] = jnp.dot(
                act_low, down_ref[0], preferred_element_type=jnp.float32
            ).astype(jnp.bfloat16)
            dx_ref[0, rows, :width] = lax.dot_general(
                down, up_ref[0], (((1,), (1,)), ((), ())), preferred_element_type=jnp.float32
            ).astype(jnp.bfloat16)
            high = dot.astype(jnp.bfloat16).astype(jnp.float32)
            dx_ref[0, rows, width:] = jnp.where(
                lane == expert, high, jnp.where(lane == expert + expert_count, dot - high, 0.0)
            ).astype(jnp.bfloat16)
            return carry

        lax.fori_loop(0, tiles_ref[expert], tile, 0)

        def weights(depth):
            rows = pl.ds(0, depth)
            for i in range(width // TILE):
                part = pl.ds(i * TILE, TILE)
                dup_ref[0, part, :] = lax.dot_general(
                    x_ref[0, rows, part], dpre[rows, :], (((0,), (0,)), ((), ())),
                    preferred_element_type=jnp.float32,
                ).astype(jnp.bfloat16)
                ddown_ref[0, part, :] = lax.dot_general(
                    g_ref[0, rows, part], mixed[rows, :], (((0,), (0,)), ((), ())),
                    preferred_element_type=jnp.float32,
                ).astype(jnp.bfloat16)

        pl.when(tiles_ref[expert] <= 3)(lambda: weights(3 * TILE))
        pl.when(tiles_ref[expert] > 3)(lambda: weights(room))

    def whole(*dims):
        return pl.BlockSpec((1, *dims), lambda e, tiles: (e + first, 0, 0))

    def own(*dims):
        return pl.BlockSpec((1, *dims), lambda e, tiles: (e, 0, 0))

    shapes = [
        ((room, width), jnp.bfloat16),
        ((room, cols), jnp.bfloat16),
        ((width, hidden), jnp.bfloat16),
        ((width, hidden), jnp.bfloat16),
        ((1, hidden), jnp.float32),
    ]
    return pl.pallas_call(
        kernel,
        grid_spec=pltpu.PrefetchScalarGridSpec(
            num_scalar_prefetch=1,
            grid=(count,),
            in_specs=[
                whole(room, cols),
                whole(room, width),
                whole(width, hidden),
                whole(1, hidden),
                whole(hidden, width),
            ]
            + [pl.BlockSpec(memory_space=pl.ANY)] * len(after),
            out_specs=[own(*dims) for dims, _ in shapes],
            scratch_shapes=[pltpu.VMEM((room, hidden), jnp.bfloat16)] * 2,
        ),
        out_shape=[jax.ShapeDtypeStruct((count, *dims), kind) for dims, kind in shapes],
        compiler_params=pltpu.CompilerParams(vmem_limit_bytes=VMEM),
        cost_estimate=pl.CostEstimate(
            flops=count * 12 * 768 * width * hidden,
            bytes_accessed=count * (4 * room * (cols + width) + 8 * width * hidden),
            transcendentals=count * 768 * hidden,
        ),
        name="experts",
    )(tiles, inputs, grads, up_weight, up_bias[:, None, :], down_weight, *after)


def call(kernel, name, grid, ins, outs, after=(), scratch=(), us=5, each=1, turn=None):
    turn = jnp.zeros((1,), jnp.int32) if turn is None else turn

    def spec(shape, split):
        zeros = (0,) * (len(shape) - 1)
        if split == "turned":
            return pl.BlockSpec((each, *shape[1:]), lambda i, t: ((i + t[0]) % grid, *zeros))
        if split:
            return pl.BlockSpec((each, *shape[1:]), lambda i, t: (i, *zeros))
        return pl.BlockSpec(tuple(shape), lambda i, t: (0, *zeros))

    count, late = len(ins), len(after)

    def body(turn_ref, *refs):
        kernel(*refs[:count], *refs[count + late :])

    return pl.pallas_call(
        body,
        grid_spec=pltpu.PrefetchScalarGridSpec(
            num_scalar_prefetch=1,
            grid=(grid,),
            in_specs=[spec(a.shape, split) for a, split in ins]
            + [pl.BlockSpec(memory_space=pl.ANY)] * late,
            out_specs=[spec(a.shape, split) for a, split in outs],
            scratch_shapes=list(scratch),
        ),
        out_shape=[a for a, _ in outs],
        compiler_params=pltpu.CompilerParams(vmem_limit_bytes=VMEM),
        cost_estimate=cost(us),
        name=name,
    )(turn, *[a for a, _ in ins], *after)


def shape_of(dims, kind):
    return jax.ShapeDtypeStruct(tuple(dims), kind)


def normal(x):
    centered = x - jnp.mean(x, axis=-1, keepdims=True)
    spread_of = lax.rsqrt(jnp.mean(centered * centered, axis=-1, keepdims=True) + EPSILON)
    return centered * spread_of, spread_of


def contract(left, right, left_dim, right_dim):
    return lax.dot_general(
        left, right, (((left_dim,), (right_dim,)), ((), ())), preferred_element_type=jnp.float32
    )


def head_masks(width):
    lane = lax.broadcasted_iota(jnp.int32, (1, width), 1)
    return [(lane >= h * HD) & (lane < (h + 1) * HD) for h in range(width // HD)]


def head_probs(q, k, mask):
    own = jnp.where(mask, q, jnp.zeros_like(q)) * jnp.bfloat16(HD ** (-0.5))
    scores = contract(own, k, 1, 1)
    column = lax.broadcasted_iota(jnp.int32, scores.shape, 1)
    scores = jnp.where(column < SEQ, scores, -1e30)
    raised = jnp.exp(scores - jnp.max(scores, axis=-1, keepdims=True))
    return raised * (1.0 / jnp.sum(raised, axis=-1, keepdims=True))


def attention_forward(x, turn, gain, shift, weight, bias, out_weight, half, kept):
    images, seq, width = x.shape
    rows, inner = ROWS, weight.shape[2]

    def kernel(
        turn_ref, x_ref, gain_ref, shift_ref, w_ref, b_ref, wo_ref,
        *refs
    ):
        part_ref, pad_ref, n_ref, q_ref, k_ref, v_ref, o_ref, held = refs[len(kept) :]
        held[...] = jnp.zeros_like(held)
        for i in range(TRIO):
            held[i, :seq, :] = x_ref[i].astype(jnp.float32)
        value = held[...].reshape(TRIO * rows, width)
        pad_ref[...] = value.astype(jnp.bfloat16).reshape(TRIO, rows, width)
        n = (normal(value)[0] * gain_ref[...] + shift_ref[...]).astype(jnp.bfloat16)
        n_ref[...] = n.reshape(TRIO, rows, width)
        for j, ref in enumerate((q_ref, k_ref, v_ref)):
            made = jnp.dot(n, w_ref[j], preferred_element_type=jnp.float32) + b_ref[j : j + 1, :]
            ref[...] = made.astype(jnp.bfloat16).reshape(TRIO, rows, inner)
        for i in range(TRIO):
            q, k, v = q_ref[i], k_ref[i], v_ref[i]
            mixed = jnp.zeros((rows, inner), jnp.float32)
            for mask in head_masks(inner):
                probs = head_probs(q, k, mask).astype(jnp.bfloat16)
                head = jnp.dot(probs, v, preferred_element_type=jnp.float32)
                mixed = jnp.where(mask, head, mixed)
            o_ref[i] = mixed.astype(jnp.bfloat16)
        mixed = o_ref[...].reshape(TRIO * rows, inner)
        part = jnp.dot(mixed, wo_ref[...], preferred_element_type=jnp.float32)
        part_ref[...] = part.astype(jnp.bfloat16).reshape(TRIO, rows, width)

    wide = shape_of((images, rows, width), jnp.bfloat16)
    slim = shape_of((images, rows, inner), jnp.bfloat16)
    blocks = images // TRIO

    def place(i, turn):
        return (2 * i + half, 0, 0)

    def whole(array):
        return pl.BlockSpec(array.shape, lambda i, turn: (0,) * array.ndim)

    small = (gain, shift, weight, bias, out_weight)
    return pl.pallas_call(
        kernel,
        grid_spec=pltpu.PrefetchScalarGridSpec(
            num_scalar_prefetch=1,
            grid=(blocks // 2,),
            in_specs=[
                pl.BlockSpec(
                    (TRIO, seq, width), lambda i, turn: ((2 * i + half + turn[0]) % blocks, 0, 0)
                )
            ]
            + [whole(array) for array in small]
            + [pl.BlockSpec(memory_space=pl.ANY)] * len(kept),
            out_specs=[pl.BlockSpec((TRIO, rows, width), lambda i, turn: (i, 0, 0))]
            + [pl.BlockSpec((TRIO, *a.shape[1:]), place) for a in [wide] * 2 + [slim] * 4],
            scratch_shapes=[pltpu.VMEM((TRIO, rows, width), jnp.float32)],
        ),
        out_shape=[shape_of((images // 2, rows, width), jnp.bfloat16)] + [wide] * 2 + [slim] * 4,
        input_output_aliases={7 + i: 1 + i for i in range(len(kept))},
        compiler_params=pltpu.CompilerParams(vmem_limit_bytes=VMEM),
        cost_estimate=cost(9),
        name="attention_forward",
    )(turn, x, *small, *kept)


def attention_backward(da, x, n, q, k, v, o, weight, out_weight, after):
    images, rows, width = x.shape
    inner = weight.shape[2]

    def kernel(
        da_ref, x_ref, n_ref, q_ref, k_ref, v_ref, o_ref, w_ref, wo_ref,
        back_ref, dw_ref, dwo_ref, dbias_ref, sums_ref, held,
    ):
        @pl.when(pl.program_id(0) == 0)
        def _():
            dw_ref[...] = jnp.zeros_like(dw_ref)
            dwo_ref[...] = jnp.zeros_like(dwo_ref)
            dbias_ref[...] = jnp.zeros_like(dbias_ref)
            sums_ref[...] = jnp.zeros_like(sums_ref)

        joined = PAIR * rows
        da = da_ref[...].reshape(joined, width)
        do_all = contract(da, wo_ref[...], 1, 1).astype(jnp.bfloat16).reshape(PAIR, rows, inner)
        scale = HD ** (-0.5)
        for i in range(PAIR):
            q, k, v, do = q_ref[i], k_ref[i], v_ref[i], do_all[i]
            dq = dk = dv = jnp.zeros((rows, inner), jnp.float32)
            for mask in head_masks(inner):
                probs = head_probs(q, k, mask)
                dv = jnp.where(mask, contract(probs.astype(jnp.bfloat16), do, 0, 0), dv)
                dp = contract(jnp.where(mask, do, jnp.zeros_like(do)), v, 1, 1)
                ds = probs * (dp - jnp.sum(probs * dp, axis=-1, keepdims=True))
                ds = ds.astype(jnp.bfloat16)
                dq = jnp.where(mask, jnp.dot(ds, k, preferred_element_type=jnp.float32), dq)
                dk = jnp.where(mask, contract(ds, q, 0, 0), dk)
            held[0, i] = (dq * scale).astype(jnp.bfloat16)
            held[1, i] = (dk * scale).astype(jnp.bfloat16)
            held[2, i] = dv.astype(jnp.bfloat16)
        n = n_ref[...].reshape(joined, width)
        back = jnp.zeros((joined, width), jnp.float32)
        for j in range(3):
            grad = held[j].reshape(joined, inner)
            dw_ref[j] += contract(n, grad, 0, 0)
            back += contract(grad, w_ref[j], 1, 1)
            if j != 1:
                dbias_ref[j // 2 : j // 2 + 1, :] += jnp.sum(
                    grad.astype(jnp.float32), axis=0, keepdims=True
                )
        dwo_ref[0] += contract(da, o_ref[...].reshape(joined, inner), 0, 0)
        back_ref[...] = back.astype(jnp.bfloat16).reshape(PAIR, rows, width)
        unit, _ = normal(x_ref[...].reshape(joined, width).astype(jnp.float32))
        sums_ref[0:1, :] += jnp.sum(back * unit, axis=0, keepdims=True)
        sums_ref[1:2, :] += jnp.sum(back, axis=0, keepdims=True)
        sums_ref[2:3, :] += jnp.sum(da.astype(jnp.float32), axis=0, keepdims=True)

    return call(
        kernel, "attention_backward", images // PAIR,
        [(a, True) for a in (da, x, n, q, k, v, o)] + [(weight, False), (out_weight, False)],
        [
            (shape_of((images, rows, width), jnp.bfloat16), True),
            (shape_of((3, width, inner), jnp.float32), False),
            (shape_of((1, width, inner), jnp.float32), False),
            (shape_of((2, inner), jnp.float32), False),
            (shape_of((3, width), jnp.float32), False),
        ],
        after=after, each=PAIR, us=30,
        scratch=[pltpu.VMEM((3, PAIR, rows, inner), jnp.bfloat16)],
    )


def middle_norm(near, far, x, out_bias, gain, shift, after):
    each = near[0].shape[0]
    count, (_, rows, width) = 2 * each, x.shape

    def kernel(near_a, near_b, far_a, far_b, x_ref, bias_ref, gain_ref, shift_ref, *refs):
        middle_ref, n_ref = refs[len(after) :]
        early = pl.program_id(0) < each
        total = jnp.where(early, near_a[0], near_b[0]).astype(jnp.float32)
        total = total + jnp.where(early, far_a[0], far_b[0]).astype(jnp.float32)
        middle = x_ref[0].astype(jnp.float32) + total + bias_ref[...]
        middle_ref[0] = middle
        n_ref[0] = (normal(middle)[0] * gain_ref[...] + shift_ref[...]).astype(jnp.bfloat16)

    block = (1, rows, width)
    low = pl.BlockSpec(block, lambda i: (jnp.minimum(i, each - 1), 0, 0))
    high = pl.BlockSpec(block, lambda i: (jnp.maximum(i - each, 0), 0, 0))
    one = pl.BlockSpec(block, lambda i: (i, 0, 0))
    flat = pl.BlockSpec((1, width), lambda i: (0, 0))
    return pl.pallas_call(
        kernel,
        grid=(count,),
        in_specs=[low, high, low, high, one, flat, flat, flat]
        + [pl.BlockSpec(memory_space=pl.ANY)] * len(after),
        out_specs=[one, one],
        out_shape=[shape_of((count, rows, width), kind) for kind in (jnp.float32, jnp.bfloat16)],
        compiler_params=pltpu.CompilerParams(vmem_limit_bytes=VMEM),
        cost_estimate=cost(7),
        name="middle_norm",
    )(*near, *far, x, out_bias, gain, shift, *after)


def norm_back(dn, unit, spread_of, gain):
    dz = dn * gain
    mean = jnp.mean(dz, axis=-1, keepdims=True)
    return spread_of * (dz - mean - unit * jnp.mean(dz * unit, axis=-1, keepdims=True))


def middle_back(near, far, dots, gates, chosen, pair, n, router_weight, down_bias, middle, upstream, gain, after):
    count, wide = down_bias.shape[0], pair.shape[2]

    def kernel(
        near_ref, far_ref, dots_ref, gates_ref, chosen_ref, pair_ref, n_ref, router_ref, bias_ref,
        middle_ref, g_ref, gain_ref, grad_ref, da_ref, sums_ref, drouter_ref, dbias_ref,
    ):
        @pl.when(pl.program_id(0) == 0)
        def _():
            sums_ref[...] = jnp.zeros_like(sums_ref)
            drouter_ref[...] = jnp.zeros_like(drouter_ref)
            dbias_ref[...] = jnp.zeros_like(dbias_ref)

        g = g_ref[0]
        lane = lax.broadcasted_iota(jnp.int32, (g.shape[0], count), 1)
        named = (lane == chosen_ref[0, :, 0:1]) | (lane == chosen_ref[0, :, 1:2])
        dmix = dots_ref[0] + jnp.where(named, contract(g, bias_ref[...], 1, 1), 0.0)
        gate = gates_ref[0, :, :count]
        dlogits = gate * (dmix - jnp.sum(gate * dmix, axis=-1, keepdims=True))
        dlogits = dlogits.astype(jnp.bfloat16)
        drouter_ref[...] += contract(dlogits, n_ref[0], 0, 0)
        dbias_ref[...] += contract(pair_ref[0], g, 0, 0)
        dn = near_ref[0].astype(jnp.float32) + far_ref[0].astype(jnp.float32)
        dn = dn + contract(dlogits, router_ref[...], 1, 1)
        unit, spread_of = normal(middle_ref[0])
        grad = g.astype(jnp.float32) + norm_back(dn, unit, spread_of, gain_ref[...])
        grad_ref[0] = grad
        da_ref[0] = grad.astype(jnp.bfloat16)
        sums_ref[0:1, :] += jnp.sum(dn * unit, axis=0, keepdims=True)
        sums_ref[1:2, :] += jnp.sum(dn, axis=0, keepdims=True)

    width = middle.shape[2]
    return call(
        kernel, "middle_back", middle.shape[0],
        [(a, True) for a in (near, far, dots, gates, chosen, pair, n)]
        + [(router_weight, False), (down_bias, False), (middle, True), (upstream, True), (gain, False)],
        [
            (shape_of(middle.shape, jnp.float32), True),
            (shape_of(middle.shape, jnp.bfloat16), True),
            (shape_of((2, width), jnp.float32), False),
            (shape_of((count, width), jnp.float32), False),
            (shape_of((wide, width), jnp.float32), False),
        ],
        after=after, us=8,
    )


def finish(near, far, middle, pair, down_bias, after):
    def kernel(near_ref, far_ref, middle_ref, pair_ref, bias_ref, out_ref):
        total = near_ref[0].astype(jnp.float32) + far_ref[0].astype(jnp.float32)
        total = total + jnp.dot(pair_ref[0], bias_ref[...], preferred_element_type=jnp.float32)
        out_ref[0] = (middle_ref[0] + total).astype(jnp.bfloat16)

    return call(
        kernel, "finish", middle.shape[0],
        [(near, True), (far, True), (middle, True), (pair, True), (down_bias, False)],
        [(shape_of(middle.shape, jnp.bfloat16), True)],
        after=after, us=8,
    )[0]


def input_back(own, other, x, own_grad, other_grad, gain, turn, after):
    images, _, width = x.shape
    half = images // 2

    def kernel(turn_ref, own_ref, other_ref, x_ref, own_grad_ref, other_grad_ref, gain_ref, *refs):
        out_ref = refs[-1]
        step = pl.program_id(0)
        place = (step + turn_ref[0]) % images
        mine = step < half
        dn = jnp.where(mine, own_ref[0], other_ref[0]).astype(jnp.float32)
        unit, spread_of = normal(x_ref[0].astype(jnp.float32))
        grad = jnp.where(mine, own_grad_ref[0], other_grad_ref[0])
        grad = grad + norm_back(dn, unit, spread_of, gain_ref[...])
        for j in range(images):

            @pl.when(place == j)
            def _():
                out_ref[j * SEQ : (j + 1) * SEQ, :] = grad[:SEQ]

    def low(shape):
        return pl.BlockSpec((1, *shape[1:]), lambda i, t: (jnp.minimum(i, half - 1), 0, 0))

    def high(shape):
        return pl.BlockSpec((1, *shape[1:]), lambda i, t: (jnp.maximum(i - half, 0), 0, 0))

    return pl.pallas_call(
        kernel,
        grid_spec=pltpu.PrefetchScalarGridSpec(
            num_scalar_prefetch=1,
            grid=(images,),
            in_specs=[
                low(own.shape),
                high(other.shape),
                pl.BlockSpec((1, *x.shape[1:]), lambda i, t: (i, 0, 0)),
                low(own_grad.shape),
                high(other_grad.shape),
                pl.BlockSpec(gain.shape, lambda i, t: (0, 0)),
            ]
            + [pl.BlockSpec(memory_space=pl.ANY)] * len(after),
            out_specs=pl.BlockSpec((images * SEQ, width), lambda i, t: (0, 0)),
        ),
        out_shape=jax.ShapeDtypeStruct((images * SEQ, width), jnp.float32),
        compiler_params=pltpu.CompilerParams(vmem_limit_bytes=VMEM),
        cost_estimate=cost(15),
        name="input_back",
    )(turn, own, other, x, own_grad, other_grad, gain, *after)


def to_core(value):
    return lax.ppermute(value, "tensor", pairs(lax.axis_size("tensor"), 1))


def across(value):
    return lax.ppermute(value, "tensor", pairs(lax.axis_size("tensor"), 2))


def core_sum(part, zero):
    half = part.shape[0] // 2
    got = to_core(part[half:])
    return (part[:half].astype(jnp.float32) + got.astype(jnp.float32) + zero).astype(jnp.bfloat16)


def zero_of(value):
    return value[(0,) * value.ndim].astype(jnp.float32) * 0.0


def ring_owner(way, step):
    index = lax.axis_index("dp")
    place = jnp.where(index % 2 == 0, index // 2, 7 - index // 2)
    place = (place - way * (step + 1)) % 8
    return jnp.where(place < 4, 2 * place, 15 - 2 * place).astype(jnp.int32)


def ring_hop(value, way):
    path = [(RING[i], RING[(i + way) % len(RING)]) for i in range(len(RING))]
    return lax.ppermute(value, "dp", path)


def ring_add(got, sources, way, steps, kinds, after):
    groups, came = len(sources), got.shape[0]
    many, total, cols = sources[0].shape
    rows, part = total // 8, 2
    owners = jnp.stack([ring_owner(way, step) for step in steps])
    joint = all(kind == kinds[0] for kind in kinds)

    def kernel(owners_ref, held, *refs):
        outs = refs[groups + len(after) :]
        for g in range(groups):
            value = refs[g][...]
            if g < came:
                value = value.astype(jnp.float32) + held[g].astype(jnp.float32)
            if joint:
                outs[0][g] = value.astype(kinds[g])
            else:
                outs[g][0] = value.astype(kinds[g])

    def source(slot):
        return pl.BlockSpec((part, rows, cols), lambda i, own: (i, own[slot], 0))

    def stack(count):
        return pl.BlockSpec((count, part, rows, cols), lambda i, own: (0, i, 0, 0))

    if joint:
        outs = [((groups, many, rows, cols), kinds[0])]
    else:
        outs = [((1, many, rows, cols), kind) for kind in kinds]
    return pl.pallas_call(
        kernel,
        grid_spec=pltpu.PrefetchScalarGridSpec(
            num_scalar_prefetch=1,
            grid=(many // part,),
            in_specs=[stack(came)]
            + [source(i) for i in range(groups)]
            + [pl.BlockSpec(memory_space=pl.ANY)] * len(after),
            out_specs=[stack(dims[0]) for dims, _ in outs],
        ),
        out_shape=[jax.ShapeDtypeStruct(dims, kind) for dims, kind in outs],
        compiler_params=pltpu.CompilerParams(vmem_limit_bytes=VMEM),
        cost_estimate=cost(3),
        name="ring_add",
    )(owners, got, *sources, *after)


def halving_scatter(values):
    if lax.axis_size("dp") != 8:
        return lax.psum_scatter(values.astype(jnp.bfloat16), "dp", scatter_dimension=1, tiled=True).astype(jnp.float32)
    index = lax.axis_index("dp")
    many, rows, cols = values.shape
    values = values.reshape(many, 2, 2, 2, rows // 8, cols)
    for bit, axis in ((0, 3), (1, 2), (2, 1)):
        mine = (index >> bit) % 2
        keep = lax.dynamic_index_in_dim(values, mine, axis, keepdims=True)
        give = lax.dynamic_index_in_dim(values, 1 - mine, axis, keepdims=True)
        got = lax.ppermute(give.astype(jnp.bfloat16), "dp", pairs(8, 1 << bit))
        values = keep.astype(jnp.float32) + got.astype(jnp.float32)
    return values.reshape(many, rows // 8, cols)


def on_device(
    embedded,
    attn_gain,
    attn_shift,
    qkv_weight,
    qv_bias,
    out_weight,
    out_bias,
    moe_gain,
    moe_shift,
    router_weight,
    up_weight,
    up_bias,
    down_weight,
    down_bias,
    routes,
    cotangent,
):
    tok_rows, width = embedded.shape
    images = tok_rows // SEQ
    half = images // 2
    head_width = qkv_weight.shape[2]
    expert_count = up_weight.shape[0]
    core = lax.axis_index("tensor") % 2
    f32 = jnp.float32

    def own_first(value, fill):
        value = value.reshape(images, SEQ, value.shape[1])
        value = jnp.pad(value, ((0, 0), (0, ROWS - SEQ), (0, 0)), constant_values=fill)
        return jnp.where(core == 0, value, jnp.roll(value, half, axis=0))

    def in_order(own, other):
        low = jnp.where(core == 0, own, other)
        high = jnp.where(core == 0, other, own)
        return jnp.concatenate([low, high])[:, :SEQ].reshape(tok_rows, width)

    def row(value):
        return value.astype(f32)[None]

    def imaged(value):
        return value.reshape(images, ROWS, value.shape[1])

    turn = (half * core).astype(jnp.int32)[None]
    bias_rows = jnp.stack([qv_bias[0], jnp.zeros_like(qv_bias[0]), qv_bias[1]]).astype(f32)
    images_in = embedded.reshape(images, SEQ, width)
    kept, near, far = (), [], []
    for i in range(2):
        part, *kept = attention_forward(
            images_in, turn // TRIO, row(attn_gain), row(attn_shift),
            qkv_weight, bias_rows, out_weight, i, tuple(kept),
        )
        near.append(core_sum(part, 0.0))
        far.append(across(near[i]))
    x, normed, queries, keys, values, mixed = kept

    chosen = own_first(routes, -1).reshape(images * ROWS, 2)
    rows, columns, plan, tiles = route_plan(chosen, expert_count)
    upstream = own_first(cotangent, 0)
    grad_buffers = spread(upstream.reshape(images * ROWS, width), rows, plan, expert_count)

    middle, own_normed = middle_norm(
        near, far, x, row(out_bias), row(moe_gain), row(moe_shift), (grad_buffers,)
    )
    moe_normed = jnp.concatenate([own_normed, to_core(own_normed)]).reshape(images * ROWS, width)
    extra = 128
    router_twice = jnp.pad(
        jnp.concatenate([router_weight, router_weight], axis=1),
        ((0, 0), (0, extra - 2 * expert_count)),
    )
    bias_twice = jnp.pad(
        jnp.concatenate([down_bias, down_bias]), ((0, extra - 2 * expert_count), (0, 0))
    )
    buffers, gates, mix_pair = gated_spread(
        moe_normed, rows, plan, chosen, router_twice, expert_count, extra
    )
    gates, mix_pair, chosen = imaged(gates), imaged(mix_pair), imaged(chosen)
    group = expert_count // GROUPS

    def experts_of(i, after):
        return expert_pass(
            buffers, grad_buffers, up_weight, up_bias, down_weight, tiles, i * group, group, after
        )

    ringed = lax.axis_size("dp") == len(RING)
    low = jnp.bfloat16
    y_first, back_first, *first, bias_first = experts_of(0, ())
    moving = ()
    if ringed:
        rows_each = width // 8
        moving = [
            lax.dynamic_slice_in_dim(grad, ring_owner(way, 0) * rows_each, rows_each, 1)[None]
            for grad, way in zip(first, (1, -1))
        ]
    y_second, back_second, *second, bias_second = experts_of(1, tuple(moving))

    def round_trip(step, kinds, *after):
        if not ringed:
            return ()
        made = []
        for d, way in enumerate((1, -1)):
            got = ring_hop(moving[d], way)
            if step < 8:
                made.append(ring_add(got, [first[d], second[d]], way, [step, step - 1], kinds, after))
            else:
                made.append(ring_add(got, [second[d]], way, [step - 1], kinds, after))
        return [piece for pieces in zip(*made) for piece in pieces]

    moving = round_trip(1, [low, low])
    back_part, dots = collect((back_first, back_second), columns, plan, width, tuple(moving))
    back_near = core_sum(imaged(back_part), 0.0)
    back_far = across(back_near)
    dots = dots[:, : 2 * expert_count].T
    dots = dots[:expert_count] + dots[expert_count:]
    own_rows = half * ROWS
    dots = dots[:, :own_rows] + to_core(dots[:, own_rows:])
    dots = (dots + across(dots)).T.reshape(half, ROWS, expert_count)
    moving = round_trip(2, [low, low], back_near)
    (moe_part,) = collect((y_first, y_second), columns, plan, width, (back_near, *moving))
    moving = round_trip(3, [low, low], moe_part)
    middle_grad, own_da, moe_sums, router_sums, bias_sums = middle_back(
        back_near, back_far, dots, gates, chosen, mix_pair, imaged(moe_normed), router_weight,
        down_bias, middle, upstream, row(moe_gain), tuple(moving),
    )
    da = jnp.concatenate([own_da, to_core(own_da)])
    y_near = core_sum(imaged(moe_part), zero_of(back_far))
    y_far = across(y_near)
    other_grad = to_core(middle_grad)
    moving = round_trip(4, [low, low], own_da)
    normed_back, grad_qkv, grad_out, grad_qv_bias, sums = attention_backward(
        da, x, normed, queries, keys, values, mixed, qkv_weight, out_weight, (y_far, *moving)
    )
    last_near = core_sum(normed_back, 0.0)
    last_far = across(last_near)
    moving = round_trip(5, [low, low], last_near)
    near_zero, far_zero = zero_of(last_near), zero_of(last_far)
    own_out = finish(y_near, y_far, middle, mix_pair, bias_twice, (last_near,))
    layer_out = in_order(own_out, to_core(own_out))
    router_bias = [router_sums, bias_sums[:expert_count] + bias_sums[expert_count : 2 * expert_count]]
    tensor_parts = jnp.concatenate([sums[:2]] + [0.5 * part for part in (moe_sums, *router_bias)])
    packed = jnp.concatenate(
        [
            small_sum(tensor_parts + far_zero, "tensor"),
            sums[2:],
            jnp.pad(grad_qv_bias, ((0, 0), (0, width - head_width))),
            bias_first[:, 0],
            bias_second[:, 0],
        ]
    )
    packed = small_sum(packed, "dp")
    slim = halving_scatter(jnp.concatenate([grad_qkv, grad_out]) + near_zero)
    if ringed:
        moving = round_trip(6, [low, low], own_out)
        up_first, down_first, *moving = round_trip(7, [f32, low])
        up_second, down_second = round_trip(8, [f32])
    else:
        up_first, down_first, up_second, down_second = [
            lax.psum_scatter(grad, "dp", scatter_dimension=1, tiled=True).astype(f32)[None]
            for grad in (*first, *second)
        ]
    grad_up = jnp.concatenate([up_first[0], up_second[0]])
    grad_down = jnp.concatenate([down_first[0], down_second[0]]).transpose(0, 2, 1)
    last = (last_near.astype(f32) + last_far.astype(f32)).astype(jnp.bfloat16)
    grad_embedded = input_back(
        last, to_core(last), x, middle_grad, other_grad, row(attn_gain), turn,
        (layer_out, packed, slim),
    )
    base = 4 + 2 * expert_count
    return (
        layer_out,
        grad_embedded,
        packed[0],
        packed[1],
        slim[:3],
        packed[base + 1 : base + 3, :head_width],
        slim[3].T,
        packed[base],
        packed[2],
        packed[3],
        packed[4 : 4 + expert_count].T,
        grad_up,
        packed[base + 3 :],
        grad_down,
        packed[4 + expert_count : base],
    )


def solution(mesh):
    return jax.shard_map(
        on_device,
        mesh=mesh,
        in_specs=(
            P("dp", None),
            P(),
            P(),
            P(None, None, "tensor"),
            P(None, "tensor"),
            P("tensor", None),
            P(),
            P(),
            P(),
            P(),
            P(None, None, "tensor"),
            P(None, "tensor"),
            P(None, "tensor", None),
            P(),
            P("dp", None),
            P("dp", None),
        ),
        out_specs=(
            P("dp", None),
            P("dp", None),
            P(),
            P(),
            P(None, "dp", "tensor"),
            P(None, "tensor"),
            P("tensor", "dp"),
            P(),
            P(),
            P(),
            P(),
            P(None, "dp", "tensor"),
            P(None, "tensor"),
            P(None, "tensor", "dp"),
            P(),
        ),
        check_vma=False,
    )
```

```python
import jax
import jax.numpy as jnp
from jax import lax
from jax.experimental import pallas as pl
from jax.experimental.pallas import tpu as pltpu
from jax.sharding import PartitionSpec as P

SEQ = 197
HD = 64
EPSILON = 1e-06
RING = (0, 2, 4, 6, 7, 5, 3, 1)


def pairs(count, bit):
    return [(i, i ^ bit) for i in range(count)]


ROWS = 208
PAIR = 2
TRIO = 3
BLOCK = 416
GROUPS = 2
LOCAL = 960
ROOM = 1024
TILE = 256
VMEM = 56 * 1024 * 1024


def cost(us):
    return pl.CostEstimate(flops=int(us * 2e8), bytes_accessed=0, transcendentals=0)


def route_plan(routes, expert_count):
    tokens = routes.shape[0]
    blocks = -(-tokens // BLOCK)
    padded = jnp.pad(routes.T, ((0, 0), (0, blocks * BLOCK - tokens)), constant_values=-1)
    experts = jnp.arange(expert_count, dtype=jnp.int32)[:, None]
    first = padded[0][None, :] == experts
    second = padded[1][None, :] == experts
    named = (first | second).reshape(expert_count * blocks, BLOCK)
    ahead = jnp.arange(BLOCK)[:, None] < jnp.arange(BLOCK)[None, :]
    rank = jnp.dot(
        named.astype(jnp.bfloat16), ahead.astype(jnp.bfloat16), preferred_element_type=jnp.float32
    )
    rank = rank.astype(jnp.int32).reshape(expert_count, blocks, BLOCK)
    chunks = (jnp.sum(named.astype(jnp.int32), axis=1).reshape(expert_count, blocks) + 15) // 16
    inside = jnp.cumsum(chunks, axis=0) - chunks
    offset = jnp.cumsum(chunks, axis=1) - chunks
    place = (rank + 16 * inside[:, :, None]).reshape(expert_count, blocks * BLOCK)
    target = jnp.stack(
        [jnp.sum(jnp.where(hot, place + 1, 0), axis=0) - 1 for hot in (first, second)]
    )
    tiles = (jnp.sum(chunks, axis=1) * 16 + TILE - 1) // TILE
    plan = jnp.concatenate([chunks.T.reshape(-1), inside.T.reshape(-1), offset.T.reshape(-1)])
    rows = target.reshape(2, blocks, BLOCK).transpose(1, 0, 2)
    return rows, target.T, plan, tiles


def spread(source, rows, plan, expert_count):
    blocks, cols = rows.shape[0], source.shape[1]

    def kernel(plan_ref, rows_ref, source_ref, out_ref, local):
        block = pl.program_id(0)

        @pl.when(block == 0)
        def _():
            out_ref[...] = jnp.zeros_like(out_ref)

        part = LOCAL // 3
        for i in range(3):
            slot = lax.broadcasted_iota(jnp.int32, (part, BLOCK), 0) + i * part
            hot = (slot == rows_ref[0, 0:1, :]) | (slot == rows_ref[0, 1:2, :])
            local[pl.ds(i * part, part), :] = jnp.dot(
                jnp.where(hot, 1.0, 0.0).astype(jnp.bfloat16),
                source_ref[...],
                preferred_element_type=jnp.float32,
            ).astype(jnp.bfloat16)
        for e in range(expert_count):
            at = block * expert_count + e
            size = blocks * expert_count
            begin, goal = plan_ref[size + at], plan_ref[2 * size + at]

            def move(j, carry):
                here = pl.ds(pl.multiple_of((begin + j) * 16, 16), 16)
                there = pl.ds(pl.multiple_of((goal + j) * 16, 16), 16)
                out_ref[e, there, :] = local[here, :]
                return carry

            lax.fori_loop(0, plan_ref[at], move, 0)

    return pl.pallas_call(
        kernel,
        grid_spec=pltpu.PrefetchScalarGridSpec(
            num_scalar_prefetch=1,
            grid=(blocks,),
            in_specs=[
                pl.BlockSpec((1, 2, BLOCK), lambda b, plan: (b, 0, 0)),
                pl.BlockSpec((BLOCK, cols), lambda b, plan: (b, 0)),
            ],
            out_specs=pl.BlockSpec((expert_count, ROOM, cols), lambda b, plan: (0, 0, 0)),
            scratch_shapes=[pltpu.VMEM((LOCAL, cols), jnp.bfloat16)],
        ),
        out_shape=jax.ShapeDtypeStruct((expert_count, ROOM, cols), jnp.bfloat16),
        compiler_params=pltpu.CompilerParams(vmem_limit_bytes=VMEM),
        cost_estimate=cost(15),
        name="spread",
    )(plan, rows, source)


def gated_spread(own, other, rows, plan, chosen, router, expert_count, extra):
    blocks, cols = rows.shape[0], own.shape[1]
    both = cols + extra

    def kernel(
        plan_ref, rows_ref, own_ref, other_ref, chosen_ref, router_ref,
        out_ref, gate_ref, pair_ref, local,
    ):
        block = pl.program_id(0)
        source = jnp.where(block < blocks // 2, own_ref[...], other_ref[...])

        @pl.when(block == 0)
        def _():
            out_ref[...] = jnp.zeros_like(out_ref)

        logits = jnp.dot(source, router_ref[...], preferred_element_type=jnp.float32)
        lane = lax.broadcasted_iota(jnp.int32, logits.shape, 1)
        first, second = lane < expert_count, lane < 2 * expert_count
        expert = jnp.where(first, lane, lane - expert_count)
        top = jnp.max(jnp.where(first, logits, -jnp.inf), axis=-1, keepdims=True)
        raised = jnp.where(second, jnp.exp(logits - top), 0.0)
        gate = raised / jnp.sum(jnp.where(first, raised, 0.0), axis=-1, keepdims=True)
        named = (expert == chosen_ref[:, 0:1]) | (expert == chosen_ref[:, 1:2])
        mixing = jnp.where(named & second, gate, 0.0)
        high = mixing.astype(jnp.bfloat16).astype(jnp.float32)
        pair = jnp.where(first, high, mixing - high).astype(jnp.bfloat16)
        gate_ref[...] = gate
        pair_ref[...] = pair
        part = LOCAL // 3
        for i in range(3):
            slot = lax.broadcasted_iota(jnp.int32, (part, BLOCK), 0) + i * part
            hot = (slot == rows_ref[0, 0:1, :]) | (slot == rows_ref[0, 1:2, :])
            hot = jnp.where(hot, 1.0, 0.0).astype(jnp.bfloat16)
            for begin, end, value in ((0, cols, source), (cols, both, pair)):
                local[pl.ds(i * part, part), begin:end] = jnp.dot(
                    hot, value, preferred_element_type=jnp.float32
                ).astype(jnp.bfloat16)
        for e in range(expert_count):
            at = block * expert_count + e
            size = blocks * expert_count
            begin, goal = plan_ref[size + at], plan_ref[2 * size + at]

            def move(j, carry):
                here = pl.ds(pl.multiple_of((begin + j) * 16, 16), 16)
                there = pl.ds(pl.multiple_of((goal + j) * 16, 16), 16)
                out_ref[e, there, :] = local[here, :]
                return carry

            lax.fori_loop(0, plan_ref[at], move, 0)

    return pl.pallas_call(
        kernel,
        grid_spec=pltpu.PrefetchScalarGridSpec(
            num_scalar_prefetch=1,
            grid=(blocks,),
            in_specs=[
                pl.BlockSpec((1, 2, BLOCK), lambda b, plan: (b, 0, 0)),
                pl.BlockSpec((BLOCK, cols), lambda b, plan: (jnp.minimum(b, blocks // 2 - 1), 0)),
                pl.BlockSpec((BLOCK, cols), lambda b, plan: (jnp.maximum(b - blocks // 2, 0), 0)),
                pl.BlockSpec((BLOCK, 2), lambda b, plan: (b, 0)),
                pl.BlockSpec(router.shape, lambda b, plan: (0, 0)),
            ],
            out_specs=[
                pl.BlockSpec((expert_count, ROOM, both), lambda b, plan: (0, 0, 0)),
                pl.BlockSpec((BLOCK, extra), lambda b, plan: (b, 0)),
                pl.BlockSpec((BLOCK, extra), lambda b, plan: (b, 0)),
            ],
            scratch_shapes=[pltpu.VMEM((LOCAL, both), jnp.bfloat16)],
        ),
        out_shape=[
            jax.ShapeDtypeStruct((expert_count, ROOM, both), jnp.bfloat16),
            jax.ShapeDtypeStruct((blocks * BLOCK, extra), jnp.float32),
            jax.ShapeDtypeStruct((blocks * BLOCK, extra), jnp.bfloat16),
        ],
        compiler_params=pltpu.CompilerParams(vmem_limit_bytes=VMEM),
        cost_estimate=cost(20),
        name="gated_spread",
    )(plan, rows, own, other, chosen, router)


def collect(buffers, columns, plan, kept, after):
    each, room, cols = buffers[0].shape
    expert_count = each * len(buffers)
    blocks = columns.shape[0] // BLOCK
    extra = cols - kept

    def kernel(plan_ref, columns_ref, *refs):
        held, refs = refs[: len(buffers)], refs[len(buffers) + len(after) :]
        own_ref, other_ref, local = refs[0], refs[1], refs[-1]
        block = pl.program_id(0)
        mine = block < blocks // 2

        @pl.when(block == 0)
        def _():
            local[...] = jnp.zeros_like(local)

        for e in range(expert_count):
            at = block * expert_count + e
            size = blocks * expert_count
            begin, goal = plan_ref[size + at], plan_ref[2 * size + at]

            def move(j, carry):
                here = pl.ds(pl.multiple_of((begin + j) * 16, 16), 16)
                there = pl.ds(pl.multiple_of((goal + j) * 16, 16), 16)
                local[here, :] = held[e // each][e % each, there, :]
                return carry

            lax.fori_loop(0, plan_ref[at], move, 0)
        part = BLOCK // 2
        for i in range(2):
            rows = pl.ds(i * part, part)
            slot = lax.broadcasted_iota(jnp.int32, (part, LOCAL), 1)
            hot = (slot == columns_ref[rows, 0:1]) | (slot == columns_ref[rows, 1:2])
            total = jnp.dot(
                jnp.where(hot, 1.0, 0.0).astype(jnp.bfloat16),
                local[...],
                preferred_element_type=jnp.float32,
            )
            low = total[:, :kept].astype(jnp.bfloat16)

            @pl.when(mine)
            def _():
                own_ref[rows, :] = low

            @pl.when(jnp.logical_not(mine))
            def _():
                other_ref[rows, :] = low

            if extra:
                refs[2][rows, :] = total[:, kept:]

    out_specs = [
        pl.BlockSpec((BLOCK, kept), lambda b, plan: (jnp.minimum(b, blocks // 2 - 1), 0)),
        pl.BlockSpec((BLOCK, kept), lambda b, plan: (jnp.maximum(b - blocks // 2, 0), 0)),
    ]
    out_shape = [jax.ShapeDtypeStruct((blocks // 2 * BLOCK, kept), jnp.bfloat16)] * 2
    if extra:
        out_specs.append(pl.BlockSpec((BLOCK, extra), lambda b, plan: (b, 0)))
        out_shape.append(jax.ShapeDtypeStruct((blocks * BLOCK, extra), jnp.float32))
    return pl.pallas_call(
        kernel,
        grid_spec=pltpu.PrefetchScalarGridSpec(
            num_scalar_prefetch=1,
            grid=(blocks,),
            in_specs=[
                pl.BlockSpec((BLOCK, 2), lambda b, plan: (b, 0)),
            ]
            + [pl.BlockSpec((each, room, cols), lambda b, plan: (0, 0, 0))] * len(buffers)
            + [pl.BlockSpec(memory_space=pl.ANY)] * len(after),
            out_specs=out_specs,
            scratch_shapes=[pltpu.VMEM((LOCAL, cols), jnp.bfloat16)],
        ),
        out_shape=out_shape,
        compiler_params=pltpu.CompilerParams(vmem_limit_bytes=VMEM),
        cost_estimate=cost(16),
        name="collect",
    )(plan, columns, *buffers, *after)


GELU_A = 0.7978845608028654
GELU_B = 0.044715


def expert_pass(inputs, grads, up_weight, up_bias, down_weight, tiles, first, count, after):
    expert_count, room, cols = inputs.shape
    width, hidden = up_weight.shape[1:]

    def kernel(
        tiles_ref, x_ref, g_ref, up_ref, bias_ref, down_ref, *refs
    ):
        y_ref, dx_ref, dup_ref, ddown_ref, dbias_ref, mixed, dpre = refs[len(after) :]
        step = pl.program_id(0)
        expert = step + first

        @pl.when(step == 0)
        def _():
            mixed[...] = jnp.zeros_like(mixed)
            dpre[...] = jnp.zeros_like(dpre)

        dbias_ref[...] = jnp.zeros_like(dbias_ref)
        lane = lax.broadcasted_iota(jnp.int32, (TILE, cols - width), 1)

        def tile(r, carry):
            rows = pl.ds(pl.multiple_of(r * TILE, TILE), TILE)
            x = x_ref[0, rows, :width]
            g = g_ref[0, rows, :]
            gates = x_ref[0, rows, width:].astype(jnp.float32)
            own = (lane == expert) | (lane == expert + expert_count)
            mix = jnp.sum(jnp.where(own, gates, 0.0), axis=1, keepdims=True)
            pre = jnp.dot(x, up_ref[0], preferred_element_type=jnp.float32)
            pre = pre + bias_ref[0].astype(jnp.float32)
            back = lax.dot_general(
                g, down_ref[0], (((1,), (1,)), ((), ())), preferred_element_type=jnp.float32
            )
            square = pre * pre
            bend = jnp.tanh(pre * (GELU_A + GELU_A * GELU_B * square))
            upper = 0.5 + 0.5 * bend
            act = pre * upper
            slope = upper + 0.5 * pre * (1.0 - bend * bend) * (
                GELU_A + 3.0 * GELU_A * GELU_B * square
            )
            dot = jnp.sum(act * back, axis=1, keepdims=True)
            act_low = (mix * act).astype(jnp.bfloat16)
            down = (mix * back * slope).astype(jnp.bfloat16)
            mixed[rows, :] = act_low
            dpre[rows, :] = down
            dbias_ref[0] += jnp.sum(down.astype(jnp.float32), axis=0, keepdims=True)
            y_ref[0, rows, :] = jnp.dot(
                act_low, down_ref[0], preferred_element_type=jnp.float32
            ).astype(jnp.bfloat16)
            dx_ref[0, rows, :width] = lax.dot_general(
                down, up_ref[0], (((1,), (1,)), ((), ())), preferred_element_type=jnp.float32
            ).astype(jnp.bfloat16)
            high = dot.astype(jnp.bfloat16).astype(jnp.float32)
            dx_ref[0, rows, width:] = jnp.where(
                lane == expert, high, jnp.where(lane == expert + expert_count, dot - high, 0.0)
            ).astype(jnp.bfloat16)
            return carry

        lax.fori_loop(0, tiles_ref[expert], tile, 0)

        def weights(depth):
            rows = pl.ds(0, depth)
            for i in range(width // TILE):
                part = pl.ds(i * TILE, TILE)
                dup_ref[0, part, :] = lax.dot_general(
                    x_ref[0, rows, part], dpre[rows, :], (((0,), (0,)), ((), ())),
                    preferred_element_type=jnp.float32,
                ).astype(jnp.bfloat16)
                ddown_ref[0, part, :] = lax.dot_general(
                    g_ref[0, rows, part], mixed[rows, :], (((0,), (0,)), ((), ())),
                    preferred_element_type=jnp.float32,
                ).astype(jnp.bfloat16)

        pl.when(tiles_ref[expert] <= 3)(lambda: weights(3 * TILE))
        pl.when(tiles_ref[expert] > 3)(lambda: weights(room))

    def whole(*dims):
        return pl.BlockSpec((1, *dims), lambda e, tiles: (e + first, 0, 0))

    def own(*dims):
        return pl.BlockSpec((1, *dims), lambda e, tiles: (e, 0, 0))

    shapes = [
        ((room, width), jnp.bfloat16),
        ((room, cols), jnp.bfloat16),
        ((width, hidden), jnp.bfloat16),
        ((width, hidden), jnp.bfloat16),
        ((1, hidden), jnp.float32),
    ]
    return pl.pallas_call(
        kernel,
        grid_spec=pltpu.PrefetchScalarGridSpec(
            num_scalar_prefetch=1,
            grid=(count,),
            in_specs=[
                whole(room, cols),
                whole(room, width),
                whole(width, hidden),
                whole(1, hidden),
                whole(hidden, width),
            ]
            + [pl.BlockSpec(memory_space=pl.ANY)] * len(after),
            out_specs=[own(*dims) for dims, _ in shapes],
            scratch_shapes=[pltpu.VMEM((room, hidden), jnp.bfloat16)] * 2,
        ),
        out_shape=[jax.ShapeDtypeStruct((count, *dims), kind) for dims, kind in shapes],
        compiler_params=pltpu.CompilerParams(vmem_limit_bytes=VMEM),
        cost_estimate=pl.CostEstimate(
            flops=count * 12 * 768 * width * hidden,
            bytes_accessed=count * (4 * room * (cols + width) + 8 * width * hidden),
            transcendentals=count * 768 * hidden,
        ),
        name="experts",
    )(tiles, inputs, grads, up_weight, up_bias[:, None, :], down_weight, *after)


def call(kernel, name, grid, ins, outs, after=(), scratch=(), us=5, each=1, turn=None):
    turn = jnp.zeros((1,), jnp.int32) if turn is None else turn

    def spec(shape, split):
        zeros = (0,) * (len(shape) - 1)
        if split == "turned":
            return pl.BlockSpec((each, *shape[1:]), lambda i, t: ((i + t[0]) % grid, *zeros))
        if split == "low":
            return pl.BlockSpec(
                (each, *shape[1:]), lambda i, t: (jnp.minimum(i, grid // 2 - 1), *zeros)
            )
        if split == "high":
            return pl.BlockSpec(
                (each, *shape[1:]), lambda i, t: (jnp.maximum(i - grid // 2, 0), *zeros)
            )
        if split:
            return pl.BlockSpec((each, *shape[1:]), lambda i, t: (i, *zeros))
        return pl.BlockSpec(tuple(shape), lambda i, t: (0, *zeros))

    count, late = len(ins), len(after)

    def body(turn_ref, *refs):
        kernel(*refs[:count], *refs[count + late :])

    return pl.pallas_call(
        body,
        grid_spec=pltpu.PrefetchScalarGridSpec(
            num_scalar_prefetch=1,
            grid=(grid,),
            in_specs=[spec(a.shape, split) for a, split in ins]
            + [pl.BlockSpec(memory_space=pl.ANY)] * late,
            out_specs=[spec(a.shape, split) for a, split in outs],
            scratch_shapes=list(scratch),
        ),
        out_shape=[a for a, _ in outs],
        compiler_params=pltpu.CompilerParams(vmem_limit_bytes=VMEM),
        cost_estimate=cost(us),
        name=name,
    )(turn, *[a for a, _ in ins], *after)


def shape_of(dims, kind):
    return jax.ShapeDtypeStruct(tuple(dims), kind)


def normal(x):
    centered = x - jnp.mean(x, axis=-1, keepdims=True)
    spread_of = lax.rsqrt(jnp.mean(centered * centered, axis=-1, keepdims=True) + EPSILON)
    return centered * spread_of, spread_of


def contract(left, right, left_dim, right_dim):
    return lax.dot_general(
        left, right, (((left_dim,), (right_dim,)), ((), ())), preferred_element_type=jnp.float32
    )


def head_masks(width):
    lane = lax.broadcasted_iota(jnp.int32, (1, width), 1)
    return [(lane >= h * HD) & (lane < (h + 1) * HD) for h in range(width // HD)]


def head_probs(q, k, mask):
    own = jnp.where(mask, q, jnp.zeros_like(q)) * jnp.bfloat16(HD ** (-0.5))
    scores = contract(own, k, 1, 1)
    column = lax.broadcasted_iota(jnp.int32, scores.shape, 1)
    scores = jnp.where(column < SEQ, scores, -1e30)
    raised = jnp.exp(scores - jnp.max(scores, axis=-1, keepdims=True))
    return raised * (1.0 / jnp.sum(raised, axis=-1, keepdims=True))


def attention_forward(x, turn, gain, shift, weight, bias, out_weight, half, kept, after):
    images, seq, width = x.shape
    rows, inner = ROWS, weight.shape[2]

    def kernel(
        turn_ref, x_ref, gain_ref, shift_ref, w_ref, b_ref, wo_ref,
        *refs
    ):
        own_ref, other_ref, pad_ref, n_ref, q_ref, k_ref, v_ref, o_ref, held = refs[
            len(kept) + len(after) :
        ]
        held[...] = jnp.zeros_like(held)
        for i in range(TRIO):
            held[i, :seq, :] = x_ref[i].astype(jnp.float32)
        value = held[...].reshape(TRIO * rows, width)
        pad_ref[...] = value.astype(jnp.bfloat16).reshape(TRIO, rows, width)
        n = (normal(value)[0] * gain_ref[...] + shift_ref[...]).astype(jnp.bfloat16)
        n_ref[...] = n.reshape(TRIO, rows, width)
        for j, ref in enumerate((q_ref, k_ref, v_ref)):
            made = jnp.dot(n, w_ref[j], preferred_element_type=jnp.float32) + b_ref[j : j + 1, :]
            ref[...] = made.astype(jnp.bfloat16).reshape(TRIO, rows, inner)
        for i in range(TRIO):
            q, k, v = q_ref[i], k_ref[i], v_ref[i]
            mixed = jnp.zeros((rows, inner), jnp.float32)
            for mask in head_masks(inner):
                probs = head_probs(q, k, mask).astype(jnp.bfloat16)
                head = jnp.dot(probs, v, preferred_element_type=jnp.float32)
                mixed = jnp.where(mask, head, mixed)
            o_ref[i] = mixed.astype(jnp.bfloat16)
        mixed = o_ref[...].reshape(TRIO * rows, inner)
        part = jnp.dot(mixed, wo_ref[...], preferred_element_type=jnp.float32)
        part = part.astype(jnp.bfloat16).reshape(TRIO, rows, width)

        @pl.when(pl.program_id(0) == 0)
        def _():
            other_ref[...] = part

        @pl.when(pl.program_id(0) == 1)
        def _():
            own_ref[...] = part


    wide = shape_of((images, rows, width), jnp.bfloat16)
    slim = shape_of((images, rows, inner), jnp.bfloat16)
    blocks = images // TRIO

    def place(i, turn):
        return (2 * (1 - i) + half, 0, 0)

    def whole(array):
        return pl.BlockSpec(array.shape, lambda i, turn: (0,) * array.ndim)

    small = (gain, shift, weight, bias, out_weight)
    return pl.pallas_call(
        kernel,
        grid_spec=pltpu.PrefetchScalarGridSpec(
            num_scalar_prefetch=1,
            grid=(blocks // 2,),
            in_specs=[
                pl.BlockSpec(
                    (TRIO, seq, width), lambda i, turn: ((2 * (1 - i) + half + turn[0]) % blocks, 0, 0)
                )
            ]
            + [whole(array) for array in small]
            + [pl.BlockSpec(memory_space=pl.ANY)] * (len(kept) + len(after)),
            out_specs=[pl.BlockSpec((TRIO, rows, width), lambda i, turn: (0, 0, 0))] * 2
            + [pl.BlockSpec((TRIO, *a.shape[1:]), place) for a in [wide] * 2 + [slim] * 4],
            scratch_shapes=[pltpu.VMEM((TRIO, rows, width), jnp.float32)],
        ),
        out_shape=[shape_of((TRIO, rows, width), jnp.bfloat16)] * 2 + [wide] * 2 + [slim] * 4,
        input_output_aliases={7 + i: 2 + i for i in range(len(kept))},
        compiler_params=pltpu.CompilerParams(vmem_limit_bytes=VMEM),
        cost_estimate=cost(9),
        name="attention_forward",
    )(turn, x, *small, *kept, *after)


def attention_backward(own_da, other_da, x, n, q, k, v, o, weight, out_weight, after):
    images, rows, width = x.shape
    inner = weight.shape[2]

    def kernel(
        own_ref, other_ref, x_ref, n_ref, q_ref, k_ref, v_ref, o_ref, w_ref, wo_ref,
        own_back_ref, other_back_ref, dw_ref, dwo_ref, dbias_ref, sums_ref, held,
    ):
        @pl.when(pl.program_id(0) == 0)
        def _():
            dw_ref[...] = jnp.zeros_like(dw_ref)
            dwo_ref[...] = jnp.zeros_like(dwo_ref)
            dbias_ref[...] = jnp.zeros_like(dbias_ref)
            sums_ref[...] = jnp.zeros_like(sums_ref)

        joined = PAIR * rows
        mine = pl.program_id(0) < images // PAIR // 2
        da = jnp.where(mine, own_ref[...], other_ref[...]).reshape(joined, width)
        do_all = contract(da, wo_ref[...], 1, 1).astype(jnp.bfloat16).reshape(PAIR, rows, inner)
        scale = HD ** (-0.5)
        for i in range(PAIR):
            q, k, v, do = q_ref[i], k_ref[i], v_ref[i], do_all[i]
            dq = dk = dv = jnp.zeros((rows, inner), jnp.float32)
            for mask in head_masks(inner):
                probs = head_probs(q, k, mask)
                dv = jnp.where(mask, contract(probs.astype(jnp.bfloat16), do, 0, 0), dv)
                dp = contract(jnp.where(mask, do, jnp.zeros_like(do)), v, 1, 1)
                ds = probs * (dp - jnp.sum(probs * dp, axis=-1, keepdims=True))
                ds = ds.astype(jnp.bfloat16)
                dq = jnp.where(mask, jnp.dot(ds, k, preferred_element_type=jnp.float32), dq)
                dk = jnp.where(mask, contract(ds, q, 0, 0), dk)
            held[0, i] = (dq * scale).astype(jnp.bfloat16)
            held[1, i] = (dk * scale).astype(jnp.bfloat16)
            held[2, i] = dv.astype(jnp.bfloat16)
        n = n_ref[...].reshape(joined, width)
        back = jnp.zeros((joined, width), jnp.float32)
        for j in range(3):
            grad = held[j].reshape(joined, inner)
            dw_ref[j] += contract(n, grad, 0, 0)
            back += contract(grad, w_ref[j], 1, 1)
            if j != 1:
                dbias_ref[j // 2 : j // 2 + 1, :] += jnp.sum(
                    grad.astype(jnp.float32), axis=0, keepdims=True
                )
        dwo_ref[0] += contract(da, o_ref[...].reshape(joined, inner), 0, 0)
        back_low = back.astype(jnp.bfloat16).reshape(PAIR, rows, width)

        @pl.when(mine)
        def _():
            own_back_ref[...] = back_low

        @pl.when(jnp.logical_not(mine))
        def _():
            other_back_ref[...] = back_low

        unit, _ = normal(x_ref[...].reshape(joined, width).astype(jnp.float32))
        sums_ref[0:1, :] += jnp.sum(back * unit, axis=0, keepdims=True)
        sums_ref[1:2, :] += jnp.sum(back, axis=0, keepdims=True)
        sums_ref[2:3, :] += jnp.sum(da.astype(jnp.float32), axis=0, keepdims=True)

    return call(
        kernel, "attention_backward", images // PAIR,
        [(own_da, "low"), (other_da, "high")]
        + [(a, True) for a in (x, n, q, k, v, o)] + [(weight, False), (out_weight, False)],
        [
            (shape_of((images // 2, rows, width), jnp.bfloat16), "low"),
            (shape_of((images // 2, rows, width), jnp.bfloat16), "high"),
            (shape_of((3, width, inner), jnp.float32), False),
            (shape_of((1, width, inner), jnp.float32), False),
            (shape_of((2, inner), jnp.float32), False),
            (shape_of((3, width), jnp.float32), False),
        ],
        after=after, each=PAIR, us=30,
        scratch=[pltpu.VMEM((3, PAIR, rows, inner), jnp.bfloat16)],
    )


def middle_norm(near, far, x, out_bias, gain, shift, after):
    each = near[0].shape[0]
    count, (_, rows, width) = 2 * each, x.shape

    def kernel(near_a, near_b, far_a, far_b, x_ref, bias_ref, gain_ref, shift_ref, *refs):
        middle_ref, n_ref = refs[len(after) :]
        early = pl.program_id(0) < each
        total = jnp.where(early, near_a[0], near_b[0]).astype(jnp.float32)
        total = total + jnp.where(early, far_a[0], far_b[0]).astype(jnp.float32)
        middle = x_ref[0].astype(jnp.float32) + total + bias_ref[...]
        middle_ref[0] = middle
        n_ref[0] = (normal(middle)[0] * gain_ref[...] + shift_ref[...]).astype(jnp.bfloat16)

    block = (1, rows, width)
    low = pl.BlockSpec(block, lambda i: (jnp.minimum(i, each - 1), 0, 0))
    high = pl.BlockSpec(block, lambda i: (jnp.maximum(i - each, 0), 0, 0))
    one = pl.BlockSpec(block, lambda i: (i, 0, 0))
    flat = pl.BlockSpec((1, width), lambda i: (0, 0))
    return pl.pallas_call(
        kernel,
        grid=(count,),
        in_specs=[low, high, low, high, one, flat, flat, flat]
        + [pl.BlockSpec(memory_space=pl.ANY)] * len(after),
        out_specs=[one, one],
        out_shape=[shape_of((count, rows, width), kind) for kind in (jnp.float32, jnp.bfloat16)],
        compiler_params=pltpu.CompilerParams(vmem_limit_bytes=VMEM),
        cost_estimate=cost(7),
        name="middle_norm",
    )(*near, *far, x, out_bias, gain, shift, *after)


def norm_back(dn, unit, spread_of, gain):
    dz = dn * gain
    mean = jnp.mean(dz, axis=-1, keepdims=True)
    return spread_of * (dz - mean - unit * jnp.mean(dz * unit, axis=-1, keepdims=True))


def middle_back(near, far, dots, gates, chosen, pair, n, router_weight, down_bias, middle, upstream, gain, after):
    count, wide = down_bias.shape[0], pair.shape[2]

    def kernel(
        near_ref, far_ref, dots_ref, gates_ref, chosen_ref, pair_ref, n_ref, router_ref, bias_ref,
        middle_ref, g_ref, gain_ref, grad_ref, da_ref, sums_ref, drouter_ref, dbias_ref,
    ):
        @pl.when(pl.program_id(0) == 0)
        def _():
            sums_ref[...] = jnp.zeros_like(sums_ref)
            drouter_ref[...] = jnp.zeros_like(drouter_ref)
            dbias_ref[...] = jnp.zeros_like(dbias_ref)

        g = g_ref[0]
        lane = lax.broadcasted_iota(jnp.int32, (g.shape[0], count), 1)
        named = (lane == chosen_ref[0, :, 0:1]) | (lane == chosen_ref[0, :, 1:2])
        dmix = dots_ref[0] + jnp.where(named, contract(g, bias_ref[...], 1, 1), 0.0)
        gate = gates_ref[0, :, :count]
        dlogits = gate * (dmix - jnp.sum(gate * dmix, axis=-1, keepdims=True))
        dlogits = dlogits.astype(jnp.bfloat16)
        drouter_ref[...] += contract(dlogits, n_ref[0], 0, 0)
        dbias_ref[...] += contract(pair_ref[0], g, 0, 0)
        dn = near_ref[0].astype(jnp.float32) + far_ref[0].astype(jnp.float32)
        dn = dn + contract(dlogits, router_ref[...], 1, 1)
        unit, spread_of = normal(middle_ref[0])
        grad = g.astype(jnp.float32) + norm_back(dn, unit, spread_of, gain_ref[...])
        grad_ref[0] = grad
        da_ref[0] = grad.astype(jnp.bfloat16)
        sums_ref[0:1, :] += jnp.sum(dn * unit, axis=0, keepdims=True)
        sums_ref[1:2, :] += jnp.sum(dn, axis=0, keepdims=True)

    width = middle.shape[2]
    return call(
        kernel, "middle_back", middle.shape[0],
        [(a, True) for a in (near, far, dots, gates, chosen, pair, n)]
        + [(router_weight, False), (down_bias, False), (middle, True), (upstream, True), (gain, False)],
        [
            (shape_of(middle.shape, jnp.float32), True),
            (shape_of(middle.shape, jnp.bfloat16), True),
            (shape_of((2, width), jnp.float32), False),
            (shape_of((count, width), jnp.float32), False),
            (shape_of((wide, width), jnp.float32), False),
        ],
        after=after, us=8,
    )


def finish(near, far, middle, pair, down_bias, after):
    def kernel(near_ref, far_ref, middle_ref, pair_ref, bias_ref, out_ref):
        total = near_ref[0].astype(jnp.float32) + far_ref[0].astype(jnp.float32)
        total = total + jnp.dot(pair_ref[0], bias_ref[...], preferred_element_type=jnp.float32)
        out_ref[0] = (middle_ref[0] + total).astype(jnp.bfloat16)

    return call(
        kernel, "finish", middle.shape[0],
        [(near, True), (far, True), (middle, True), (pair, True), (down_bias, False)],
        [(shape_of(middle.shape, jnp.bfloat16), True)],
        after=after, us=8,
    )[0]


def input_back(own, other, x, own_grad, other_grad, gain, turn, after):
    images, _, width = x.shape
    half = images // 2

    def kernel(turn_ref, own_ref, other_ref, x_ref, own_grad_ref, other_grad_ref, gain_ref, *refs):
        out_ref = refs[-1]
        step = pl.program_id(0)
        place = (step + turn_ref[0]) % images
        mine = step < half
        dn = jnp.where(mine, own_ref[0], other_ref[0]).astype(jnp.float32)
        unit, spread_of = normal(x_ref[0].astype(jnp.float32))
        grad = jnp.where(mine, own_grad_ref[0], other_grad_ref[0])
        grad = grad + norm_back(dn, unit, spread_of, gain_ref[...])
        for j in range(images):

            @pl.when(place == j)
            def _():
                out_ref[j * SEQ : (j + 1) * SEQ, :] = grad[:SEQ]

    def low(shape):
        return pl.BlockSpec((1, *shape[1:]), lambda i, t: (jnp.minimum(i, half - 1), 0, 0))

    def high(shape):
        return pl.BlockSpec((1, *shape[1:]), lambda i, t: (jnp.maximum(i - half, 0), 0, 0))

    return pl.pallas_call(
        kernel,
        grid_spec=pltpu.PrefetchScalarGridSpec(
            num_scalar_prefetch=1,
            grid=(images,),
            in_specs=[
                low(own.shape),
                high(other.shape),
                pl.BlockSpec((1, *x.shape[1:]), lambda i, t: (i, 0, 0)),
                low(own_grad.shape),
                high(other_grad.shape),
                pl.BlockSpec(gain.shape, lambda i, t: (0, 0)),
            ]
            + [pl.BlockSpec(memory_space=pl.ANY)] * len(after),
            out_specs=pl.BlockSpec((images * SEQ, width), lambda i, t: (0, 0)),
        ),
        out_shape=jax.ShapeDtypeStruct((images * SEQ, width), jnp.float32),
        compiler_params=pltpu.CompilerParams(vmem_limit_bytes=VMEM),
        cost_estimate=cost(15),
        name="input_back",
    )(turn, own, other, x, own_grad, other_grad, gain, *after)


def to_core(value):
    return lax.ppermute(value, "tensor", pairs(lax.axis_size("tensor"), 1))


def across(value):
    return lax.ppermute(value, "tensor", pairs(lax.axis_size("tensor"), 2))


def core_sum(own, other, zero):
    got = to_core(other)
    return (own.astype(jnp.float32) + got.astype(jnp.float32) + zero).astype(jnp.bfloat16)


def zero_of(value):
    return value[(0,) * value.ndim].astype(jnp.float32) * 0.0


def ring_owner(way, step):
    index = lax.axis_index("dp")
    place = jnp.where(index % 2 == 0, index // 2, 7 - index // 2)
    place = (place - way * (step + 1)) % 8
    return jnp.where(place < 4, 2 * place, 15 - 2 * place).astype(jnp.int32)


def ring_hop(value, way):
    path = [(RING[i], RING[(i + way) % len(RING)]) for i in range(len(RING))]
    return lax.ppermute(value, "dp", path)


def ring_add(got, sources, steps, kinds, after):
    groups, came = len(sources), got[0].shape[0]
    many, total, cols = sources[0][0].shape
    rows, part = total // 8, 2
    owners = jnp.stack([ring_owner(way, step) for step in steps for way in (1, -1)])
    joint = all(kind == kinds[0] for kind in kinds)

    def kernel(owners_ref, *refs):
        held, locals_, outs = refs[:2], refs[2 : 2 + 2 * groups], refs[2 + 2 * groups + len(after) :]
        for g in range(groups):
            for d in range(2):
                value = locals_[2 * g + d][...]
                if g < came:
                    value = value.astype(jnp.float32) + held[d][g].astype(jnp.float32)
                if joint:
                    outs[d][g] = value.astype(kinds[g])
                else:
                    outs[2 * g + d][0] = value.astype(kinds[g])

    def source(slot):
        return pl.BlockSpec((part, rows, cols), lambda i, own: (i, own[slot], 0))

    def stack(count):
        return pl.BlockSpec((count, part, rows, cols), lambda i, own: (0, i, 0, 0))

    if joint:
        outs = [((groups, many, rows, cols), kinds[0])] * 2
    else:
        outs = [((1, many, rows, cols), kind) for kind in kinds for _ in range(2)]
    return pl.pallas_call(
        kernel,
        grid_spec=pltpu.PrefetchScalarGridSpec(
            num_scalar_prefetch=1,
            grid=(many // part,),
            in_specs=[stack(came)] * 2
            + [source(i) for i in range(2 * groups)]
            + [pl.BlockSpec(memory_space=pl.ANY)] * len(after),
            out_specs=[stack(dims[0]) for dims, _ in outs],
        ),
        out_shape=[jax.ShapeDtypeStruct(dims, kind) for dims, kind in outs],
        compiler_params=pltpu.CompilerParams(vmem_limit_bytes=VMEM),
        cost_estimate=cost(5),
        name="ring_add",
    )(owners, *got, *[piece for pair in sources for piece in pair], *after)


def on_device(
    embedded,
    attn_gain,
    attn_shift,
    qkv_weight,
    qv_bias,
    out_weight,
    out_bias,
    moe_gain,
    moe_shift,
    router_weight,
    up_weight,
    up_bias,
    down_weight,
    down_bias,
    routes,
    cotangent,
):
    tok_rows, width = embedded.shape
    images = tok_rows // SEQ
    half = images // 2
    head_width = qkv_weight.shape[2]
    expert_count = up_weight.shape[0]
    core = lax.axis_index("tensor") % 2
    f32 = jnp.float32

    def own_first(value, fill):
        value = value.reshape(images, SEQ, value.shape[1])
        value = jnp.pad(value, ((0, 0), (0, ROWS - SEQ), (0, 0)), constant_values=fill)
        return jnp.where(core == 0, value, jnp.roll(value, half, axis=0))

    def in_order(own, other):
        low = jnp.where(core == 0, own, other)
        high = jnp.where(core == 0, other, own)
        return jnp.concatenate([low, high])[:, :SEQ].reshape(tok_rows, width)

    def row(value):
        return value.astype(f32)[None]

    def imaged(value):
        return value.reshape(-1, ROWS, value.shape[1])

    turn = (half * core).astype(jnp.int32)[None]
    bias_rows = jnp.stack([qv_bias[0], jnp.zeros_like(qv_bias[0]), qv_bias[1]]).astype(f32)
    images_in = embedded.reshape(images, SEQ, width)
    kept, near, far = (), [], []
    for i in range(2):
        own, other, *kept = attention_forward(
            images_in, turn // TRIO, row(attn_gain), row(attn_shift),
            qkv_weight, bias_rows, out_weight, i, tuple(kept), tuple(near),
        )
        near.append(core_sum(own, other, 0.0))
        far.append(across(near[i]))
    x, normed, queries, keys, values, mixed = kept

    chosen = own_first(routes, -1).reshape(images * ROWS, 2)
    rows, columns, plan, tiles = route_plan(chosen, expert_count)
    upstream = own_first(cotangent, 0)
    grad_buffers = spread(upstream.reshape(images * ROWS, width), rows, plan, expert_count)

    extra = 128
    router_twice = jnp.pad(
        jnp.concatenate([router_weight, router_weight], axis=1),
        ((0, 0), (0, extra - 2 * expert_count)),
    )
    bias_twice = jnp.pad(
        jnp.concatenate([down_bias, down_bias]), ((0, extra - 2 * expert_count), (0, 0))
    )
    middle, own_normed = middle_norm(
        near, far, x, row(out_bias), row(moe_gain), row(moe_shift),
        (grad_buffers, router_twice, bias_twice, tiles),
    )
    own_rows = half * ROWS
    buffers, gates, mix_pair = gated_spread(
        own_normed.reshape(own_rows, width), to_core(own_normed).reshape(own_rows, width),
        rows, plan, chosen, router_twice, expert_count, extra,
    )
    gates, mix_pair, chosen = imaged(gates), imaged(mix_pair), imaged(chosen)
    group = expert_count // GROUPS

    def experts_of(i, after):
        return expert_pass(
            buffers, grad_buffers, up_weight, up_bias, down_weight, tiles, i * group, group, after
        )

    ringed = lax.axis_size("dp") == len(RING)
    low = jnp.bfloat16
    y_first, back_first, *first, bias_first = experts_of(0, ())
    moving = ()
    if ringed:
        rows_each = width // 8
        moving = [
            lax.dynamic_slice_in_dim(grad, ring_owner(way, 0) * rows_each, rows_each, 1)[None]
            for grad, way in zip(first, (1, -1))
        ]
    y_second, back_second, *second, bias_second = experts_of(1, tuple(moving))

    def round_trip(step, kinds, *after):
        if not ringed:
            return ()
        got = [ring_hop(value, way) for value, way in zip(moving, (1, -1))]
        if step < 8:
            return ring_add(got, [first, second], [step, step - 1], kinds, after)
        return ring_add(got, [second], [step - 1], kinds, after)

    moving = round_trip(1, [low, low])
    own, other, dots = collect((back_first, back_second), columns, plan, width, tuple(moving))
    back_near = core_sum(imaged(own), imaged(other), 0.0)
    back_far = across(back_near)
    dots = dots[:, : 2 * expert_count].T
    dots = dots[:expert_count] + dots[expert_count:]
    dots = dots[:, :own_rows] + to_core(dots[:, own_rows:])
    dots = (dots + across(dots)).T.reshape(half, ROWS, expert_count)
    moving = round_trip(2, [low, low], back_near)
    own_y, other_y = collect((y_first, y_second), columns, plan, width, (back_near, *moving))
    moving = round_trip(3, [low, low], other_y)
    middle_grad, own_da, moe_sums, router_sums, bias_sums = middle_back(
        back_near, back_far, dots, gates, chosen, mix_pair, own_normed, router_weight,
        down_bias, middle, upstream, row(moe_gain), tuple(moving),
    )
    y_near = core_sum(imaged(own_y), imaged(other_y), zero_of(back_far))
    y_far = across(y_near)
    other_da, other_grad = to_core(own_da), to_core(middle_grad)
    moving = round_trip(4, [low, low], own_da)
    own, other, grad_qkv, grad_out, grad_qv_bias, sums = attention_backward(
        own_da, other_da, x, normed, queries, keys, values, mixed, qkv_weight, out_weight,
        (y_far, *moving),
    )
    last_near = core_sum(own, other, 0.0)
    last_far = across(last_near)
    slim = jnp.concatenate([grad_qkv, grad_out]).astype(low)
    slim = lax.psum_scatter(slim, "dp", scatter_dimension=1, tiled=True).astype(f32)
    moving = round_trip(5, [low, low], last_near)

    def after_round(value):
        return value + zero_of(moving[1]) if ringed else value

    def meet(value, axis, bit):
        return value + lax.ppermute(value, axis, pairs(lax.axis_size(axis), bit))

    own_out = finish(y_near, y_far, middle, mix_pair, bias_twice, (last_near, *moving))
    layer_out = in_order(own_out, to_core(own_out))
    router_bias = [router_sums, bias_sums[:expert_count] + bias_sums[expert_count : 2 * expert_count]]
    tensor_parts = jnp.concatenate([sums[:2]] + [0.5 * part for part in (moe_sums, *router_bias)])
    tensor_parts = meet(meet(after_round(tensor_parts), "tensor", 1), "tensor", 2)
    packed = jnp.concatenate(
        [
            tensor_parts,
            sums[2:],
            jnp.pad(grad_qv_bias, ((0, 0), (0, width - head_width))),
            bias_first[:, 0],
            bias_second[:, 0],
        ]
    )
    moving = round_trip(6, [low, low], layer_out)
    last = (last_near.astype(f32) + last_far.astype(f32)).astype(low)
    grad_embedded = input_back(
        last, to_core(last), x, middle_grad, other_grad, row(attn_gain), turn, tuple(moving)
    )
    if ringed:
        packed = meet(after_round(packed), "dp", 1)
        up_first, down_first, *moving = round_trip(7, [f32, low], grad_embedded, packed)
        packed = meet(after_round(packed), "dp", 2)
        up_second, down_second = round_trip(8, [f32], packed)
        packed = meet(packed + zero_of(up_second), "dp", 4)
    else:
        packed = lax.psum(packed, "dp")
        up_first, down_first, up_second, down_second = [
            lax.psum_scatter(grad, "dp", scatter_dimension=1, tiled=True).astype(f32)[None]
            for grad in (*first, *second)
        ]
    grad_up = jnp.concatenate([up_first[0], up_second[0]])
    grad_down = jnp.concatenate([down_first[0], down_second[0]]).transpose(0, 2, 1)
    base = 4 + 2 * expert_count
    return (
        layer_out,
        grad_embedded,
        packed[0],
        packed[1],
        slim[:3],
        packed[base + 1 : base + 3, :head_width],
        slim[3].T,
        packed[base],
        packed[2],
        packed[3],
        packed[4 : 4 + expert_count].T,
        grad_up,
        packed[base + 3 :],
        grad_down,
        packed[4 + expert_count : base],
    )


def solution(mesh):
    return jax.shard_map(
        on_device,
        mesh=mesh,
        in_specs=(
            P("dp", None),
            P(),
            P(),
            P(None, None, "tensor"),
            P(None, "tensor"),
            P("tensor", None),
            P(),
            P(),
            P(),
            P(),
            P(None, None, "tensor"),
            P(None, "tensor"),
            P(None, "tensor", None),
            P(),
            P("dp", None),
            P("dp", None),
        ),
        out_specs=(
            P("dp", None),
            P("dp", None),
            P(),
            P(),
            P(None, "dp", "tensor"),
            P(None, "tensor"),
            P("tensor", "dp"),
            P(),
            P(),
            P(),
            P(),
            P(None, "dp", "tensor"),
            P(None, "tensor"),
            P(None, "tensor", "dp"),
            P(),
        ),
        check_vma=False,
    )
```

```python
import jax
import jax.numpy as jnp
from jax import lax
from jax.experimental import pallas as pl
from jax.experimental.pallas import tpu as pltpu
from jax.sharding import PartitionSpec as P

SEQ = 197
HD = 64
EPSILON = 1e-06
RING = (0, 2, 4, 6, 7, 5, 3, 1)


def pairs(count, bit):
    return [(i, i ^ bit) for i in range(count)]


ROWS = 208
PAIR = 2
TRIO = 3
BLOCK = 416
GROUPS = 2
LOCAL = 960
ROOM = 1024
TILE = 256
VMEM = 56 * 1024 * 1024


def cost(us):
    return pl.CostEstimate(flops=int(us * 1.1e9), bytes_accessed=0, transcendentals=0)


def route_plan(routes, expert_count):
    tokens = routes.shape[0]
    blocks = -(-tokens // BLOCK)
    padded = jnp.pad(routes.T, ((0, 0), (0, blocks * BLOCK - tokens)), constant_values=-1)
    experts = jnp.arange(expert_count, dtype=jnp.int32)[:, None]
    first = padded[0][None, :] == experts
    second = padded[1][None, :] == experts
    named = (first | second).reshape(expert_count * blocks, BLOCK)
    ahead = jnp.arange(BLOCK)[:, None] < jnp.arange(BLOCK)[None, :]
    rank = jnp.dot(
        named.astype(jnp.bfloat16), ahead.astype(jnp.bfloat16), preferred_element_type=jnp.float32
    )
    rank = rank.astype(jnp.int32).reshape(expert_count, blocks, BLOCK)
    chunks = (jnp.sum(named.astype(jnp.int32), axis=1).reshape(expert_count, blocks) + 15) // 16
    inside = jnp.cumsum(chunks, axis=0) - chunks
    offset = jnp.cumsum(chunks, axis=1) - chunks
    place = (rank + 16 * inside[:, :, None]).reshape(expert_count, blocks * BLOCK)
    target = jnp.stack(
        [jnp.sum(jnp.where(hot, place + 1, 0), axis=0) - 1 for hot in (first, second)]
    )
    tiles = (jnp.sum(chunks, axis=1) * 16 + TILE - 1) // TILE
    plan = jnp.concatenate([chunks.T.reshape(-1), inside.T.reshape(-1), offset.T.reshape(-1)])
    rows = target.reshape(2, blocks, BLOCK).transpose(1, 0, 2)
    return rows, target.T, plan, tiles


def spread(source, rows, plan, expert_count):
    blocks, cols = rows.shape[0], source.shape[1]

    def kernel(plan_ref, rows_ref, source_ref, out_ref, local):
        block = pl.program_id(0)

        @pl.when(block == 0)
        def _():
            out_ref[...] = jnp.zeros_like(out_ref)

        part = LOCAL // 3
        for i in range(3):
            slot = lax.broadcasted_iota(jnp.int32, (part, BLOCK), 0) + i * part
            hot = (slot == rows_ref[0, 0:1, :]) | (slot == rows_ref[0, 1:2, :])
            local[pl.ds(i * part, part), :] = jnp.dot(
                jnp.where(hot, 1.0, 0.0).astype(jnp.bfloat16),
                source_ref[...],
                preferred_element_type=jnp.float32,
            ).astype(jnp.bfloat16)
        for e in range(expert_count):
            at = block * expert_count + e
            size = blocks * expert_count
            begin, goal = plan_ref[size + at], plan_ref[2 * size + at]

            def move(j, carry):
                here = pl.ds(pl.multiple_of((begin + j) * 16, 16), 16)
                there = pl.ds(pl.multiple_of((goal + j) * 16, 16), 16)
                out_ref[e, there, :] = local[here, :]
                return carry

            lax.fori_loop(0, plan_ref[at], move, 0)

    return pl.pallas_call(
        kernel,
        grid_spec=pltpu.PrefetchScalarGridSpec(
            num_scalar_prefetch=1,
            grid=(blocks,),
            in_specs=[
                pl.BlockSpec((1, 2, BLOCK), lambda b, plan: (b, 0, 0)),
                pl.BlockSpec((BLOCK, cols), lambda b, plan: (b, 0)),
            ],
            out_specs=pl.BlockSpec((expert_count, ROOM, cols), lambda b, plan: (0, 0, 0)),
            scratch_shapes=[pltpu.VMEM((LOCAL, cols), jnp.bfloat16)],
        ),
        out_shape=jax.ShapeDtypeStruct((expert_count, ROOM, cols), jnp.bfloat16),
        compiler_params=pltpu.CompilerParams(vmem_limit_bytes=VMEM),
        cost_estimate=cost(15),
        name="spread",
    )(plan, rows, source)


def gated_spread(own, other, rows, plan, chosen, router, expert_count, extra):
    blocks, cols = rows.shape[0], own.shape[1]
    both = cols + extra

    def kernel(
        plan_ref, rows_ref, own_ref, other_ref, chosen_ref, router_ref,
        out_ref, gate_ref, pair_ref, local,
    ):
        block = pl.program_id(0)
        source = jnp.where(block < blocks // 2, own_ref[...], other_ref[...])

        @pl.when(block == 0)
        def _():
            out_ref[...] = jnp.zeros_like(out_ref)

        logits = jnp.dot(source, router_ref[...], preferred_element_type=jnp.float32)
        lane = lax.broadcasted_iota(jnp.int32, logits.shape, 1)
        first, second = lane < expert_count, lane < 2 * expert_count
        expert = jnp.where(first, lane, lane - expert_count)
        top = jnp.max(jnp.where(first, logits, -jnp.inf), axis=-1, keepdims=True)
        raised = jnp.where(second, jnp.exp(logits - top), 0.0)
        gate = raised / jnp.sum(jnp.where(first, raised, 0.0), axis=-1, keepdims=True)
        named = (expert == chosen_ref[:, 0:1]) | (expert == chosen_ref[:, 1:2])
        mixing = jnp.where(named & second, gate, 0.0)
        high = mixing.astype(jnp.bfloat16).astype(jnp.float32)
        pair = jnp.where(first, high, mixing - high).astype(jnp.bfloat16)
        gate_ref[...] = gate
        pair_ref[...] = pair
        part = LOCAL // 3
        for i in range(3):
            slot = lax.broadcasted_iota(jnp.int32, (part, BLOCK), 0) + i * part
            hot = (slot == rows_ref[0, 0:1, :]) | (slot == rows_ref[0, 1:2, :])
            hot = jnp.where(hot, 1.0, 0.0).astype(jnp.bfloat16)
            for begin, end, value in ((0, cols, source), (cols, both, pair)):
                local[pl.ds(i * part, part), begin:end] = jnp.dot(
                    hot, value, preferred_element_type=jnp.float32
                ).astype(jnp.bfloat16)
        for e in range(expert_count):
            at = block * expert_count + e
            size = blocks * expert_count
            begin, goal = plan_ref[size + at], plan_ref[2 * size + at]

            def move(j, carry):
                here = pl.ds(pl.multiple_of((begin + j) * 16, 16), 16)
                there = pl.ds(pl.multiple_of((goal + j) * 16, 16), 16)
                out_ref[e, there, :] = local[here, :]
                return carry

            lax.fori_loop(0, plan_ref[at], move, 0)

    return pl.pallas_call(
        kernel,
        grid_spec=pltpu.PrefetchScalarGridSpec(
            num_scalar_prefetch=1,
            grid=(blocks,),
            in_specs=[
                pl.BlockSpec((1, 2, BLOCK), lambda b, plan: (b, 0, 0)),
                pl.BlockSpec((BLOCK, cols), lambda b, plan: (jnp.minimum(b, blocks // 2 - 1), 0)),
                pl.BlockSpec((BLOCK, cols), lambda b, plan: (jnp.maximum(b - blocks // 2, 0), 0)),
                pl.BlockSpec((BLOCK, 2), lambda b, plan: (b, 0)),
                pl.BlockSpec(router.shape, lambda b, plan: (0, 0)),
            ],
            out_specs=[
                pl.BlockSpec((expert_count, ROOM, both), lambda b, plan: (0, 0, 0)),
                pl.BlockSpec((BLOCK, extra), lambda b, plan: (b, 0)),
                pl.BlockSpec((BLOCK, extra), lambda b, plan: (b, 0)),
            ],
            scratch_shapes=[pltpu.VMEM((LOCAL, both), jnp.bfloat16)],
        ),
        out_shape=[
            jax.ShapeDtypeStruct((expert_count, ROOM, both), jnp.bfloat16),
            jax.ShapeDtypeStruct((blocks * BLOCK, extra), jnp.float32),
            jax.ShapeDtypeStruct((blocks * BLOCK, extra), jnp.bfloat16),
        ],
        compiler_params=pltpu.CompilerParams(vmem_limit_bytes=VMEM),
        cost_estimate=cost(20),
        name="gated_spread",
    )(plan, rows, own, other, chosen, router)


def collect(buffers, columns, plan, kept, after):
    each, room, cols = buffers[0].shape
    expert_count = each * len(buffers)
    blocks = columns.shape[0] // BLOCK
    extra = cols - kept

    def kernel(plan_ref, columns_ref, *refs):
        held, refs = refs[: len(buffers)], refs[len(buffers) + len(after) :]
        own_ref, other_ref, local = refs[0], refs[1], refs[-1]
        block = pl.program_id(0)
        mine = block < blocks // 2

        @pl.when(block == 0)
        def _():
            local[...] = jnp.zeros_like(local)

        for e in range(expert_count):
            at = block * expert_count + e
            size = blocks * expert_count
            begin, goal = plan_ref[size + at], plan_ref[2 * size + at]

            def move(j, carry):
                here = pl.ds(pl.multiple_of((begin + j) * 16, 16), 16)
                there = pl.ds(pl.multiple_of((goal + j) * 16, 16), 16)
                local[here, :] = held[e // each][e % each, there, :]
                return carry

            lax.fori_loop(0, plan_ref[at], move, 0)
        part = BLOCK // 2
        for i in range(2):
            rows = pl.ds(i * part, part)
            slot = lax.broadcasted_iota(jnp.int32, (part, LOCAL), 1)
            hot = (slot == columns_ref[rows, 0:1]) | (slot == columns_ref[rows, 1:2])
            total = jnp.dot(
                jnp.where(hot, 1.0, 0.0).astype(jnp.bfloat16),
                local[...],
                preferred_element_type=jnp.float32,
            )
            low = total[:, :kept].astype(jnp.bfloat16)

            @pl.when(mine)
            def _():
                own_ref[rows, :] = low

            @pl.when(jnp.logical_not(mine))
            def _():
                other_ref[rows, :] = low

            if extra:
                refs[2][rows, :] = total[:, kept:]

    out_specs = [
        pl.BlockSpec((BLOCK, kept), lambda b, plan: (jnp.minimum(b, blocks // 2 - 1), 0)),
        pl.BlockSpec((BLOCK, kept), lambda b, plan: (jnp.maximum(b - blocks // 2, 0), 0)),
    ]
    out_shape = [jax.ShapeDtypeStruct((blocks // 2 * BLOCK, kept), jnp.bfloat16)] * 2
    if extra:
        out_specs.append(pl.BlockSpec((BLOCK, extra), lambda b, plan: (b, 0)))
        out_shape.append(jax.ShapeDtypeStruct((blocks * BLOCK, extra), jnp.float32))
    return pl.pallas_call(
        kernel,
        grid_spec=pltpu.PrefetchScalarGridSpec(
            num_scalar_prefetch=1,
            grid=(blocks,),
            in_specs=[
                pl.BlockSpec((BLOCK, 2), lambda b, plan: (b, 0)),
            ]
            + [pl.BlockSpec((each, room, cols), lambda b, plan: (0, 0, 0))] * len(buffers)
            + [pl.BlockSpec(memory_space=pl.ANY)] * len(after),
            out_specs=out_specs,
            scratch_shapes=[pltpu.VMEM((LOCAL, cols), jnp.bfloat16)],
        ),
        out_shape=out_shape,
        compiler_params=pltpu.CompilerParams(vmem_limit_bytes=VMEM),
        cost_estimate=cost(16),
        name="collect",
    )(plan, columns, *buffers, *after)


GELU_A = 0.7978845608028654
GELU_B = 0.044715


def expert_pass(inputs, grads, up_weight, up_bias, down_weight, tiles, first, count, after):
    expert_count, room, cols = inputs.shape
    width, hidden = up_weight.shape[1:]

    def kernel(
        tiles_ref, x_ref, g_ref, up_ref, bias_ref, down_ref, *refs
    ):
        y_ref, dx_ref, dup_ref, ddown_ref, dbias_ref, mixed, dpre = refs[len(after) :]
        step = pl.program_id(0)
        expert = step + first

        @pl.when(step == 0)
        def _():
            mixed[...] = jnp.zeros_like(mixed)
            dpre[...] = jnp.zeros_like(dpre)

        dbias_ref[...] = jnp.zeros_like(dbias_ref)
        lane = lax.broadcasted_iota(jnp.int32, (TILE, cols - width), 1)

        def tile(r, carry):
            rows = pl.ds(pl.multiple_of(r * TILE, TILE), TILE)
            x = x_ref[0, rows, :width]
            g = g_ref[0, rows, :]
            gates = x_ref[0, rows, width:].astype(jnp.float32)
            own = (lane == expert) | (lane == expert + expert_count)
            mix = jnp.sum(jnp.where(own, gates, 0.0), axis=1, keepdims=True)
            pre = jnp.dot(x, up_ref[0], preferred_element_type=jnp.float32)
            pre = pre + bias_ref[0].astype(jnp.float32)
            back = lax.dot_general(
                g, down_ref[0], (((1,), (1,)), ((), ())), preferred_element_type=jnp.float32
            )
            square = pre * pre
            bend = jnp.tanh(pre * (GELU_A + GELU_A * GELU_B * square))
            upper = 0.5 + 0.5 * bend
            act = pre * upper
            slope = upper + 0.5 * pre * (1.0 - bend * bend) * (
                GELU_A + 3.0 * GELU_A * GELU_B * square
            )
            dot = jnp.sum(act * back, axis=1, keepdims=True)
            act_low = (mix * act).astype(jnp.bfloat16)
            down = (mix * back * slope).astype(jnp.bfloat16)
            mixed[rows, :] = act_low
            dpre[rows, :] = down
            dbias_ref[0] += jnp.sum(down.astype(jnp.float32), axis=0, keepdims=True)
            y_ref[0, rows, :] = jnp.dot(
                act_low, down_ref[0], preferred_element_type=jnp.float32
            ).astype(jnp.bfloat16)
            dx_ref[0, rows, :width] = lax.dot_general(
                down, up_ref[0], (((1,), (1,)), ((), ())), preferred_element_type=jnp.float32
            ).astype(jnp.bfloat16)
            high = dot.astype(jnp.bfloat16).astype(jnp.float32)
            dx_ref[0, rows, width:] = jnp.where(
                lane == expert, high, jnp.where(lane == expert + expert_count, dot - high, 0.0)
            ).astype(jnp.bfloat16)
            return carry

        lax.fori_loop(0, tiles_ref[expert], tile, 0)

        def weights(depth):
            rows = pl.ds(0, depth)
            for i in range(width // TILE):
                part = pl.ds(i * TILE, TILE)
                dup_ref[0, part, :] = lax.dot_general(
                    x_ref[0, rows, part], dpre[rows, :], (((0,), (0,)), ((), ())),
                    preferred_element_type=jnp.float32,
                ).astype(jnp.bfloat16)
                ddown_ref[0, part, :] = lax.dot_general(
                    g_ref[0, rows, part], mixed[rows, :], (((0,), (0,)), ((), ())),
                    preferred_element_type=jnp.float32,
                ).astype(jnp.bfloat16)

        pl.when(tiles_ref[expert] <= 3)(lambda: weights(3 * TILE))
        pl.when(tiles_ref[expert] > 3)(lambda: weights(room))

    def whole(*dims):
        return pl.BlockSpec((1, *dims), lambda e, tiles: (e + first, 0, 0))

    def own(*dims):
        return pl.BlockSpec((1, *dims), lambda e, tiles: (e, 0, 0))

    shapes = [
        ((room, width), jnp.bfloat16),
        ((room, cols), jnp.bfloat16),
        ((width, hidden), jnp.bfloat16),
        ((width, hidden), jnp.bfloat16),
        ((1, hidden), jnp.float32),
    ]
    return pl.pallas_call(
        kernel,
        grid_spec=pltpu.PrefetchScalarGridSpec(
            num_scalar_prefetch=1,
            grid=(count,),
            in_specs=[
                whole(room, cols),
                whole(room, width),
                whole(width, hidden),
                whole(1, hidden),
                whole(hidden, width),
            ]
            + [pl.BlockSpec(memory_space=pl.ANY)] * len(after),
            out_specs=[own(*dims) for dims, _ in shapes],
            scratch_shapes=[pltpu.VMEM((room, hidden), jnp.bfloat16)] * 2,
        ),
        out_shape=[jax.ShapeDtypeStruct((count, *dims), kind) for dims, kind in shapes],
        compiler_params=pltpu.CompilerParams(vmem_limit_bytes=VMEM),
        cost_estimate=pl.CostEstimate(
            flops=count * 12 * 768 * width * hidden,
            bytes_accessed=count * (4 * room * (cols + width) + 8 * width * hidden),
            transcendentals=count * 768 * hidden,
        ),
        name="experts",
    )(tiles, inputs, grads, up_weight, up_bias[:, None, :], down_weight, *after)


def call(kernel, name, grid, ins, outs, after=(), scratch=(), us=5, each=1, turn=None):
    turn = jnp.zeros((1,), jnp.int32) if turn is None else turn

    def spec(shape, split):
        zeros = (0,) * (len(shape) - 1)
        if split == "turned":
            return pl.BlockSpec((each, *shape[1:]), lambda i, t: ((i + t[0]) % grid, *zeros))
        if split == "low":
            return pl.BlockSpec(
                (each, *shape[1:]), lambda i, t: (jnp.minimum(i, grid // 2 - 1), *zeros)
            )
        if split == "high":
            return pl.BlockSpec(
                (each, *shape[1:]), lambda i, t: (jnp.maximum(i - grid // 2, 0), *zeros)
            )
        if split:
            return pl.BlockSpec((each, *shape[1:]), lambda i, t: (i, *zeros))
        return pl.BlockSpec(tuple(shape), lambda i, t: (0, *zeros))

    count, late = len(ins), len(after)

    def body(turn_ref, *refs):
        kernel(*refs[:count], *refs[count + late :])

    return pl.pallas_call(
        body,
        grid_spec=pltpu.PrefetchScalarGridSpec(
            num_scalar_prefetch=1,
            grid=(grid,),
            in_specs=[spec(a.shape, split) for a, split in ins]
            + [pl.BlockSpec(memory_space=pl.ANY)] * late,
            out_specs=[spec(a.shape, split) for a, split in outs],
            scratch_shapes=list(scratch),
        ),
        out_shape=[a for a, _ in outs],
        compiler_params=pltpu.CompilerParams(vmem_limit_bytes=VMEM),
        cost_estimate=cost(us),
        name=name,
    )(turn, *[a for a, _ in ins], *after)


def shape_of(dims, kind):
    return jax.ShapeDtypeStruct(tuple(dims), kind)


def normal(x):
    centered = x - jnp.mean(x, axis=-1, keepdims=True)
    spread_of = lax.rsqrt(jnp.mean(centered * centered, axis=-1, keepdims=True) + EPSILON)
    return centered * spread_of, spread_of


def contract(left, right, left_dim, right_dim):
    return lax.dot_general(
        left, right, (((left_dim,), (right_dim,)), ((), ())), preferred_element_type=jnp.float32
    )


def head_masks(width):
    lane = lax.broadcasted_iota(jnp.int32, (1, width), 1)
    return [(lane >= h * HD) & (lane < (h + 1) * HD) for h in range(width // HD)]


def head_probs(q, k, mask):
    own = jnp.where(mask, q, jnp.zeros_like(q)) * jnp.bfloat16(HD ** (-0.5))
    scores = contract(own, k, 1, 1)
    column = lax.broadcasted_iota(jnp.int32, scores.shape, 1)
    scores = jnp.where(column < SEQ, scores, -1e30)
    raised = jnp.exp(scores - jnp.max(scores, axis=-1, keepdims=True))
    return raised * (1.0 / jnp.sum(raised, axis=-1, keepdims=True))


def attention_forward(x, turn, gain, shift, weight, bias, out_weight):
    images, seq, width = x.shape
    rows, inner = ROWS, weight.shape[2]
    blocks = images // TRIO

    def kernel(
        turn_ref, x_ref, gain_ref, shift_ref, w_ref, b_ref, wo_ref,
        *refs
    ):
        own_ref, other_ref, pad_ref, n_ref, q_ref, k_ref, v_ref, o_ref, held = refs
        held[...] = jnp.zeros_like(held)
        for i in range(TRIO):
            held[i, :seq, :] = x_ref[i].astype(jnp.float32)
        value = held[...].reshape(TRIO * rows, width)
        pad_ref[...] = value.astype(jnp.bfloat16).reshape(TRIO, rows, width)
        n = (normal(value)[0] * gain_ref[...] + shift_ref[...]).astype(jnp.bfloat16)
        n_ref[...] = n.reshape(TRIO, rows, width)
        for j, ref in enumerate((q_ref, k_ref, v_ref)):
            made = jnp.dot(n, w_ref[j], preferred_element_type=jnp.float32) + b_ref[j : j + 1, :]
            ref[...] = made.astype(jnp.bfloat16).reshape(TRIO, rows, inner)
        for i in range(TRIO):
            q, k, v = q_ref[i], k_ref[i], v_ref[i]
            mixed = jnp.zeros((rows, inner), jnp.float32)
            for mask in head_masks(inner):
                probs = head_probs(q, k, mask).astype(jnp.bfloat16)
                head = jnp.dot(probs, v, preferred_element_type=jnp.float32)
                mixed = jnp.where(mask, head, mixed)
            o_ref[i] = mixed.astype(jnp.bfloat16)
        mixed = o_ref[...].reshape(TRIO * rows, inner)
        part = jnp.dot(mixed, wo_ref[...], preferred_element_type=jnp.float32)
        part = part.astype(jnp.bfloat16).reshape(TRIO, rows, width)

        @pl.when(pl.program_id(0) < blocks // 2)
        def _():
            other_ref[...] = part

        @pl.when(pl.program_id(0) >= blocks // 2)
        def _():
            own_ref[...] = part


    wide = shape_of((images, rows, width), jnp.bfloat16)
    slim = shape_of((images, rows, inner), jnp.bfloat16)
    def place(i, turn):
        return ((i + blocks // 2) % blocks, 0, 0)

    def whole(array):
        return pl.BlockSpec(array.shape, lambda i, turn: (0,) * array.ndim)

    small = (gain, shift, weight, bias, out_weight)
    return pl.pallas_call(
        kernel,
        grid_spec=pltpu.PrefetchScalarGridSpec(
            num_scalar_prefetch=1,
            grid=(blocks,),
            in_specs=[
                pl.BlockSpec(
                    (TRIO, seq, width), lambda i, turn: ((i + blocks // 2 + turn[0]) % blocks, 0, 0)
                )
            ]
            + [whole(array) for array in small],
            out_specs=[
                pl.BlockSpec(
                    (TRIO, rows, width), lambda i, turn: (jnp.maximum(i - blocks // 2, 0), 0, 0)
                ),
                pl.BlockSpec(
                    (TRIO, rows, width), lambda i, turn: (jnp.minimum(i, blocks // 2 - 1), 0, 0)
                ),
            ]
            + [pl.BlockSpec((TRIO, *a.shape[1:]), place) for a in [wide] * 2 + [slim] * 4],
            scratch_shapes=[pltpu.VMEM((TRIO, rows, width), jnp.float32)],
        ),
        out_shape=[shape_of((images // 2, rows, width), jnp.bfloat16)] * 2 + [wide] * 2 + [slim] * 4,
        compiler_params=pltpu.CompilerParams(vmem_limit_bytes=VMEM),
        cost_estimate=cost(18),
        name="attention_forward",
    )(turn, x, *small)


def attention_backward(own_da, other_da, x, n, q, k, v, o, weight, out_weight, after):
    images, rows, width = x.shape
    inner = weight.shape[2]

    def kernel(
        own_ref, other_ref, x_ref, n_ref, q_ref, k_ref, v_ref, o_ref, w_ref, wo_ref,
        own_back_ref, other_back_ref, dw_ref, dwo_ref, dbias_ref, sums_ref, held,
    ):
        @pl.when(pl.program_id(0) == 0)
        def _():
            dw_ref[...] = jnp.zeros_like(dw_ref)
            dwo_ref[...] = jnp.zeros_like(dwo_ref)
            dbias_ref[...] = jnp.zeros_like(dbias_ref)
            sums_ref[...] = jnp.zeros_like(sums_ref)

        joined = PAIR * rows
        mine = pl.program_id(0) < images // PAIR // 2
        da = jnp.where(mine, own_ref[...], other_ref[...]).reshape(joined, width)
        do_all = contract(da, wo_ref[...], 1, 1).astype(jnp.bfloat16).reshape(PAIR, rows, inner)
        scale = HD ** (-0.5)
        for i in range(PAIR):
            q, k, v, do = q_ref[i], k_ref[i], v_ref[i], do_all[i]
            dq = dk = dv = jnp.zeros((rows, inner), jnp.float32)
            for mask in head_masks(inner):
                probs = head_probs(q, k, mask)
                dv = jnp.where(mask, contract(probs.astype(jnp.bfloat16), do, 0, 0), dv)
                dp = contract(jnp.where(mask, do, jnp.zeros_like(do)), v, 1, 1)
                ds = probs * (dp - jnp.sum(probs * dp, axis=-1, keepdims=True))
                ds = ds.astype(jnp.bfloat16)
                dq = jnp.where(mask, jnp.dot(ds, k, preferred_element_type=jnp.float32), dq)
                dk = jnp.where(mask, contract(ds, q, 0, 0), dk)
            held[0, i] = (dq * scale).astype(jnp.bfloat16)
            held[1, i] = (dk * scale).astype(jnp.bfloat16)
            held[2, i] = dv.astype(jnp.bfloat16)
        n = n_ref[...].reshape(joined, width)
        back = jnp.zeros((joined, width), jnp.float32)
        for j in range(3):
            grad = held[j].reshape(joined, inner)
            dw_ref[j] += contract(n, grad, 0, 0)
            back += contract(grad, w_ref[j], 1, 1)
            if j != 1:
                dbias_ref[j // 2 : j // 2 + 1, :] += jnp.sum(
                    grad.astype(jnp.float32), axis=0, keepdims=True
                )
        dwo_ref[0] += contract(da, o_ref[...].reshape(joined, inner), 0, 0)
        back_low = back.astype(jnp.bfloat16).reshape(PAIR, rows, width)

        @pl.when(mine)
        def _():
            own_back_ref[...] = back_low

        @pl.when(jnp.logical_not(mine))
        def _():
            other_back_ref[...] = back_low

        unit, _ = normal(x_ref[...].reshape(joined, width).astype(jnp.float32))
        sums_ref[0:1, :] += jnp.sum(back * unit, axis=0, keepdims=True)
        sums_ref[1:2, :] += jnp.sum(back, axis=0, keepdims=True)
        sums_ref[2:3, :] += jnp.sum(da.astype(jnp.float32), axis=0, keepdims=True)

    return call(
        kernel, "attention_backward", images // PAIR,
        [(own_da, "low"), (other_da, "high")]
        + [(a, True) for a in (x, n, q, k, v, o)] + [(weight, False), (out_weight, False)],
        [
            (shape_of((images // 2, rows, width), jnp.bfloat16), "low"),
            (shape_of((images // 2, rows, width), jnp.bfloat16), "high"),
            (shape_of((3, width, inner), jnp.float32), False),
            (shape_of((1, width, inner), jnp.float32), False),
            (shape_of((2, inner), jnp.float32), False),
            (shape_of((3, width), jnp.float32), False),
        ],
        after=after, each=PAIR, us=30,
        scratch=[pltpu.VMEM((3, PAIR, rows, inner), jnp.bfloat16)],
    )


def middle_norm(near, far, x, out_bias, gain, shift, after):
    def kernel(near_ref, far_ref, x_ref, bias_ref, gain_ref, shift_ref, middle_ref, n_ref):
        total = near_ref[0].astype(jnp.float32) + far_ref[0].astype(jnp.float32)
        middle = x_ref[0].astype(jnp.float32) + total + bias_ref[...]
        middle_ref[0] = middle
        n_ref[0] = (normal(middle)[0] * gain_ref[...] + shift_ref[...]).astype(jnp.bfloat16)

    return call(
        kernel, "middle_norm", near.shape[0],
        [(near, True), (far, True), (x, True), (out_bias, False), (gain, False), (shift, False)],
        [(shape_of(near.shape, jnp.float32), True), (shape_of(near.shape, jnp.bfloat16), True)],
        after=after, us=8,
    )


def norm_back(dn, unit, spread_of, gain):
    dz = dn * gain
    mean = jnp.mean(dz, axis=-1, keepdims=True)
    return spread_of * (dz - mean - unit * jnp.mean(dz * unit, axis=-1, keepdims=True))


def middle_back(near, far, dots, gates, chosen, pair, n, router_weight, down_bias, middle, upstream, gain, after):
    count, wide = down_bias.shape[0], pair.shape[2]

    def kernel(
        near_ref, far_ref, dots_ref, gates_ref, chosen_ref, pair_ref, n_ref, router_ref, bias_ref,
        middle_ref, g_ref, gain_ref, grad_ref, da_ref, sums_ref, drouter_ref, dbias_ref,
    ):
        @pl.when(pl.program_id(0) == 0)
        def _():
            sums_ref[...] = jnp.zeros_like(sums_ref)
            drouter_ref[...] = jnp.zeros_like(drouter_ref)
            dbias_ref[...] = jnp.zeros_like(dbias_ref)

        g = g_ref[0]
        lane = lax.broadcasted_iota(jnp.int32, (g.shape[0], count), 1)
        named = (lane == chosen_ref[0, :, 0:1]) | (lane == chosen_ref[0, :, 1:2])
        dmix = dots_ref[0] + jnp.where(named, contract(g, bias_ref[...], 1, 1), 0.0)
        gate = gates_ref[0, :, :count]
        dlogits = gate * (dmix - jnp.sum(gate * dmix, axis=-1, keepdims=True))
        dlogits = dlogits.astype(jnp.bfloat16)
        drouter_ref[...] += contract(dlogits, n_ref[0], 0, 0)
        dbias_ref[...] += contract(pair_ref[0], g, 0, 0)
        dn = near_ref[0].astype(jnp.float32) + far_ref[0].astype(jnp.float32)
        dn = dn + contract(dlogits, router_ref[...], 1, 1)
        unit, spread_of = normal(middle_ref[0])
        grad = g.astype(jnp.float32) + norm_back(dn, unit, spread_of, gain_ref[...])
        grad_ref[0] = grad
        da_ref[0] = grad.astype(jnp.bfloat16)
        sums_ref[0:1, :] += jnp.sum(dn * unit, axis=0, keepdims=True)
        sums_ref[1:2, :] += jnp.sum(dn, axis=0, keepdims=True)

    width = middle.shape[2]
    return call(
        kernel, "middle_back", middle.shape[0],
        [(a, True) for a in (near, far, dots, gates, chosen, pair, n)]
        + [(router_weight, False), (down_bias, False), (middle, True), (upstream, True), (gain, False)],
        [
            (shape_of(middle.shape, jnp.float32), True),
            (shape_of(middle.shape, jnp.bfloat16), True),
            (shape_of((2, width), jnp.float32), False),
            (shape_of((count, width), jnp.float32), False),
            (shape_of((wide, width), jnp.float32), False),
        ],
        after=after, us=8,
    )


def finish(near, far, middle, pair, down_bias, after):
    def kernel(near_ref, far_ref, middle_ref, pair_ref, bias_ref, out_ref):
        total = near_ref[0].astype(jnp.float32) + far_ref[0].astype(jnp.float32)
        total = total + jnp.dot(pair_ref[0], bias_ref[...], preferred_element_type=jnp.float32)
        out_ref[0] = (middle_ref[0] + total).astype(jnp.bfloat16)

    return call(
        kernel, "finish", middle.shape[0],
        [(near, True), (far, True), (middle, True), (pair, True), (down_bias, False)],
        [(shape_of(middle.shape, jnp.bfloat16), True)],
        after=after, us=8,
    )[0]


def input_back(own, other, x, own_grad, other_grad, gain, turn, after):
    images, _, width = x.shape
    half = images // 2

    def kernel(turn_ref, own_ref, other_ref, x_ref, own_grad_ref, other_grad_ref, gain_ref, *refs):
        out_ref = refs[-1]
        step = pl.program_id(0)
        place = (step + turn_ref[0]) % images
        mine = step < half
        dn = jnp.where(mine, own_ref[0], other_ref[0]).astype(jnp.float32)
        unit, spread_of = normal(x_ref[0].astype(jnp.float32))
        grad = jnp.where(mine, own_grad_ref[0], other_grad_ref[0])
        grad = grad + norm_back(dn, unit, spread_of, gain_ref[...])
        for j in range(images):

            @pl.when(place == j)
            def _():
                out_ref[j * SEQ : (j + 1) * SEQ, :] = grad[:SEQ]

    def low(shape):
        return pl.BlockSpec((1, *shape[1:]), lambda i, t: (jnp.minimum(i, half - 1), 0, 0))

    def high(shape):
        return pl.BlockSpec((1, *shape[1:]), lambda i, t: (jnp.maximum(i - half, 0), 0, 0))

    return pl.pallas_call(
        kernel,
        grid_spec=pltpu.PrefetchScalarGridSpec(
            num_scalar_prefetch=1,
            grid=(images,),
            in_specs=[
                low(own.shape),
                high(other.shape),
                pl.BlockSpec((1, *x.shape[1:]), lambda i, t: (i, 0, 0)),
                low(own_grad.shape),
                high(other_grad.shape),
                pl.BlockSpec(gain.shape, lambda i, t: (0, 0)),
            ]
            + [pl.BlockSpec(memory_space=pl.ANY)] * len(after),
            out_specs=pl.BlockSpec((images * SEQ, width), lambda i, t: (0, 0)),
        ),
        out_shape=jax.ShapeDtypeStruct((images * SEQ, width), jnp.float32),
        compiler_params=pltpu.CompilerParams(vmem_limit_bytes=VMEM),
        cost_estimate=cost(15),
        name="input_back",
    )(turn, own, other, x, own_grad, other_grad, gain, *after)


def to_core(value):
    return lax.ppermute(value, "tensor", pairs(lax.axis_size("tensor"), 1))


def across(value):
    return lax.ppermute(value, "tensor", pairs(lax.axis_size("tensor"), 2))


def core_sum(own, other, zero):
    got = to_core(other)
    return (own.astype(jnp.float32) + got.astype(jnp.float32) + zero).astype(jnp.bfloat16)


def zero_of(value):
    return value[(0,) * value.ndim].astype(jnp.float32) * 0.0


def ring_owner(way, step):
    index = lax.axis_index("dp")
    place = jnp.where(index % 2 == 0, index // 2, 7 - index // 2)
    place = (place - way * (step + 1)) % 8
    return jnp.where(place < 4, 2 * place, 15 - 2 * place).astype(jnp.int32)


def ring_hop(value, way):
    path = [(RING[i], RING[(i + way) % len(RING)]) for i in range(len(RING))]
    return lax.ppermute(value, "dp", path)


def ring_add(got, sources, steps, kinds, after, carry=()):
    groups, came = len(sources), got[0].shape[0]
    many, total, cols = sources[0][0].shape
    rows, part = total // 8, 2
    owners = jnp.stack([ring_owner(way, step) for step in steps for way in (1, -1)])
    joint = all(kind == kinds[0] for kind in kinds)

    def kernel(owners_ref, *refs):
        held, locals_ = refs[:2], refs[2 : 2 + 2 * groups]
        outs = refs[2 + 2 * groups + len(after) + len(carry) :]
        for g in range(groups):
            for d in range(2):
                value = locals_[2 * g + d][...]
                if g < came:
                    value = value.astype(jnp.float32) + held[d][g].astype(jnp.float32)
                if joint:
                    outs[d][g] = value.astype(kinds[g])
                else:
                    outs[2 * g + d][0] = value.astype(kinds[g])

    def source(slot):
        return pl.BlockSpec((part, rows, cols), lambda i, own: (i, own[slot], 0))

    def stack(count):
        return pl.BlockSpec((count, part, rows, cols), lambda i, own: (0, i, 0, 0))

    if joint:
        outs = [((groups, many, rows, cols), kinds[0])] * 2
    else:
        outs = [((1, many, rows, cols), kind) for kind in kinds for _ in range(2)]
    return pl.pallas_call(
        kernel,
        grid_spec=pltpu.PrefetchScalarGridSpec(
            num_scalar_prefetch=1,
            grid=(many // part,),
            in_specs=[stack(came)] * 2
            + [source(i) for i in range(2 * groups)]
            + [pl.BlockSpec(memory_space=pl.ANY)] * (len(after) + len(carry)),
            out_specs=[stack(dims[0]) for dims, _ in outs]
            + [pl.BlockSpec(memory_space=pl.ANY)] * len(carry),
        ),
        out_shape=[jax.ShapeDtypeStruct(dims, kind) for dims, kind in outs]
        + [jax.ShapeDtypeStruct(value.shape, value.dtype) for value in carry],
        input_output_aliases={
            3 + 2 * groups + len(after) + i: len(outs) + i for i in range(len(carry))
        },
        compiler_params=pltpu.CompilerParams(vmem_limit_bytes=VMEM),
        cost_estimate=cost(5),
        name="ring_add",
    )(owners, *got, *[piece for pair in sources for piece in pair], *after, *carry)


def on_device(
    embedded,
    attn_gain,
    attn_shift,
    qkv_weight,
    qv_bias,
    out_weight,
    out_bias,
    moe_gain,
    moe_shift,
    router_weight,
    up_weight,
    up_bias,
    down_weight,
    down_bias,
    routes,
    cotangent,
):
    tok_rows, width = embedded.shape
    images = tok_rows // SEQ
    half = images // 2
    head_width = qkv_weight.shape[2]
    expert_count = up_weight.shape[0]
    core = lax.axis_index("tensor") % 2
    f32 = jnp.float32

    def own_first(value, fill):
        value = value.reshape(images, SEQ, value.shape[1])
        value = jnp.pad(value, ((0, 0), (0, ROWS - SEQ), (0, 0)), constant_values=fill)
        return jnp.where(core == 0, value, jnp.roll(value, half, axis=0))

    def in_order(own, other):
        low = jnp.where(core == 0, own, other)
        high = jnp.where(core == 0, other, own)
        return jnp.concatenate([low, high])[:, :SEQ].reshape(tok_rows, width)

    def row(value):
        return value.astype(f32)[None]

    def imaged(value):
        return value.reshape(-1, ROWS, value.shape[1])

    turn = (half * core).astype(jnp.int32)[None]
    bias_rows = jnp.stack([qv_bias[0], jnp.zeros_like(qv_bias[0]), qv_bias[1]]).astype(f32)
    images_in = embedded.reshape(images, SEQ, width)
    own, other, x, normed, queries, keys, values, mixed = attention_forward(
        images_in, turn // TRIO, row(attn_gain), row(attn_shift), qkv_weight, bias_rows, out_weight
    )
    near = core_sum(own, other, 0.0)
    far = across(near)

    chosen = own_first(routes, -1).reshape(images * ROWS, 2)
    rows, columns, plan, tiles = route_plan(chosen, expert_count)
    upstream = own_first(cotangent, 0)
    grad_buffers = spread(upstream.reshape(images * ROWS, width), rows, plan, expert_count)

    extra = 128
    router_twice = jnp.pad(
        jnp.concatenate([router_weight, router_weight], axis=1),
        ((0, 0), (0, extra - 2 * expert_count)),
    )
    bias_twice = jnp.pad(
        jnp.concatenate([down_bias, down_bias]), ((0, extra - 2 * expert_count), (0, 0))
    )
    middle, own_normed = middle_norm(
        near, far, x, row(out_bias), row(moe_gain), row(moe_shift),
        (grad_buffers, router_twice, bias_twice, tiles),
    )
    own_rows = half * ROWS
    buffers, gates, mix_pair = gated_spread(
        own_normed.reshape(own_rows, width), to_core(own_normed).reshape(own_rows, width),
        rows, plan, chosen, router_twice, expert_count, extra,
    )
    gates, mix_pair, chosen = imaged(gates), imaged(mix_pair), imaged(chosen)
    group = expert_count // GROUPS

    def experts_of(i, after):
        return expert_pass(
            buffers, grad_buffers, up_weight, up_bias, down_weight, tiles, i * group, group, after
        )

    ringed = lax.axis_size("dp") == len(RING)
    low = jnp.bfloat16
    y_first, back_first, *first, bias_first = experts_of(0, ())
    moving = ()
    if ringed:
        rows_each = width // 8
        moving = [
            lax.dynamic_slice_in_dim(grad, ring_owner(way, 0) * rows_each, rows_each, 1)[None]
            for grad, way in zip(first, (1, -1))
        ]
    y_second, back_second, *second, bias_second = experts_of(1, tuple(moving))

    def round_trip(step, kinds, after=(), carry=()):
        if not ringed:
            return carry
        got = [ring_hop(value, way) for value, way in zip(moving, (1, -1))]
        if step < 8:
            return ring_add(got, [first, second], [step, step - 1], kinds, after, carry)
        return ring_add(got, [second], [step - 1], kinds, after, carry)

    moving = round_trip(1, [low, low])
    own, other, dots = collect((back_first, back_second), columns, plan, width, tuple(moving))
    back_near = core_sum(imaged(own), imaged(other), 0.0)
    back_far = across(back_near)
    dots = dots[:, : 2 * expert_count].T
    dots = dots[:expert_count] + dots[expert_count:]
    dots = dots[:, :own_rows] + to_core(dots[:, own_rows:])
    dots = (dots + across(dots)).T.reshape(half, ROWS, expert_count)
    moving = round_trip(2, [low, low], (back_near,))
    own_y, other_y = collect((y_first, y_second), columns, plan, width, (back_near, *moving))
    moving = round_trip(3, [low, low], (other_y,))
    middle_grad, own_da, moe_sums, router_sums, bias_sums = middle_back(
        back_near, back_far, dots, gates, chosen, mix_pair, own_normed, router_weight,
        down_bias, middle, upstream, row(moe_gain), tuple(moving),
    )
    *moving, own_da = round_trip(4, [low, low], (), (own_da,))
    other_da, other_grad = to_core(own_da), to_core(middle_grad)
    y_near = core_sum(imaged(own_y), imaged(other_y), zero_of(own_da))
    y_far = across(y_near)
    own, other, grad_qkv, grad_out, grad_qv_bias, sums = attention_backward(
        own_da, other_da, x, normed, queries, keys, values, mixed, qkv_weight, out_weight,
        (y_near, *moving),
    )
    *moving, own, other = round_trip(5, [low, low], (y_far,), (own, other))
    last_near = core_sum(own, other, 0.0)
    last_far = across(last_near)

    def after_round(value):
        return value + zero_of(moving[1]).astype(value.dtype) if ringed else value

    def meet(value, axis, bit):
        return value + lax.ppermute(value, axis, pairs(lax.axis_size(axis), bit))

    def halve(values, bit, axis):
        mine = (lax.axis_index("dp") >> bit) % 2
        keep = lax.dynamic_index_in_dim(values, mine, axis, keepdims=True)
        give = lax.dynamic_index_in_dim(values, 1 - mine, axis, keepdims=True).astype(low)
        return keep, lax.ppermute(give, "dp", pairs(8, 1 << bit))

    own_out = finish(y_near, y_far, middle, mix_pair, bias_twice, (last_near, *moving))
    layer_out = in_order(own_out, to_core(own_out))
    router_bias = [router_sums, bias_sums[:expert_count] + bias_sums[expert_count : 2 * expert_count]]
    packed = jnp.concatenate(
        [
            sums[:2],
            0.5 * moe_sums,
            *[0.5 * part for part in router_bias],
            sums[2:],
            jnp.pad(grad_qv_bias, ((0, 0), (0, width - head_width))),
            bias_first[:, 0],
            bias_second[:, 0],
        ]
    )
    slim = jnp.concatenate([grad_qkv, grad_out])
    base = 4 + 2 * expert_count
    last = (last_near.astype(f32) + last_far.astype(f32)).astype(low)
    other_last = to_core(last)

    def input_grad():
        return input_back(
            last, other_last, x, middle_grad, other_grad, row(attn_gain), turn, tuple(moving)
        )

    if ringed:
        slim = slim.reshape(4, 2, 2, 2, width // 8, head_width)
        packed = after_round(packed)
        for step, bit, axis in ((6, 0, 3), (7, 1, 2), (8, 2, 1)):
            keep, got = halve(after_round(slim) if step > 6 else slim, bit, axis)
            sent = lax.ppermute(packed, "dp", pairs(8, 1 << bit))
            if step == 6:
                moving = round_trip(6, [low, low], (last_near, layer_out))
            elif step == 7:
                up_first, down_first, *moving = round_trip(7, [f32, low])
                grad_embedded = input_grad()
            else:
                moving = round_trip(8, [f32], (grad_embedded,))
            slim = keep.astype(f32) + got.astype(f32) + zero_of(moving[0])
            packed = after_round(packed + sent)
        up_second, down_second = moving
        slim = slim.reshape(4, width // 8, head_width)
    else:
        grad_embedded = input_grad()
        packed = lax.psum(packed, "dp")
        slim = lax.psum_scatter(slim, "dp", scatter_dimension=1, tiled=True)
        up_first, down_first, up_second, down_second = [
            lax.psum_scatter(grad, "dp", scatter_dimension=1, tiled=True).astype(f32)[None]
            for grad in (*first, *second)
        ]
    grad_up = jnp.concatenate([up_first[0], up_second[0]])
    grad_down = jnp.concatenate([down_first[0], down_second[0]]).transpose(0, 2, 1)
    tensor_parts = meet(meet(packed[:base], "tensor", 1), "tensor", 2)
    packed = jnp.concatenate([tensor_parts, packed[base:]])
    return (
        layer_out,
        grad_embedded,
        packed[0],
        packed[1],
        slim[:3],
        packed[base + 1 : base + 3, :head_width],
        slim[3].T,
        packed[base],
        packed[2],
        packed[3],
        packed[4 : 4 + expert_count].T,
        grad_up,
        packed[base + 3 :],
        grad_down,
        packed[4 + expert_count : base],
    )


def solution(mesh):
    return jax.shard_map(
        on_device,
        mesh=mesh,
        in_specs=(
            P("dp", None),
            P(),
            P(),
            P(None, None, "tensor"),
            P(None, "tensor"),
            P("tensor", None),
            P(),
            P(),
            P(),
            P(),
            P(None, None, "tensor"),
            P(None, "tensor"),
            P(None, "tensor", None),
            P(),
            P("dp", None),
            P("dp", None),
        ),
        out_specs=(
            P("dp", None),
            P("dp", None),
            P(),
            P(),
            P(None, "dp", "tensor"),
            P(None, "tensor"),
            P("tensor", "dp"),
            P(),
            P(),
            P(),
            P(),
            P(None, "dp", "tensor"),
            P(None, "tensor"),
            P(None, "tensor", "dp"),
            P(),
        ),
        check_vma=False,
    )
```

```python
import jax
import jax.numpy as jnp
from jax import lax
from jax.experimental import pallas as pl
from jax.experimental.pallas import tpu as pltpu
from jax.sharding import PartitionSpec as P

SEQ = 197
HD = 64
EPSILON = 1e-06
RING = (0, 2, 4, 6, 7, 5, 3, 1)


def pairs(count, bit):
    return [(i, i ^ bit) for i in range(count)]


ROWS = 208
PAIR = 2
BLOCK = 416
GROUPS = 2
LOCAL = 960
ROOM = 1024
TILE = 256
VMEM = 56 * 1024 * 1024


def cost(us):
    return pl.CostEstimate(flops=int(us * 1.1e9), bytes_accessed=0, transcendentals=0)


def route_plan(routes, expert_count):
    tokens = routes.shape[0]
    blocks = -(-tokens // BLOCK)
    padded = jnp.pad(routes.T, ((0, 0), (0, blocks * BLOCK - tokens)), constant_values=-1)
    experts = jnp.arange(expert_count, dtype=jnp.int32)[:, None]
    first = padded[0][None, :] == experts
    second = padded[1][None, :] == experts
    named = (first | second).reshape(expert_count * blocks, BLOCK)
    ahead = jnp.arange(BLOCK)[:, None] < jnp.arange(BLOCK)[None, :]
    rank = jnp.dot(
        named.astype(jnp.bfloat16), ahead.astype(jnp.bfloat16), preferred_element_type=jnp.float32
    )
    rank = rank.astype(jnp.int32).reshape(expert_count, blocks, BLOCK)
    chunks = (jnp.sum(named.astype(jnp.int32), axis=1).reshape(expert_count, blocks) + 15) // 16
    inside = jnp.cumsum(chunks, axis=0) - chunks
    offset = jnp.cumsum(chunks, axis=1) - chunks
    place = (rank + 16 * inside[:, :, None]).reshape(expert_count, blocks * BLOCK)
    target = jnp.stack(
        [jnp.sum(jnp.where(hot, place + 1, 0), axis=0) - 1 for hot in (first, second)]
    )
    tiles = (jnp.sum(chunks, axis=1) * 16 + TILE - 1) // TILE
    plan = jnp.concatenate([chunks.T.reshape(-1), inside.T.reshape(-1), offset.T.reshape(-1)])
    rows = target.reshape(2, blocks, BLOCK).transpose(1, 0, 2)
    return rows, target.T, plan, tiles


def spread(source, rows, plan, expert_count):
    blocks, cols = rows.shape[0], source.shape[1]

    def kernel(plan_ref, rows_ref, source_ref, out_ref, local):
        block = pl.program_id(0)

        @pl.when(block == 0)
        def _():
            out_ref[...] = jnp.zeros_like(out_ref)

        part = LOCAL // 3
        for i in range(3):
            slot = lax.broadcasted_iota(jnp.int32, (part, BLOCK), 0) + i * part
            hot = (slot == rows_ref[0, 0:1, :]) | (slot == rows_ref[0, 1:2, :])
            local[pl.ds(i * part, part), :] = jnp.dot(
                jnp.where(hot, 1.0, 0.0).astype(jnp.bfloat16),
                source_ref[...],
                preferred_element_type=jnp.float32,
            ).astype(jnp.bfloat16)
        for e in range(expert_count):
            at = block * expert_count + e
            size = blocks * expert_count
            begin, goal = plan_ref[size + at], plan_ref[2 * size + at]

            def move(j, carry):
                here = pl.ds(pl.multiple_of((begin + j) * 16, 16), 16)
                there = pl.ds(pl.multiple_of((goal + j) * 16, 16), 16)
                out_ref[e, there, :] = local[here, :]
                return carry

            lax.fori_loop(0, plan_ref[at], move, 0)

    return pl.pallas_call(
        kernel,
        grid_spec=pltpu.PrefetchScalarGridSpec(
            num_scalar_prefetch=1,
            grid=(blocks,),
            in_specs=[
                pl.BlockSpec((1, 2, BLOCK), lambda b, plan: (b, 0, 0)),
                pl.BlockSpec((BLOCK, cols), lambda b, plan: (b, 0)),
            ],
            out_specs=pl.BlockSpec((expert_count, ROOM, cols), lambda b, plan: (0, 0, 0)),
            scratch_shapes=[pltpu.VMEM((LOCAL, cols), jnp.bfloat16)],
        ),
        out_shape=jax.ShapeDtypeStruct((expert_count, ROOM, cols), jnp.bfloat16),
        compiler_params=pltpu.CompilerParams(vmem_limit_bytes=VMEM),
        cost_estimate=cost(15),
        name="spread",
    )(plan, rows, source)


def gated_spread(own, other, rows, plan, chosen, router, expert_count, extra):
    blocks, cols = rows.shape[0], own.shape[1]
    both = cols + extra

    def kernel(
        plan_ref, rows_ref, own_ref, other_ref, chosen_ref, router_ref,
        out_ref, gate_ref, pair_ref, local,
    ):
        block = pl.program_id(0)
        source = jnp.where(block < blocks // 2, own_ref[...], other_ref[...])

        @pl.when(block == 0)
        def _():
            out_ref[...] = jnp.zeros_like(out_ref)

        logits = jnp.dot(source, router_ref[...], preferred_element_type=jnp.float32)
        lane = lax.broadcasted_iota(jnp.int32, logits.shape, 1)
        first, second = lane < expert_count, lane < 2 * expert_count
        expert = jnp.where(first, lane, lane - expert_count)
        top = jnp.max(jnp.where(first, logits, -jnp.inf), axis=-1, keepdims=True)
        raised = jnp.where(second, jnp.exp(logits - top), 0.0)
        gate = raised / jnp.sum(jnp.where(first, raised, 0.0), axis=-1, keepdims=True)
        named = (expert == chosen_ref[:, 0:1]) | (expert == chosen_ref[:, 1:2])
        mixing = jnp.where(named & second, gate, 0.0)
        high = mixing.astype(jnp.bfloat16).astype(jnp.float32)
        pair = jnp.where(first, high, mixing - high).astype(jnp.bfloat16)
        gate_ref[...] = gate
        pair_ref[...] = pair
        part = LOCAL // 3
        for i in range(3):
            slot = lax.broadcasted_iota(jnp.int32, (part, BLOCK), 0) + i * part
            hot = (slot == rows_ref[0, 0:1, :]) | (slot == rows_ref[0, 1:2, :])
            hot = jnp.where(hot, 1.0, 0.0).astype(jnp.bfloat16)
            for begin, end, value in ((0, cols, source), (cols, both, pair)):
                local[pl.ds(i * part, part), begin:end] = jnp.dot(
                    hot, value, preferred_element_type=jnp.float32
                ).astype(jnp.bfloat16)
        for e in range(expert_count):
            at = block * expert_count + e
            size = blocks * expert_count
            begin, goal = plan_ref[size + at], plan_ref[2 * size + at]

            def move(j, carry):
                here = pl.ds(pl.multiple_of((begin + j) * 16, 16), 16)
                there = pl.ds(pl.multiple_of((goal + j) * 16, 16), 16)
                out_ref[e, there, :] = local[here, :]
                return carry

            lax.fori_loop(0, plan_ref[at], move, 0)

    return pl.pallas_call(
        kernel,
        grid_spec=pltpu.PrefetchScalarGridSpec(
            num_scalar_prefetch=1,
            grid=(blocks,),
            in_specs=[
                pl.BlockSpec((1, 2, BLOCK), lambda b, plan: (b, 0, 0)),
                pl.BlockSpec((BLOCK, cols), lambda b, plan: (jnp.minimum(b, blocks // 2 - 1), 0)),
                pl.BlockSpec((BLOCK, cols), lambda b, plan: (jnp.maximum(b - blocks // 2, 0), 0)),
                pl.BlockSpec((BLOCK, 2), lambda b, plan: (b, 0)),
                pl.BlockSpec(router.shape, lambda b, plan: (0, 0)),
            ],
            out_specs=[
                pl.BlockSpec((expert_count, ROOM, both), lambda b, plan: (0, 0, 0)),
                pl.BlockSpec((BLOCK, extra), lambda b, plan: (b, 0)),
                pl.BlockSpec((BLOCK, extra), lambda b, plan: (b, 0)),
            ],
            scratch_shapes=[pltpu.VMEM((LOCAL, both), jnp.bfloat16)],
        ),
        out_shape=[
            jax.ShapeDtypeStruct((expert_count, ROOM, both), jnp.bfloat16),
            jax.ShapeDtypeStruct((blocks * BLOCK, extra), jnp.float32),
            jax.ShapeDtypeStruct((blocks * BLOCK, extra), jnp.bfloat16),
        ],
        compiler_params=pltpu.CompilerParams(vmem_limit_bytes=VMEM),
        cost_estimate=cost(20),
        name="gated_spread",
    )(plan, rows, own, other, chosen, router)


def collect(buffers, columns, plan, kept, after):
    each, room, cols = buffers[0].shape
    expert_count = each * len(buffers)
    blocks = columns.shape[0] // BLOCK
    extra = cols - kept

    def kernel(plan_ref, columns_ref, *refs):
        held, refs = refs[: len(buffers)], refs[len(buffers) + len(after) :]
        own_ref, other_ref, local = refs[0], refs[1], refs[-1]
        block = pl.program_id(0)
        mine = block < blocks // 2

        @pl.when(block == 0)
        def _():
            local[...] = jnp.zeros_like(local)

        for e in range(expert_count):
            at = block * expert_count + e
            size = blocks * expert_count
            begin, goal = plan_ref[size + at], plan_ref[2 * size + at]

            def move(j, carry):
                here = pl.ds(pl.multiple_of((begin + j) * 16, 16), 16)
                there = pl.ds(pl.multiple_of((goal + j) * 16, 16), 16)
                local[here, :] = held[e // each][e % each, there, :]
                return carry

            lax.fori_loop(0, plan_ref[at], move, 0)
        part = BLOCK // 2
        for i in range(2):
            rows = pl.ds(i * part, part)
            slot = lax.broadcasted_iota(jnp.int32, (part, LOCAL), 1)
            hot = (slot == columns_ref[rows, 0:1]) | (slot == columns_ref[rows, 1:2])
            total = jnp.dot(
                jnp.where(hot, 1.0, 0.0).astype(jnp.bfloat16),
                local[...],
                preferred_element_type=jnp.float32,
            )
            low = total[:, :kept].astype(jnp.bfloat16)

            @pl.when(mine)
            def _():
                own_ref[rows, :] = low

            @pl.when(jnp.logical_not(mine))
            def _():
                other_ref[rows, :] = low

            if extra:
                refs[2][rows, :] = total[:, kept:]

    out_specs = [
        pl.BlockSpec((BLOCK, kept), lambda b, plan: (jnp.minimum(b, blocks // 2 - 1), 0)),
        pl.BlockSpec((BLOCK, kept), lambda b, plan: (jnp.maximum(b - blocks // 2, 0), 0)),
    ]
    out_shape = [jax.ShapeDtypeStruct((blocks // 2 * BLOCK, kept), jnp.bfloat16)] * 2
    if extra:
        out_specs.append(pl.BlockSpec((BLOCK, extra), lambda b, plan: (b, 0)))
        out_shape.append(jax.ShapeDtypeStruct((blocks * BLOCK, extra), jnp.float32))
    return pl.pallas_call(
        kernel,
        grid_spec=pltpu.PrefetchScalarGridSpec(
            num_scalar_prefetch=1,
            grid=(blocks,),
            in_specs=[
                pl.BlockSpec((BLOCK, 2), lambda b, plan: (b, 0)),
            ]
            + [pl.BlockSpec((each, room, cols), lambda b, plan: (0, 0, 0))] * len(buffers)
            + [pl.BlockSpec(memory_space=pl.ANY)] * len(after),
            out_specs=out_specs,
            scratch_shapes=[pltpu.VMEM((LOCAL, cols), jnp.bfloat16)],
        ),
        out_shape=out_shape,
        compiler_params=pltpu.CompilerParams(vmem_limit_bytes=VMEM),
        cost_estimate=cost(16),
        name="collect",
    )(plan, columns, *buffers, *after)


GELU_A = 0.7978845608028654
GELU_B = 0.044715


def expert_pass(inputs, grads, up_weight, up_bias, down_weight, tiles, first, count, after):
    expert_count, room, cols = inputs.shape
    width, hidden = up_weight.shape[1:]

    def kernel(
        tiles_ref, x_ref, g_ref, up_ref, bias_ref, down_ref, *refs
    ):
        y_ref, dx_ref, dup_ref, ddown_ref, dbias_ref, mixed, dpre = refs[len(after) :]
        step = pl.program_id(0)
        expert = step + first

        @pl.when(step == 0)
        def _():
            mixed[...] = jnp.zeros_like(mixed)
            dpre[...] = jnp.zeros_like(dpre)

        dbias_ref[...] = jnp.zeros_like(dbias_ref)
        lane = lax.broadcasted_iota(jnp.int32, (TILE, cols - width), 1)

        def tile(r, carry):
            rows = pl.ds(pl.multiple_of(r * TILE, TILE), TILE)
            x = x_ref[0, rows, :width]
            g = g_ref[0, rows, :]
            gates = x_ref[0, rows, width:].astype(jnp.float32)
            own = (lane == expert) | (lane == expert + expert_count)
            mix = jnp.sum(jnp.where(own, gates, 0.0), axis=1, keepdims=True)
            pre = jnp.dot(x, up_ref[0], preferred_element_type=jnp.float32)
            pre = pre + bias_ref[0].astype(jnp.float32)
            back = lax.dot_general(
                g, down_ref[0], (((1,), (1,)), ((), ())), preferred_element_type=jnp.float32
            )
            square = pre * pre
            bend = jnp.tanh(pre * (GELU_A + GELU_A * GELU_B * square))
            upper = 0.5 + 0.5 * bend
            act = pre * upper
            slope = upper + 0.5 * pre * (1.0 - bend * bend) * (
                GELU_A + 3.0 * GELU_A * GELU_B * square
            )
            dot = jnp.sum(act * back, axis=1, keepdims=True)
            act_low = (mix * act).astype(jnp.bfloat16)
            down = (mix * back * slope).astype(jnp.bfloat16)
            mixed[rows, :] = act_low
            dpre[rows, :] = down
            dbias_ref[0] += jnp.sum(down.astype(jnp.float32), axis=0, keepdims=True)
            y_ref[0, rows, :] = jnp.dot(
                act_low, down_ref[0], preferred_element_type=jnp.float32
            ).astype(jnp.bfloat16)
            dx_ref[0, rows, :width] = lax.dot_general(
                down, up_ref[0], (((1,), (1,)), ((), ())), preferred_element_type=jnp.float32
            ).astype(jnp.bfloat16)
            high = dot.astype(jnp.bfloat16).astype(jnp.float32)
            dx_ref[0, rows, width:] = jnp.where(
                lane == expert, high, jnp.where(lane == expert + expert_count, dot - high, 0.0)
            ).astype(jnp.bfloat16)
            return carry

        lax.fori_loop(0, tiles_ref[expert], tile, 0)

        def weights(depth):
            rows = pl.ds(0, depth)
            for i in range(width // TILE):
                part = pl.ds(i * TILE, TILE)
                dup_ref[0, part, :] = lax.dot_general(
                    x_ref[0, rows, part], dpre[rows, :], (((0,), (0,)), ((), ())),
                    preferred_element_type=jnp.float32,
                ).astype(jnp.bfloat16)
                ddown_ref[0, part, :] = lax.dot_general(
                    g_ref[0, rows, part], mixed[rows, :], (((0,), (0,)), ((), ())),
                    preferred_element_type=jnp.float32,
                ).astype(jnp.bfloat16)

        pl.when(tiles_ref[expert] <= 3)(lambda: weights(3 * TILE))
        pl.when(tiles_ref[expert] > 3)(lambda: weights(room))

    def whole(*dims):
        return pl.BlockSpec((1, *dims), lambda e, tiles: (e + first, 0, 0))

    def own(*dims):
        return pl.BlockSpec((1, *dims), lambda e, tiles: (e, 0, 0))

    shapes = [
        ((room, width), jnp.bfloat16),
        ((room, cols), jnp.bfloat16),
        ((width, hidden), jnp.bfloat16),
        ((width, hidden), jnp.bfloat16),
        ((1, hidden), jnp.float32),
    ]
    return pl.pallas_call(
        kernel,
        grid_spec=pltpu.PrefetchScalarGridSpec(
            num_scalar_prefetch=1,
            grid=(count,),
            in_specs=[
                whole(room, cols),
                whole(room, width),
                whole(width, hidden),
                whole(1, hidden),
                whole(hidden, width),
            ]
            + [pl.BlockSpec(memory_space=pl.ANY)] * len(after),
            out_specs=[own(*dims) for dims, _ in shapes],
            scratch_shapes=[pltpu.VMEM((room, hidden), jnp.bfloat16)] * 2,
        ),
        out_shape=[jax.ShapeDtypeStruct((count, *dims), kind) for dims, kind in shapes],
        compiler_params=pltpu.CompilerParams(vmem_limit_bytes=VMEM),
        cost_estimate=pl.CostEstimate(
            flops=count * 12 * 768 * width * hidden,
            bytes_accessed=count * (4 * room * (cols + width) + 8 * width * hidden),
            transcendentals=count * 768 * hidden,
        ),
        name="experts",
    )(tiles, inputs, grads, up_weight, up_bias[:, None, :], down_weight, *after)


def call(kernel, name, grid, ins, outs, after=(), scratch=(), us=5, each=1, turn=None):
    turn = jnp.zeros((1,), jnp.int32) if turn is None else turn

    def spec(shape, split):
        zeros = (0,) * (len(shape) - 1)
        if split == "turned":
            return pl.BlockSpec((each, *shape[1:]), lambda i, t: ((i + t[0]) % grid, *zeros))
        if split == "low":
            return pl.BlockSpec(
                (each, *shape[1:]), lambda i, t: (jnp.minimum(i, grid // 2 - 1), *zeros)
            )
        if split == "high":
            return pl.BlockSpec(
                (each, *shape[1:]), lambda i, t: (jnp.maximum(i - grid // 2, 0), *zeros)
            )
        if split:
            return pl.BlockSpec((each, *shape[1:]), lambda i, t: (i, *zeros))
        return pl.BlockSpec(tuple(shape), lambda i, t: (0, *zeros))

    count, late = len(ins), len(after)

    def body(turn_ref, *refs):
        kernel(*refs[:count], *refs[count + late :])

    return pl.pallas_call(
        body,
        grid_spec=pltpu.PrefetchScalarGridSpec(
            num_scalar_prefetch=1,
            grid=(grid,),
            in_specs=[spec(a.shape, split) for a, split in ins]
            + [pl.BlockSpec(memory_space=pl.ANY)] * late,
            out_specs=[spec(a.shape, split) for a, split in outs],
            scratch_shapes=list(scratch),
        ),
        out_shape=[a for a, _ in outs],
        compiler_params=pltpu.CompilerParams(vmem_limit_bytes=VMEM),
        cost_estimate=cost(us),
        name=name,
    )(turn, *[a for a, _ in ins], *after)


def shape_of(dims, kind):
    return jax.ShapeDtypeStruct(tuple(dims), kind)


def normal(x):
    centered = x - jnp.mean(x, axis=-1, keepdims=True)
    spread_of = lax.rsqrt(jnp.mean(centered * centered, axis=-1, keepdims=True) + EPSILON)
    return centered * spread_of, spread_of


def contract(left, right, left_dim, right_dim):
    return lax.dot_general(
        left, right, (((left_dim,), (right_dim,)), ((), ())), preferred_element_type=jnp.float32
    )


def head_masks(width):
    lane = lax.broadcasted_iota(jnp.int32, (1, width), 1)
    return [(lane >= h * HD) & (lane < (h + 1) * HD) for h in range(width // HD)]


def head_probs(q, k, mask):
    own = jnp.where(mask, q, jnp.zeros_like(q)) * jnp.bfloat16(HD ** (-0.5))
    scores = contract(own, k, 1, 1)
    column = lax.broadcasted_iota(jnp.int32, scores.shape, 1)
    scores = jnp.where(column < SEQ, scores, -1e30)
    raised = jnp.exp(scores - jnp.max(scores, axis=-1, keepdims=True))
    return raised * (1.0 / jnp.sum(raised, axis=-1, keepdims=True))


def attention_forward(x, turn, gain, shift, weight, bias, out_weight):
    images, seq, width = x.shape
    rows, inner = ROWS, weight.shape[2]
    blocks = images // PAIR

    def kernel(
        turn_ref, x_ref, gain_ref, shift_ref, w_ref, b_ref, wo_ref,
        *refs
    ):
        own_ref, other_ref, pad_ref, n_ref, q_ref, k_ref, v_ref, o_ref, held = refs
        held[...] = jnp.zeros_like(held)
        for i in range(PAIR):
            held[i, :seq, :] = x_ref[i].astype(jnp.float32)
        value = held[...].reshape(PAIR * rows, width)
        pad_ref[...] = value.astype(jnp.bfloat16).reshape(PAIR, rows, width)
        n = (normal(value)[0] * gain_ref[...] + shift_ref[...]).astype(jnp.bfloat16)
        n_ref[...] = n.reshape(PAIR, rows, width)
        for j, ref in enumerate((q_ref, k_ref, v_ref)):
            made = jnp.dot(n, w_ref[j], preferred_element_type=jnp.float32) + b_ref[j : j + 1, :]
            ref[...] = made.astype(jnp.bfloat16).reshape(PAIR, rows, inner)
        for i in range(PAIR):
            q, k, v = q_ref[i], k_ref[i], v_ref[i]
            mixed = jnp.zeros((rows, inner), jnp.float32)
            for mask in head_masks(inner):
                probs = head_probs(q, k, mask).astype(jnp.bfloat16)
                head = jnp.dot(probs, v, preferred_element_type=jnp.float32)
                mixed = jnp.where(mask, head, mixed)
            o_ref[i] = mixed.astype(jnp.bfloat16)
        mixed = o_ref[...].reshape(PAIR * rows, inner)
        part = jnp.dot(mixed, wo_ref[...], preferred_element_type=jnp.float32)
        part = part.astype(jnp.bfloat16).reshape(PAIR, rows, width)

        @pl.when(pl.program_id(0) < blocks // 2)
        def _():
            other_ref[...] = part

        @pl.when(pl.program_id(0) >= blocks // 2)
        def _():
            own_ref[...] = part


    wide = shape_of((images, rows, width), jnp.bfloat16)
    slim = shape_of((images, rows, inner), jnp.bfloat16)
    def place(i, turn):
        return ((i + blocks // 2) % blocks, 0, 0)

    def whole(array):
        return pl.BlockSpec(array.shape, lambda i, turn: (0,) * array.ndim)

    small = (gain, shift, weight, bias, out_weight)
    return pl.pallas_call(
        kernel,
        grid_spec=pltpu.PrefetchScalarGridSpec(
            num_scalar_prefetch=1,
            grid=(blocks,),
            in_specs=[
                pl.BlockSpec(
                    (PAIR, seq, width), lambda i, turn: ((i + blocks // 2 + turn[0]) % blocks, 0, 0)
                )
            ]
            + [whole(array) for array in small],
            out_specs=[
                pl.BlockSpec(
                    (PAIR, rows, width), lambda i, turn: (jnp.maximum(i - blocks // 2, 0), 0, 0)
                ),
                pl.BlockSpec(
                    (PAIR, rows, width), lambda i, turn: (jnp.minimum(i, blocks // 2 - 1), 0, 0)
                ),
            ]
            + [pl.BlockSpec((PAIR, *a.shape[1:]), place) for a in [wide] * 2 + [slim] * 4],
            scratch_shapes=[pltpu.VMEM((PAIR, rows, width), jnp.float32)],
        ),
        out_shape=[shape_of((images // 2, rows, width), jnp.bfloat16)] * 2 + [wide] * 2 + [slim] * 4,
        compiler_params=pltpu.CompilerParams(vmem_limit_bytes=VMEM),
        cost_estimate=cost(18),
        name="attention_forward",
    )(turn, x, *small)


def attention_backward(own_da, other_da, x, n, q, k, v, o, weight, out_weight, after):
    images, rows, width = x.shape
    inner = weight.shape[2]

    def kernel(
        own_ref, other_ref, x_ref, n_ref, q_ref, k_ref, v_ref, o_ref, w_ref, wo_ref,
        own_back_ref, other_back_ref, dw_ref, dwo_ref, dbias_ref, sums_ref, held,
    ):
        @pl.when(pl.program_id(0) == 0)
        def _():
            dw_ref[...] = jnp.zeros_like(dw_ref)
            dwo_ref[...] = jnp.zeros_like(dwo_ref)
            dbias_ref[...] = jnp.zeros_like(dbias_ref)
            sums_ref[...] = jnp.zeros_like(sums_ref)

        joined = PAIR * rows
        mine = pl.program_id(0) < images // PAIR // 2
        da = jnp.where(mine, own_ref[...], other_ref[...]).reshape(joined, width)
        do_all = contract(da, wo_ref[...], 1, 1).astype(jnp.bfloat16).reshape(PAIR, rows, inner)
        scale = HD ** (-0.5)
        for i in range(PAIR):
            q, k, v, do = q_ref[i], k_ref[i], v_ref[i], do_all[i]
            dq = dk = dv = jnp.zeros((rows, inner), jnp.float32)
            for mask in head_masks(inner):
                probs = head_probs(q, k, mask)
                dv = jnp.where(mask, contract(probs.astype(jnp.bfloat16), do, 0, 0), dv)
                dp = contract(jnp.where(mask, do, jnp.zeros_like(do)), v, 1, 1)
                ds = probs * (dp - jnp.sum(probs * dp, axis=-1, keepdims=True))
                ds = ds.astype(jnp.bfloat16)
                dq = jnp.where(mask, jnp.dot(ds, k, preferred_element_type=jnp.float32), dq)
                dk = jnp.where(mask, contract(ds, q, 0, 0), dk)
            held[0, i] = (dq * scale).astype(jnp.bfloat16)
            held[1, i] = (dk * scale).astype(jnp.bfloat16)
            held[2, i] = dv.astype(jnp.bfloat16)
        n = n_ref[...].reshape(joined, width)
        back = jnp.zeros((joined, width), jnp.float32)
        for j in range(3):
            grad = held[j].reshape(joined, inner)
            dw_ref[j] += contract(n, grad, 0, 0)
            back += contract(grad, w_ref[j], 1, 1)
            if j != 1:
                dbias_ref[j // 2 : j // 2 + 1, :] += jnp.sum(
                    grad.astype(jnp.float32), axis=0, keepdims=True
                )
        dwo_ref[0] += contract(da, o_ref[...].reshape(joined, inner), 0, 0)
        back_low = back.astype(jnp.bfloat16).reshape(PAIR, rows, width)

        @pl.when(mine)
        def _():
            own_back_ref[...] = back_low

        @pl.when(jnp.logical_not(mine))
        def _():
            other_back_ref[...] = back_low

        unit, _ = normal(x_ref[...].reshape(joined, width).astype(jnp.float32))
        sums_ref[0:1, :] += jnp.sum(back * unit, axis=0, keepdims=True)
        sums_ref[1:2, :] += jnp.sum(back, axis=0, keepdims=True)
        sums_ref[2:3, :] += jnp.sum(da.astype(jnp.float32), axis=0, keepdims=True)

    return call(
        kernel, "attention_backward", images // PAIR,
        [(own_da, "low"), (other_da, "high")]
        + [(a, True) for a in (x, n, q, k, v, o)] + [(weight, False), (out_weight, False)],
        [
            (shape_of((images // 2, rows, width), jnp.bfloat16), "low"),
            (shape_of((images // 2, rows, width), jnp.bfloat16), "high"),
            (shape_of((3, width, inner), jnp.float32), False),
            (shape_of((1, width, inner), jnp.float32), False),
            (shape_of((2, inner), jnp.float32), False),
            (shape_of((3, width), jnp.float32), False),
        ],
        after=after, each=PAIR, us=30,
        scratch=[pltpu.VMEM((3, PAIR, rows, inner), jnp.bfloat16)],
    )


def middle_norm(near, far, x, out_bias, gain, shift, after):
    def kernel(near_ref, far_ref, x_ref, bias_ref, gain_ref, shift_ref, middle_ref, n_ref):
        total = near_ref[0].astype(jnp.float32) + far_ref[0].astype(jnp.float32)
        middle = x_ref[0].astype(jnp.float32) + total + bias_ref[...]
        middle_ref[0] = middle
        n_ref[0] = (normal(middle)[0] * gain_ref[...] + shift_ref[...]).astype(jnp.bfloat16)

    return call(
        kernel, "middle_norm", near.shape[0],
        [(near, True), (far, True), (x, True), (out_bias, False), (gain, False), (shift, False)],
        [(shape_of(near.shape, jnp.float32), True), (shape_of(near.shape, jnp.bfloat16), True)],
        after=after, us=8,
    )


def norm_back(dn, unit, spread_of, gain):
    dz = dn * gain
    mean = jnp.mean(dz, axis=-1, keepdims=True)
    return spread_of * (dz - mean - unit * jnp.mean(dz * unit, axis=-1, keepdims=True))


def middle_back(near, far, dots, gates, chosen, pair, n, router_weight, down_bias, middle, upstream, gain, after):
    count, wide = down_bias.shape[0], pair.shape[2]

    def kernel(
        near_ref, far_ref, dots_ref, gates_ref, chosen_ref, pair_ref, n_ref, router_ref, bias_ref,
        middle_ref, g_ref, gain_ref, grad_ref, da_ref, sums_ref, drouter_ref, dbias_ref,
    ):
        @pl.when(pl.program_id(0) == 0)
        def _():
            sums_ref[...] = jnp.zeros_like(sums_ref)
            drouter_ref[...] = jnp.zeros_like(drouter_ref)
            dbias_ref[...] = jnp.zeros_like(dbias_ref)

        g = g_ref[0]
        lane = lax.broadcasted_iota(jnp.int32, (g.shape[0], count), 1)
        named = (lane == chosen_ref[0, :, 0:1]) | (lane == chosen_ref[0, :, 1:2])
        dmix = dots_ref[0] + jnp.where(named, contract(g, bias_ref[...], 1, 1), 0.0)
        gate = gates_ref[0, :, :count]
        dlogits = gate * (dmix - jnp.sum(gate * dmix, axis=-1, keepdims=True))
        dlogits = dlogits.astype(jnp.bfloat16)
        drouter_ref[...] += contract(dlogits, n_ref[0], 0, 0)
        dbias_ref[...] += contract(pair_ref[0], g, 0, 0)
        dn = near_ref[0].astype(jnp.float32) + far_ref[0].astype(jnp.float32)
        dn = dn + contract(dlogits, router_ref[...], 1, 1)
        unit, spread_of = normal(middle_ref[0])
        grad = g.astype(jnp.float32) + norm_back(dn, unit, spread_of, gain_ref[...])
        grad_ref[0] = grad
        da_ref[0] = grad.astype(jnp.bfloat16)
        sums_ref[0:1, :] += jnp.sum(dn * unit, axis=0, keepdims=True)
        sums_ref[1:2, :] += jnp.sum(dn, axis=0, keepdims=True)

    width = middle.shape[2]
    return call(
        kernel, "middle_back", middle.shape[0],
        [(a, True) for a in (near, far, dots, gates, chosen, pair, n)]
        + [(router_weight, False), (down_bias, False), (middle, True), (upstream, True), (gain, False)],
        [
            (shape_of(middle.shape, jnp.float32), True),
            (shape_of(middle.shape, jnp.bfloat16), True),
            (shape_of((2, width), jnp.float32), False),
            (shape_of((count, width), jnp.float32), False),
            (shape_of((wide, width), jnp.float32), False),
        ],
        after=after, us=8,
    )


def finish(near, far, middle, pair, down_bias, after):
    def kernel(near_ref, far_ref, middle_ref, pair_ref, bias_ref, out_ref):
        total = near_ref[0].astype(jnp.float32) + far_ref[0].astype(jnp.float32)
        total = total + jnp.dot(pair_ref[0], bias_ref[...], preferred_element_type=jnp.float32)
        out_ref[0] = (middle_ref[0] + total).astype(jnp.bfloat16)

    return call(
        kernel, "finish", middle.shape[0],
        [(near, True), (far, True), (middle, True), (pair, True), (down_bias, False)],
        [(shape_of(middle.shape, jnp.bfloat16), True)],
        after=after, us=8,
    )[0]


def input_back(own, other, x, own_grad, other_grad, gain, turn, after):
    images, _, width = x.shape
    half = images // 2

    def kernel(turn_ref, own_ref, other_ref, x_ref, own_grad_ref, other_grad_ref, gain_ref, *refs):
        out_ref = refs[-1]
        step = pl.program_id(0)
        place = (step + turn_ref[0]) % images
        mine = step < half
        dn = jnp.where(mine, own_ref[0], other_ref[0]).astype(jnp.float32)
        unit, spread_of = normal(x_ref[0].astype(jnp.float32))
        grad = jnp.where(mine, own_grad_ref[0], other_grad_ref[0])
        grad = grad + norm_back(dn, unit, spread_of, gain_ref[...])
        for j in range(images):

            @pl.when(place == j)
            def _():
                out_ref[j * SEQ : (j + 1) * SEQ, :] = grad[:SEQ]

    def low(shape):
        return pl.BlockSpec((1, *shape[1:]), lambda i, t: (jnp.minimum(i, half - 1), 0, 0))

    def high(shape):
        return pl.BlockSpec((1, *shape[1:]), lambda i, t: (jnp.maximum(i - half, 0), 0, 0))

    return pl.pallas_call(
        kernel,
        grid_spec=pltpu.PrefetchScalarGridSpec(
            num_scalar_prefetch=1,
            grid=(images,),
            in_specs=[
                low(own.shape),
                high(other.shape),
                pl.BlockSpec((1, *x.shape[1:]), lambda i, t: (i, 0, 0)),
                low(own_grad.shape),
                high(other_grad.shape),
                pl.BlockSpec(gain.shape, lambda i, t: (0, 0)),
            ]
            + [pl.BlockSpec(memory_space=pl.ANY)] * len(after),
            out_specs=pl.BlockSpec((images * SEQ, width), lambda i, t: (0, 0)),
        ),
        out_shape=jax.ShapeDtypeStruct((images * SEQ, width), jnp.float32),
        compiler_params=pltpu.CompilerParams(vmem_limit_bytes=VMEM),
        cost_estimate=cost(15),
        name="input_back",
    )(turn, own, other, x, own_grad, other_grad, gain, *after)


def to_core(value):
    return lax.ppermute(value, "tensor", pairs(lax.axis_size("tensor"), 1))


def across(value):
    return lax.ppermute(value, "tensor", pairs(lax.axis_size("tensor"), 2))


def core_sum(own, other, zero):
    got = to_core(other)
    return (own.astype(jnp.float32) + got.astype(jnp.float32) + zero).astype(jnp.bfloat16)


def zero_of(value):
    return value[(0,) * value.ndim].astype(jnp.float32) * 0.0


def ring_owner(way, step):
    index = lax.axis_index("dp")
    place = jnp.where(index % 2 == 0, index // 2, 7 - index // 2)
    place = (place - way * (step + 1)) % 8
    return jnp.where(place < 4, 2 * place, 15 - 2 * place).astype(jnp.int32)


def ring_hop(value, way):
    path = [(RING[i], RING[(i + way) % len(RING)]) for i in range(len(RING))]
    return lax.ppermute(value, "dp", path)


def ring_add(got, sources, steps, kinds, after, carry=()):
    groups, came = len(sources), got[0].shape[0]
    many, total, cols = sources[0][0].shape
    rows, part = total // 8, 2
    owners = jnp.stack([ring_owner(way, step) for step in steps for way in (1, -1)])
    joint = all(kind == kinds[0] for kind in kinds)

    def kernel(owners_ref, *refs):
        held, locals_ = refs[:2], refs[2 : 2 + 2 * groups]
        outs = refs[2 + 2 * groups + len(after) + len(carry) :]
        for g in range(groups):
            for d in range(2):
                value = locals_[2 * g + d][...]
                if g < came:
                    value = value.astype(jnp.float32) + held[d][g].astype(jnp.float32)
                if joint:
                    outs[d][g] = value.astype(kinds[g])
                else:
                    outs[2 * g + d][0] = value.astype(kinds[g])

    def source(slot):
        return pl.BlockSpec((part, rows, cols), lambda i, own: (i, own[slot], 0))

    def stack(count):
        return pl.BlockSpec((count, part, rows, cols), lambda i, own: (0, i, 0, 0))

    if joint:
        outs = [((groups, many, rows, cols), kinds[0])] * 2
    else:
        outs = [((1, many, rows, cols), kind) for kind in kinds for _ in range(2)]
    return pl.pallas_call(
        kernel,
        grid_spec=pltpu.PrefetchScalarGridSpec(
            num_scalar_prefetch=1,
            grid=(many // part,),
            in_specs=[stack(came)] * 2
            + [source(i) for i in range(2 * groups)]
            + [pl.BlockSpec(memory_space=pl.ANY)] * (len(after) + len(carry)),
            out_specs=[stack(dims[0]) for dims, _ in outs]
            + [pl.BlockSpec(memory_space=pl.ANY)] * len(carry),
        ),
        out_shape=[jax.ShapeDtypeStruct(dims, kind) for dims, kind in outs]
        + [jax.ShapeDtypeStruct(value.shape, value.dtype) for value in carry],
        input_output_aliases={
            3 + 2 * groups + len(after) + i: len(outs) + i for i in range(len(carry))
        },
        compiler_params=pltpu.CompilerParams(vmem_limit_bytes=VMEM),
        cost_estimate=cost(5),
        name="ring_add",
    )(owners, *got, *[piece for pair in sources for piece in pair], *after, *carry)


def on_device(
    embedded,
    attn_gain,
    attn_shift,
    qkv_weight,
    qv_bias,
    out_weight,
    out_bias,
    moe_gain,
    moe_shift,
    router_weight,
    up_weight,
    up_bias,
    down_weight,
    down_bias,
    routes,
    cotangent,
):
    tok_rows, width = embedded.shape
    images = tok_rows // SEQ
    half = images // 2
    head_width = qkv_weight.shape[2]
    expert_count = up_weight.shape[0]
    core = lax.axis_index("tensor") % 2
    f32 = jnp.float32

    def own_first(value, fill):
        value = value.reshape(images, SEQ, value.shape[1])
        value = jnp.pad(value, ((0, 0), (0, ROWS - SEQ), (0, 0)), constant_values=fill)
        return jnp.where(core == 0, value, jnp.roll(value, half, axis=0))

    def in_order(own, other):
        low = jnp.where(core == 0, own, other)
        high = jnp.where(core == 0, other, own)
        return jnp.concatenate([low, high])[:, :SEQ].reshape(tok_rows, width)

    def row(value):
        return value.astype(f32)[None]

    def imaged(value):
        return value.reshape(-1, ROWS, value.shape[1])

    turn = (half * core).astype(jnp.int32)[None]
    bias_rows = jnp.stack([qv_bias[0], jnp.zeros_like(qv_bias[0]), qv_bias[1]]).astype(f32)
    images_in = embedded.reshape(images, SEQ, width)
    own, other, x, normed, queries, keys, values, mixed = attention_forward(
        images_in, turn // PAIR, row(attn_gain), row(attn_shift), qkv_weight, bias_rows, out_weight
    )
    near = core_sum(own, other, 0.0)
    far = across(near)

    near_zero = zero_of(near)
    chosen = own_first(routes + near_zero.astype(jnp.int32), -1).reshape(images * ROWS, 2)
    rows, columns, plan, tiles = route_plan(chosen, expert_count)
    upstream = own_first(cotangent, 0) + near_zero.astype(jnp.bfloat16)
    grad_buffers = spread(upstream.reshape(images * ROWS, width), rows, plan, expert_count)

    extra = 128
    router_twice = jnp.pad(
        jnp.concatenate([router_weight, router_weight], axis=1),
        ((0, 0), (0, extra - 2 * expert_count)),
    )
    bias_twice = jnp.pad(
        jnp.concatenate([down_bias, down_bias]), ((0, extra - 2 * expert_count), (0, 0))
    )
    middle, own_normed = middle_norm(
        near, far, x, row(out_bias), row(moe_gain), row(moe_shift),
        (grad_buffers, router_twice, bias_twice, tiles),
    )
    own_rows = half * ROWS
    buffers, gates, mix_pair = gated_spread(
        own_normed.reshape(own_rows, width), to_core(own_normed).reshape(own_rows, width),
        rows, plan, chosen, router_twice, expert_count, extra,
    )
    gates, mix_pair, chosen = imaged(gates), imaged(mix_pair), imaged(chosen)
    group = expert_count // GROUPS

    def experts_of(i, after):
        return expert_pass(
            buffers, grad_buffers, up_weight, up_bias, down_weight, tiles, i * group, group, after
        )

    ringed = lax.axis_size("dp") == len(RING)
    low = jnp.bfloat16
    y_first, back_first, *first, bias_first = experts_of(0, ())
    moving = ()
    if ringed:
        rows_each = width // 8
        moving = [
            lax.dynamic_slice_in_dim(grad, ring_owner(way, 0) * rows_each, rows_each, 1)[None]
            for grad, way in zip(first, (1, -1))
        ]
    y_second, back_second, *second, bias_second = experts_of(1, tuple(moving))

    def round_trip(step, kinds, after=(), carry=()):
        if not ringed:
            return carry
        got = [ring_hop(value, way) for value, way in zip(moving, (1, -1))]
        if step < 8:
            return ring_add(got, [first, second], [step, step - 1], kinds, after, carry)
        return ring_add(got, [second], [step - 1], kinds, after, carry)

    moving = round_trip(1, [low, low])
    own, other, dots = collect((back_first, back_second), columns, plan, width, tuple(moving))
    sent = to_core(imaged(other))
    *moving, own = round_trip(2, [low, low], (), (own,))
    back_near = (imaged(own).astype(f32) + sent.astype(f32)).astype(low)
    back_far = across(back_near)
    dots = dots[:, : 2 * expert_count].T + zero_of(back_near)
    dots = dots[:expert_count] + dots[expert_count:]
    dots = dots[:, :own_rows] + to_core(dots[:, own_rows:])
    dots = (dots + across(dots)).T.reshape(half, ROWS, expert_count)
    own_y, other_y = collect((y_first, y_second), columns, plan, width, (back_near, *moving))
    moving = round_trip(3, [low, low], (other_y,))
    middle_grad, own_da, moe_sums, router_sums, bias_sums = middle_back(
        back_near, back_far, dots, gates, chosen, mix_pair, own_normed, router_weight,
        down_bias, middle, upstream, row(moe_gain), tuple(moving),
    )
    *moving, own_da = round_trip(4, [low, low], (), (own_da,))
    other_da, other_grad = to_core(own_da), to_core(middle_grad)
    y_near = core_sum(imaged(own_y), imaged(other_y), zero_of(own_da))
    y_far = across(y_near)
    own, other, grad_qkv, grad_out, grad_qv_bias, sums = attention_backward(
        own_da, other_da, x, normed, queries, keys, values, mixed, qkv_weight, out_weight,
        (y_near, *moving),
    )
    *moving, own, other = round_trip(5, [low, low], (y_far,), (own, other))
    last_near = core_sum(own, other, 0.0)
    last_far = across(last_near)

    def after_round(value):
        return value + zero_of(moving[1]).astype(value.dtype) if ringed else value

    def meet(value, axis, bit):
        return value + lax.ppermute(value, axis, pairs(lax.axis_size(axis), bit))

    def halve(values, bit, axis):
        mine = (lax.axis_index("dp") >> bit) % 2
        keep = lax.dynamic_index_in_dim(values, mine, axis, keepdims=True)
        give = lax.dynamic_index_in_dim(values, 1 - mine, axis, keepdims=True).astype(low)
        return keep, lax.ppermute(give, "dp", pairs(8, 1 << bit))

    def output():
        own_out = finish(y_near, y_far, middle, mix_pair, bias_twice, tuple(moving))
        return in_order(own_out, to_core(own_out))

    router_bias = [router_sums, bias_sums[:expert_count] + bias_sums[expert_count : 2 * expert_count]]
    packed = jnp.concatenate(
        [
            sums[:2],
            0.5 * moe_sums,
            *[0.5 * part for part in router_bias],
            sums[2:],
            jnp.pad(grad_qv_bias, ((0, 0), (0, width - head_width))),
            bias_first[:, 0],
            bias_second[:, 0],
        ]
    )
    slim = jnp.concatenate([grad_qkv, grad_out])
    base = 4 + 2 * expert_count
    last = (last_near.astype(f32) + last_far.astype(f32)).astype(low)
    other_last = to_core(last)

    def input_grad():
        return input_back(
            last, other_last, x, middle_grad, other_grad, row(attn_gain), turn, tuple(moving)
        )

    if ringed:
        slim = slim.reshape(4, 2, 2, 2, width // 8, head_width)
        packed = after_round(packed)
        for step, bit, axis in ((6, 0, 3), (7, 1, 2), (8, 2, 1)):
            keep, got = halve(after_round(slim), bit, axis)
            sent = lax.ppermute(packed, "dp", pairs(8, 1 << bit))
            if step == 6:
                moving = round_trip(6, [low, low], (last_near, sent, got))
                layer_out = output()
            elif step == 7:
                up_first, down_first, *moving = round_trip(7, [f32, low], (layer_out, sent, got))
                grad_embedded = input_grad()
            else:
                moving = round_trip(8, [f32], (grad_embedded, sent, got))
            slim = keep.astype(f32) + got.astype(f32) + zero_of(moving[0])
            packed = after_round(packed + sent)
        up_second, down_second = moving
        slim = slim.reshape(4, width // 8, head_width)
    else:
        layer_out = output()
        grad_embedded = input_grad()
        packed = lax.psum(packed, "dp")
        slim = lax.psum_scatter(slim, "dp", scatter_dimension=1, tiled=True)
        up_first, down_first, up_second, down_second = [
            lax.psum_scatter(grad, "dp", scatter_dimension=1, tiled=True).astype(f32)[None]
            for grad in (*first, *second)
        ]
    grad_up = jnp.concatenate([up_first[0], up_second[0]])
    grad_down = jnp.concatenate([down_first[0], down_second[0]]).transpose(0, 2, 1)
    tensor_parts = meet(meet(packed[:base], "tensor", 1), "tensor", 2)
    packed = jnp.concatenate([tensor_parts, packed[base:]])
    return (
        layer_out,
        grad_embedded,
        packed[0],
        packed[1],
        slim[:3],
        packed[base + 1 : base + 3, :head_width],
        slim[3].T,
        packed[base],
        packed[2],
        packed[3],
        packed[4 : 4 + expert_count].T,
        grad_up,
        packed[base + 3 :],
        grad_down,
        packed[4 + expert_count : base],
    )


def solution(mesh):
    return jax.shard_map(
        on_device,
        mesh=mesh,
        in_specs=(
            P("dp", None),
            P(),
            P(),
            P(None, None, "tensor"),
            P(None, "tensor"),
            P("tensor", None),
            P(),
            P(),
            P(),
            P(),
            P(None, None, "tensor"),
            P(None, "tensor"),
            P(None, "tensor", None),
            P(),
            P("dp", None),
            P("dp", None),
        ),
        out_specs=(
            P("dp", None),
            P("dp", None),
            P(),
            P(),
            P(None, "dp", "tensor"),
            P(None, "tensor"),
            P("tensor", "dp"),
            P(),
            P(),
            P(),
            P(),
            P(None, "dp", "tensor"),
            P(None, "tensor"),
            P(None, "tensor", "dp"),
            P(),
        ),
        check_vma=False,
    )
```

```python
import jax
import jax.numpy as jnp
from jax import lax
from jax.experimental import pallas as pl
from jax.experimental.pallas import tpu as pltpu
from jax.sharding import PartitionSpec as P

SEQ = 197
HD = 64
EPSILON = 1e-06
RING = (0, 2, 4, 6, 7, 5, 3, 1)


def pairs(count, bit):
    return [(i, i ^ bit) for i in range(count)]


ROWS = 208
PAIR = 2
BLOCK = 416
GROUPS = 2
LOCAL = 960
ROOM = 1024
TILE = 256
VMEM = 56 * 1024 * 1024


def cost(us):
    return pl.CostEstimate(flops=int(us * 1.1e9), bytes_accessed=0, transcendentals=0)


def route_plan(routes, expert_count):
    tokens = routes.shape[0]
    blocks = -(-tokens // BLOCK)
    padded = jnp.pad(routes.T, ((0, 0), (0, blocks * BLOCK - tokens)), constant_values=-1)
    experts = jnp.arange(expert_count, dtype=jnp.int32)[:, None]
    first = padded[0][None, :] == experts
    second = padded[1][None, :] == experts
    named = (first | second).reshape(expert_count * blocks, BLOCK)
    ahead = jnp.arange(BLOCK)[:, None] < jnp.arange(BLOCK)[None, :]
    rank = jnp.dot(
        named.astype(jnp.bfloat16), ahead.astype(jnp.bfloat16), preferred_element_type=jnp.float32
    )
    rank = rank.astype(jnp.int32).reshape(expert_count, blocks, BLOCK)
    chunks = (jnp.sum(named.astype(jnp.int32), axis=1).reshape(expert_count, blocks) + 15) // 16
    inside = jnp.cumsum(chunks, axis=0) - chunks
    offset = jnp.cumsum(chunks, axis=1) - chunks
    place = (rank + 16 * inside[:, :, None]).reshape(expert_count, blocks * BLOCK)
    target = jnp.stack(
        [jnp.sum(jnp.where(hot, place + 1, 0), axis=0) - 1 for hot in (first, second)]
    )
    tiles = (jnp.sum(chunks, axis=1) * 16 + TILE - 1) // TILE
    plan = jnp.concatenate([chunks.T.reshape(-1), inside.T.reshape(-1), offset.T.reshape(-1)])
    rows = target.reshape(2, blocks, BLOCK).transpose(1, 0, 2)
    return rows, target.T, plan, tiles


def spread(source, rows, plan, expert_count):
    blocks, cols = rows.shape[0], source.shape[1]

    def kernel(plan_ref, rows_ref, source_ref, out_ref, local):
        block = pl.program_id(0)

        @pl.when(block == 0)
        def _():
            out_ref[...] = jnp.zeros_like(out_ref)

        part = LOCAL // 3
        for i in range(3):
            slot = lax.broadcasted_iota(jnp.int32, (part, BLOCK), 0) + i * part
            hot = (slot == rows_ref[0, 0:1, :]) | (slot == rows_ref[0, 1:2, :])
            local[pl.ds(i * part, part), :] = jnp.dot(
                jnp.where(hot, 1.0, 0.0).astype(jnp.bfloat16),
                source_ref[...],
                preferred_element_type=jnp.float32,
            ).astype(jnp.bfloat16)
        for e in range(expert_count):
            at = block * expert_count + e
            size = blocks * expert_count
            begin, goal = plan_ref[size + at], plan_ref[2 * size + at]

            def move(j, carry):
                here = pl.ds(pl.multiple_of((begin + j) * 16, 16), 16)
                there = pl.ds(pl.multiple_of((goal + j) * 16, 16), 16)
                out_ref[e, there, :] = local[here, :]
                return carry

            lax.fori_loop(0, plan_ref[at], move, 0)

    return pl.pallas_call(
        kernel,
        grid_spec=pltpu.PrefetchScalarGridSpec(
            num_scalar_prefetch=1,
            grid=(blocks,),
            in_specs=[
                pl.BlockSpec((1, 2, BLOCK), lambda b, plan: (b, 0, 0)),
                pl.BlockSpec((BLOCK, cols), lambda b, plan: (b, 0)),
            ],
            out_specs=pl.BlockSpec((expert_count, ROOM, cols), lambda b, plan: (0, 0, 0)),
            scratch_shapes=[pltpu.VMEM((LOCAL, cols), jnp.bfloat16)],
        ),
        out_shape=jax.ShapeDtypeStruct((expert_count, ROOM, cols), jnp.bfloat16),
        compiler_params=pltpu.CompilerParams(vmem_limit_bytes=VMEM),
        cost_estimate=cost(15),
        name="spread",
    )(plan, rows, source)


def gated_spread(own, other, rows, plan, chosen, router, expert_count, extra):
    blocks, cols = rows.shape[0], own.shape[1]
    both = cols + extra

    def kernel(
        plan_ref, rows_ref, own_ref, other_ref, chosen_ref, router_ref,
        out_ref, gate_ref, pair_ref, local,
    ):
        block = pl.program_id(0)
        source = jnp.where(block < blocks // 2, own_ref[...], other_ref[...])

        @pl.when(block == 0)
        def _():
            out_ref[...] = jnp.zeros_like(out_ref)

        logits = jnp.dot(source, router_ref[...], preferred_element_type=jnp.float32)
        lane = lax.broadcasted_iota(jnp.int32, logits.shape, 1)
        first, second = lane < expert_count, lane < 2 * expert_count
        expert = jnp.where(first, lane, lane - expert_count)
        top = jnp.max(jnp.where(first, logits, -jnp.inf), axis=-1, keepdims=True)
        raised = jnp.where(second, jnp.exp(logits - top), 0.0)
        gate = raised / jnp.sum(jnp.where(first, raised, 0.0), axis=-1, keepdims=True)
        named = (expert == chosen_ref[:, 0:1]) | (expert == chosen_ref[:, 1:2])
        mixing = jnp.where(named & second, gate, 0.0)
        high = mixing.astype(jnp.bfloat16).astype(jnp.float32)
        pair = jnp.where(first, high, mixing - high).astype(jnp.bfloat16)
        gate_ref[...] = gate
        pair_ref[...] = pair
        part = LOCAL // 3
        for i in range(3):
            slot = lax.broadcasted_iota(jnp.int32, (part, BLOCK), 0) + i * part
            hot = (slot == rows_ref[0, 0:1, :]) | (slot == rows_ref[0, 1:2, :])
            hot = jnp.where(hot, 1.0, 0.0).astype(jnp.bfloat16)
            for begin, end, value in ((0, cols, source), (cols, both, pair)):
                local[pl.ds(i * part, part), begin:end] = jnp.dot(
                    hot, value, preferred_element_type=jnp.float32
                ).astype(jnp.bfloat16)
        for e in range(expert_count):
            at = block * expert_count + e
            size = blocks * expert_count
            begin, goal = plan_ref[size + at], plan_ref[2 * size + at]

            def move(j, carry):
                here = pl.ds(pl.multiple_of((begin + j) * 16, 16), 16)
                there = pl.ds(pl.multiple_of((goal + j) * 16, 16), 16)
                out_ref[e, there, :] = local[here, :]
                return carry

            lax.fori_loop(0, plan_ref[at], move, 0)

    return pl.pallas_call(
        kernel,
        grid_spec=pltpu.PrefetchScalarGridSpec(
            num_scalar_prefetch=1,
            grid=(blocks,),
            in_specs=[
                pl.BlockSpec((1, 2, BLOCK), lambda b, plan: (b, 0, 0)),
                pl.BlockSpec((BLOCK, cols), lambda b, plan: (jnp.minimum(b, blocks // 2 - 1), 0)),
                pl.BlockSpec((BLOCK, cols), lambda b, plan: (jnp.maximum(b - blocks // 2, 0), 0)),
                pl.BlockSpec((BLOCK, 2), lambda b, plan: (b, 0)),
                pl.BlockSpec(router.shape, lambda b, plan: (0, 0)),
            ],
            out_specs=[
                pl.BlockSpec((expert_count, ROOM, both), lambda b, plan: (0, 0, 0)),
                pl.BlockSpec((BLOCK, extra), lambda b, plan: (b, 0)),
                pl.BlockSpec((BLOCK, extra), lambda b, plan: (b, 0)),
            ],
            scratch_shapes=[pltpu.VMEM((LOCAL, both), jnp.bfloat16)],
        ),
        out_shape=[
            jax.ShapeDtypeStruct((expert_count, ROOM, both), jnp.bfloat16),
            jax.ShapeDtypeStruct((blocks * BLOCK, extra), jnp.float32),
            jax.ShapeDtypeStruct((blocks * BLOCK, extra), jnp.bfloat16),
        ],
        compiler_params=pltpu.CompilerParams(vmem_limit_bytes=VMEM),
        cost_estimate=cost(20),
        name="gated_spread",
    )(plan, rows, own, other, chosen, router)


def collect(buffers, columns, plan, kept, after):
    each, room, cols = buffers[0].shape
    expert_count = each * len(buffers)
    blocks = columns.shape[0] // BLOCK
    extra = cols - kept

    def kernel(plan_ref, columns_ref, *refs):
        held, refs = refs[: len(buffers)], refs[len(buffers) + len(after) :]
        own_ref, other_ref, local = refs[0], refs[1], refs[-1]
        block = pl.program_id(0)
        mine = block < blocks // 2

        @pl.when(block == 0)
        def _():
            local[...] = jnp.zeros_like(local)

        for e in range(expert_count):
            at = block * expert_count + e
            size = blocks * expert_count
            begin, goal = plan_ref[size + at], plan_ref[2 * size + at]

            def move(j, carry):
                here = pl.ds(pl.multiple_of((begin + j) * 16, 16), 16)
                there = pl.ds(pl.multiple_of((goal + j) * 16, 16), 16)
                local[here, :] = held[e // each][e % each, there, :]
                return carry

            lax.fori_loop(0, plan_ref[at], move, 0)
        part = BLOCK // 2
        for i in range(2):
            rows = pl.ds(i * part, part)
            slot = lax.broadcasted_iota(jnp.int32, (part, LOCAL), 1)
            hot = (slot == columns_ref[rows, 0:1]) | (slot == columns_ref[rows, 1:2])
            total = jnp.dot(
                jnp.where(hot, 1.0, 0.0).astype(jnp.bfloat16),
                local[...],
                preferred_element_type=jnp.float32,
            )
            low = total[:, :kept].astype(jnp.bfloat16)

            @pl.when(mine)
            def _():
                own_ref[rows, :] = low

            @pl.when(jnp.logical_not(mine))
            def _():
                other_ref[rows, :] = low

            if extra:
                refs[2][rows, :] = total[:, kept:]

    out_specs = [
        pl.BlockSpec((BLOCK, kept), lambda b, plan: (jnp.minimum(b, blocks // 2 - 1), 0)),
        pl.BlockSpec((BLOCK, kept), lambda b, plan: (jnp.maximum(b - blocks // 2, 0), 0)),
    ]
    out_shape = [jax.ShapeDtypeStruct((blocks // 2 * BLOCK, kept), jnp.bfloat16)] * 2
    if extra:
        out_specs.append(pl.BlockSpec((BLOCK, extra), lambda b, plan: (b, 0)))
        out_shape.append(jax.ShapeDtypeStruct((blocks * BLOCK, extra), jnp.float32))
    return pl.pallas_call(
        kernel,
        grid_spec=pltpu.PrefetchScalarGridSpec(
            num_scalar_prefetch=1,
            grid=(blocks,),
            in_specs=[
                pl.BlockSpec((BLOCK, 2), lambda b, plan: (b, 0)),
            ]
            + [pl.BlockSpec((each, room, cols), lambda b, plan: (0, 0, 0))] * len(buffers)
            + [pl.BlockSpec(memory_space=pl.ANY)] * len(after),
            out_specs=out_specs,
            scratch_shapes=[pltpu.VMEM((LOCAL, cols), jnp.bfloat16)],
        ),
        out_shape=out_shape,
        compiler_params=pltpu.CompilerParams(vmem_limit_bytes=VMEM),
        cost_estimate=cost(16),
        name="collect",
    )(plan, columns, *buffers, *after)


GELU_A = 0.7978845608028654
GELU_B = 0.044715


def expert_pass(inputs, grads, up_weight, up_bias, down_weight, tiles, first, count, after):
    expert_count, room, cols = inputs.shape
    width, hidden = up_weight.shape[1:]

    def kernel(
        tiles_ref, x_ref, g_ref, up_ref, bias_ref, down_ref, *refs
    ):
        y_ref, dx_ref, dup_ref, ddown_ref, dbias_ref, mixed, dpre = refs[len(after) :]
        step = pl.program_id(0)
        expert = step + first

        @pl.when(step == 0)
        def _():
            mixed[...] = jnp.zeros_like(mixed)
            dpre[...] = jnp.zeros_like(dpre)

        dbias_ref[...] = jnp.zeros_like(dbias_ref)
        lane = lax.broadcasted_iota(jnp.int32, (TILE, cols - width), 1)

        def tile(r, carry):
            rows = pl.ds(pl.multiple_of(r * TILE, TILE), TILE)
            x = x_ref[0, rows, :width]
            g = g_ref[0, rows, :]
            gates = x_ref[0, rows, width:].astype(jnp.float32)
            own = (lane == expert) | (lane == expert + expert_count)
            mix = jnp.sum(jnp.where(own, gates, 0.0), axis=1, keepdims=True)
            pre = jnp.dot(x, up_ref[0], preferred_element_type=jnp.float32)
            pre = pre + bias_ref[0].astype(jnp.float32)
            back = lax.dot_general(
                g, down_ref[0], (((1,), (1,)), ((), ())), preferred_element_type=jnp.float32
            )
            square = pre * pre
            bend = jnp.tanh(pre * (GELU_A + GELU_A * GELU_B * square))
            upper = 0.5 + 0.5 * bend
            act = pre * upper
            slope = upper + 0.5 * pre * (1.0 - bend * bend) * (
                GELU_A + 3.0 * GELU_A * GELU_B * square
            )
            dot = jnp.sum(act * back, axis=1, keepdims=True)
            act_low = (mix * act).astype(jnp.bfloat16)
            down = (mix * back * slope).astype(jnp.bfloat16)
            mixed[rows, :] = act_low
            dpre[rows, :] = down
            dbias_ref[0] += jnp.sum(down.astype(jnp.float32), axis=0, keepdims=True)
            y_ref[0, rows, :] = jnp.dot(
                act_low, down_ref[0], preferred_element_type=jnp.float32
            ).astype(jnp.bfloat16)
            dx_ref[0, rows, :width] = lax.dot_general(
                down, up_ref[0], (((1,), (1,)), ((), ())), preferred_element_type=jnp.float32
            ).astype(jnp.bfloat16)
            high = dot.astype(jnp.bfloat16).astype(jnp.float32)
            dx_ref[0, rows, width:] = jnp.where(
                lane == expert, high, jnp.where(lane == expert + expert_count, dot - high, 0.0)
            ).astype(jnp.bfloat16)
            return carry

        lax.fori_loop(0, tiles_ref[expert], tile, 0)

        def weights(depth):
            rows = pl.ds(0, depth)
            for i in range(width // TILE):
                part = pl.ds(i * TILE, TILE)
                dup_ref[0, part, :] = lax.dot_general(
                    x_ref[0, rows, part], dpre[rows, :], (((0,), (0,)), ((), ())),
                    preferred_element_type=jnp.float32,
                ).astype(jnp.bfloat16)
                ddown_ref[0, part, :] = lax.dot_general(
                    g_ref[0, rows, part], mixed[rows, :], (((0,), (0,)), ((), ())),
                    preferred_element_type=jnp.float32,
                ).astype(jnp.bfloat16)

        pl.when(tiles_ref[expert] <= 3)(lambda: weights(3 * TILE))
        pl.when(tiles_ref[expert] > 3)(lambda: weights(room))

    def whole(*dims):
        return pl.BlockSpec((1, *dims), lambda e, tiles: (e + first, 0, 0))

    def own(*dims):
        return pl.BlockSpec((1, *dims), lambda e, tiles: (e, 0, 0))

    shapes = [
        ((room, width), jnp.bfloat16),
        ((room, cols), jnp.bfloat16),
        ((width, hidden), jnp.bfloat16),
        ((width, hidden), jnp.bfloat16),
        ((1, hidden), jnp.float32),
    ]
    return pl.pallas_call(
        kernel,
        grid_spec=pltpu.PrefetchScalarGridSpec(
            num_scalar_prefetch=1,
            grid=(count,),
            in_specs=[
                whole(room, cols),
                whole(room, width),
                whole(width, hidden),
                whole(1, hidden),
                whole(hidden, width),
            ]
            + [pl.BlockSpec(memory_space=pl.ANY)] * len(after),
            out_specs=[own(*dims) for dims, _ in shapes],
            scratch_shapes=[pltpu.VMEM((room, hidden), jnp.bfloat16)] * 2,
        ),
        out_shape=[jax.ShapeDtypeStruct((count, *dims), kind) for dims, kind in shapes],
        compiler_params=pltpu.CompilerParams(vmem_limit_bytes=VMEM),
        cost_estimate=pl.CostEstimate(
            flops=count * 12 * 768 * width * hidden,
            bytes_accessed=count * (4 * room * (cols + width) + 8 * width * hidden),
            transcendentals=count * 768 * hidden,
        ),
        name="experts",
    )(tiles, inputs, grads, up_weight, up_bias[:, None, :], down_weight, *after)


def call(kernel, name, grid, ins, outs, after=(), scratch=(), us=5, each=1, turn=None):
    turn = jnp.zeros((1,), jnp.int32) if turn is None else turn

    def spec(shape, split):
        zeros = (0,) * (len(shape) - 1)
        if split == "turned":
            return pl.BlockSpec((each, *shape[1:]), lambda i, t: ((i + t[0]) % grid, *zeros))
        if split == "low":
            return pl.BlockSpec(
                (each, *shape[1:]), lambda i, t: (jnp.minimum(i, grid // 2 - 1), *zeros)
            )
        if split == "high":
            return pl.BlockSpec(
                (each, *shape[1:]), lambda i, t: (jnp.maximum(i - grid // 2, 0), *zeros)
            )
        if split:
            return pl.BlockSpec((each, *shape[1:]), lambda i, t: (i, *zeros))
        return pl.BlockSpec(tuple(shape), lambda i, t: (0, *zeros))

    count, late = len(ins), len(after)

    def body(turn_ref, *refs):
        kernel(*refs[:count], *refs[count + late :])

    return pl.pallas_call(
        body,
        grid_spec=pltpu.PrefetchScalarGridSpec(
            num_scalar_prefetch=1,
            grid=(grid,),
            in_specs=[spec(a.shape, split) for a, split in ins]
            + [pl.BlockSpec(memory_space=pl.ANY)] * late,
            out_specs=[spec(a.shape, split) for a, split in outs],
            scratch_shapes=list(scratch),
        ),
        out_shape=[a for a, _ in outs],
        compiler_params=pltpu.CompilerParams(vmem_limit_bytes=VMEM),
        cost_estimate=cost(us),
        name=name,
    )(turn, *[a for a, _ in ins], *after)


def shape_of(dims, kind):
    return jax.ShapeDtypeStruct(tuple(dims), kind)


def normal(x):
    centered = x - jnp.mean(x, axis=-1, keepdims=True)
    spread_of = lax.rsqrt(jnp.mean(centered * centered, axis=-1, keepdims=True) + EPSILON)
    return centered * spread_of, spread_of


def contract(left, right, left_dim, right_dim):
    return lax.dot_general(
        left, right, (((left_dim,), (right_dim,)), ((), ())), preferred_element_type=jnp.float32
    )


def head_masks(width):
    lane = lax.broadcasted_iota(jnp.int32, (1, width), 1)
    return [(lane >= h * HD) & (lane < (h + 1) * HD) for h in range(width // HD)]


def head_probs(q, k, mask):
    own = jnp.where(mask, q, jnp.zeros_like(q)) * jnp.bfloat16(HD ** (-0.5))
    scores = contract(own, k, 1, 1)
    column = lax.broadcasted_iota(jnp.int32, scores.shape, 1)
    scores = jnp.where(column < SEQ, scores, -1e30)
    raised = jnp.exp(scores - jnp.max(scores, axis=-1, keepdims=True))
    return raised * (1.0 / jnp.sum(raised, axis=-1, keepdims=True))


def attention_forward(x, turn, gain, shift, weight, bias, out_weight):
    images, seq, width = x.shape
    rows, inner = ROWS, weight.shape[2]
    blocks = images // PAIR

    def kernel(
        turn_ref, x_ref, gain_ref, shift_ref, w_ref, b_ref, wo_ref,
        *refs
    ):
        own_ref, other_ref, pad_ref, n_ref, q_ref, k_ref, v_ref, o_ref, held = refs
        held[...] = jnp.zeros_like(held)
        for i in range(PAIR):
            held[i, :seq, :] = x_ref[i].astype(jnp.float32)
        value = held[...].reshape(PAIR * rows, width)
        pad_ref[...] = value.astype(jnp.bfloat16).reshape(PAIR, rows, width)
        n = (normal(value)[0] * gain_ref[...] + shift_ref[...]).astype(jnp.bfloat16)
        n_ref[...] = n.reshape(PAIR, rows, width)
        for j, ref in enumerate((q_ref, k_ref, v_ref)):
            made = jnp.dot(n, w_ref[j], preferred_element_type=jnp.float32) + b_ref[j : j + 1, :]
            ref[...] = made.astype(jnp.bfloat16).reshape(PAIR, rows, inner)
        for i in range(PAIR):
            q, k, v = q_ref[i], k_ref[i], v_ref[i]
            mixed = jnp.zeros((rows, inner), jnp.float32)
            for mask in head_masks(inner):
                probs = head_probs(q, k, mask).astype(jnp.bfloat16)
                head = jnp.dot(probs, v, preferred_element_type=jnp.float32)
                mixed = jnp.where(mask, head, mixed)
            o_ref[i] = mixed.astype(jnp.bfloat16)
        mixed = o_ref[...].reshape(PAIR * rows, inner)
        part = jnp.dot(mixed, wo_ref[...], preferred_element_type=jnp.float32)
        part = part.astype(jnp.bfloat16).reshape(PAIR, rows, width)

        @pl.when(pl.program_id(0) < blocks // 2)
        def _():
            other_ref[...] = part

        @pl.when(pl.program_id(0) >= blocks // 2)
        def _():
            own_ref[...] = part


    wide = shape_of((images, rows, width), jnp.bfloat16)
    slim = shape_of((images, rows, inner), jnp.bfloat16)
    def place(i, turn):
        return ((i + blocks // 2) % blocks, 0, 0)

    def whole(array):
        return pl.BlockSpec(array.shape, lambda i, turn: (0,) * array.ndim)

    small = (gain, shift, weight, bias, out_weight)
    return pl.pallas_call(
        kernel,
        grid_spec=pltpu.PrefetchScalarGridSpec(
            num_scalar_prefetch=1,
            grid=(blocks,),
            in_specs=[
                pl.BlockSpec(
                    (PAIR, seq, width), lambda i, turn: ((i + blocks // 2 + turn[0]) % blocks, 0, 0)
                )
            ]
            + [whole(array) for array in small],
            out_specs=[
                pl.BlockSpec(
                    (PAIR, rows, width), lambda i, turn: (jnp.maximum(i - blocks // 2, 0), 0, 0)
                ),
                pl.BlockSpec(
                    (PAIR, rows, width), lambda i, turn: (jnp.minimum(i, blocks // 2 - 1), 0, 0)
                ),
            ]
            + [pl.BlockSpec((PAIR, *a.shape[1:]), place) for a in [wide] * 2 + [slim] * 4],
            scratch_shapes=[pltpu.VMEM((PAIR, rows, width), jnp.float32)],
        ),
        out_shape=[shape_of((images // 2, rows, width), jnp.bfloat16)] * 2 + [wide] * 2 + [slim] * 4,
        compiler_params=pltpu.CompilerParams(vmem_limit_bytes=VMEM),
        cost_estimate=cost(18),
        name="attention_forward",
    )(turn, x, *small)


def attention_backward(own_da, other_da, x, n, q, k, v, o, weight, out_weight, after):
    images, rows, width = x.shape
    inner = weight.shape[2]

    def kernel(
        own_ref, other_ref, x_ref, n_ref, q_ref, k_ref, v_ref, o_ref, w_ref, wo_ref,
        own_back_ref, other_back_ref, dw_ref, dwo_ref, dbias_ref, sums_ref, held,
    ):
        @pl.when(pl.program_id(0) == 0)
        def _():
            dw_ref[...] = jnp.zeros_like(dw_ref)
            dwo_ref[...] = jnp.zeros_like(dwo_ref)
            dbias_ref[...] = jnp.zeros_like(dbias_ref)
            sums_ref[...] = jnp.zeros_like(sums_ref)

        joined = PAIR * rows
        mine = pl.program_id(0) < images // PAIR // 2
        da = jnp.where(mine, own_ref[...], other_ref[...]).reshape(joined, width)
        do_all = contract(da, wo_ref[...], 1, 1).astype(jnp.bfloat16).reshape(PAIR, rows, inner)
        scale = HD ** (-0.5)
        for i in range(PAIR):
            q, k, v, do = q_ref[i], k_ref[i], v_ref[i], do_all[i]
            dq = dk = dv = jnp.zeros((rows, inner), jnp.float32)
            for mask in head_masks(inner):
                probs = head_probs(q, k, mask)
                dv = jnp.where(mask, contract(probs.astype(jnp.bfloat16), do, 0, 0), dv)
                dp = contract(jnp.where(mask, do, jnp.zeros_like(do)), v, 1, 1)
                ds = probs * (dp - jnp.sum(probs * dp, axis=-1, keepdims=True))
                ds = ds.astype(jnp.bfloat16)
                dq = jnp.where(mask, jnp.dot(ds, k, preferred_element_type=jnp.float32), dq)
                dk = jnp.where(mask, contract(ds, q, 0, 0), dk)
            held[0, i] = (dq * scale).astype(jnp.bfloat16)
            held[1, i] = (dk * scale).astype(jnp.bfloat16)
            held[2, i] = dv.astype(jnp.bfloat16)
        n = n_ref[...].reshape(joined, width)
        back = jnp.zeros((joined, width), jnp.float32)
        for j in range(3):
            grad = held[j].reshape(joined, inner)
            dw_ref[j] += contract(n, grad, 0, 0)
            back += contract(grad, w_ref[j], 1, 1)
            if j != 1:
                dbias_ref[j // 2 : j // 2 + 1, :] += jnp.sum(
                    grad.astype(jnp.float32), axis=0, keepdims=True
                )
        dwo_ref[0] += contract(da, o_ref[...].reshape(joined, inner), 0, 0)
        back_low = back.astype(jnp.bfloat16).reshape(PAIR, rows, width)

        @pl.when(mine)
        def _():
            own_back_ref[...] = back_low

        @pl.when(jnp.logical_not(mine))
        def _():
            other_back_ref[...] = back_low

        unit, _ = normal(x_ref[...].reshape(joined, width).astype(jnp.float32))
        sums_ref[0:1, :] += jnp.sum(back * unit, axis=0, keepdims=True)
        sums_ref[1:2, :] += jnp.sum(back, axis=0, keepdims=True)
        sums_ref[2:3, :] += jnp.sum(da.astype(jnp.float32), axis=0, keepdims=True)

    return call(
        kernel, "attention_backward", images // PAIR,
        [(own_da, "low"), (other_da, "high")]
        + [(a, True) for a in (x, n, q, k, v, o)] + [(weight, False), (out_weight, False)],
        [
            (shape_of((images // 2, rows, width), jnp.bfloat16), "low"),
            (shape_of((images // 2, rows, width), jnp.bfloat16), "high"),
            (shape_of((3, width, inner), jnp.float32), False),
            (shape_of((1, width, inner), jnp.float32), False),
            (shape_of((2, inner), jnp.float32), False),
            (shape_of((3, width), jnp.float32), False),
        ],
        after=after, each=PAIR, us=30,
        scratch=[pltpu.VMEM((3, PAIR, rows, inner), jnp.bfloat16)],
    )


def middle_norm(near, far, x, out_bias, gain, shift, after):
    def kernel(near_ref, far_ref, x_ref, bias_ref, gain_ref, shift_ref, middle_ref, n_ref):
        total = near_ref[0].astype(jnp.float32) + far_ref[0].astype(jnp.float32)
        middle = x_ref[0].astype(jnp.float32) + total + bias_ref[...]
        middle_ref[0] = middle
        n_ref[0] = (normal(middle)[0] * gain_ref[...] + shift_ref[...]).astype(jnp.bfloat16)

    return call(
        kernel, "middle_norm", near.shape[0],
        [(near, True), (far, True), (x, True), (out_bias, False), (gain, False), (shift, False)],
        [(shape_of(near.shape, jnp.float32), True), (shape_of(near.shape, jnp.bfloat16), True)],
        after=after, us=8,
    )


def norm_back(dn, unit, spread_of, gain):
    dz = dn * gain
    mean = jnp.mean(dz, axis=-1, keepdims=True)
    return spread_of * (dz - mean - unit * jnp.mean(dz * unit, axis=-1, keepdims=True))


def middle_back(near, far, dots, gates, chosen, pair, n, router_weight, down_bias, middle, upstream, gain, after):
    count, wide = down_bias.shape[0], pair.shape[2]

    def kernel(
        near_ref, far_ref, dots_ref, gates_ref, chosen_ref, pair_ref, n_ref, router_ref, bias_ref,
        middle_ref, g_ref, gain_ref, grad_ref, da_ref, sums_ref, drouter_ref, dbias_ref,
    ):
        @pl.when(pl.program_id(0) == 0)
        def _():
            sums_ref[...] = jnp.zeros_like(sums_ref)
            drouter_ref[...] = jnp.zeros_like(drouter_ref)
            dbias_ref[...] = jnp.zeros_like(dbias_ref)

        g = g_ref[0]
        lane = lax.broadcasted_iota(jnp.int32, (g.shape[0], count), 1)
        named = (lane == chosen_ref[0, :, 0:1]) | (lane == chosen_ref[0, :, 1:2])
        dmix = dots_ref[0] + jnp.where(named, contract(g, bias_ref[...], 1, 1), 0.0)
        gate = gates_ref[0, :, :count]
        dlogits = gate * (dmix - jnp.sum(gate * dmix, axis=-1, keepdims=True))
        dlogits = dlogits.astype(jnp.bfloat16)
        drouter_ref[...] += contract(dlogits, n_ref[0], 0, 0)
        dbias_ref[...] += contract(pair_ref[0], g, 0, 0)
        dn = near_ref[0].astype(jnp.float32) + far_ref[0].astype(jnp.float32)
        dn = dn + contract(dlogits, router_ref[...], 1, 1)
        unit, spread_of = normal(middle_ref[0])
        grad = g.astype(jnp.float32) + norm_back(dn, unit, spread_of, gain_ref[...])
        grad_ref[0] = grad
        da_ref[0] = grad.astype(jnp.bfloat16)
        sums_ref[0:1, :] += jnp.sum(dn * unit, axis=0, keepdims=True)
        sums_ref[1:2, :] += jnp.sum(dn, axis=0, keepdims=True)

    width = middle.shape[2]
    return call(
        kernel, "middle_back", middle.shape[0],
        [(a, True) for a in (near, far, dots, gates, chosen, pair, n)]
        + [(router_weight, False), (down_bias, False), (middle, True), (upstream, True), (gain, False)],
        [
            (shape_of(middle.shape, jnp.float32), True),
            (shape_of(middle.shape, jnp.bfloat16), True),
            (shape_of((2, width), jnp.float32), False),
            (shape_of((count, width), jnp.float32), False),
            (shape_of((wide, width), jnp.float32), False),
        ],
        after=after, us=8,
    )


def finish(near, far, middle, pair, down_bias, after):
    def kernel(near_ref, far_ref, middle_ref, pair_ref, bias_ref, out_ref):
        total = near_ref[0].astype(jnp.float32) + far_ref[0].astype(jnp.float32)
        total = total + jnp.dot(pair_ref[0], bias_ref[...], preferred_element_type=jnp.float32)
        out_ref[0] = (middle_ref[0] + total).astype(jnp.bfloat16)

    return call(
        kernel, "finish", middle.shape[0],
        [(near, True), (far, True), (middle, True), (pair, True), (down_bias, False)],
        [(shape_of(middle.shape, jnp.bfloat16), True)],
        after=after, us=8,
    )[0]


def input_back(own, other, x, own_grad, other_grad, gain, turn, after):
    images, _, width = x.shape
    half = images // 2

    def kernel(turn_ref, own_ref, other_ref, x_ref, own_grad_ref, other_grad_ref, gain_ref, *refs):
        out_ref = refs[-1]
        step = pl.program_id(0)
        place = (step + turn_ref[0]) % images
        mine = step < half
        dn = jnp.where(mine, own_ref[0], other_ref[0]).astype(jnp.float32)
        unit, spread_of = normal(x_ref[0].astype(jnp.float32))
        grad = jnp.where(mine, own_grad_ref[0], other_grad_ref[0])
        grad = grad + norm_back(dn, unit, spread_of, gain_ref[...])
        for j in range(images):

            @pl.when(place == j)
            def _():
                out_ref[j * SEQ : (j + 1) * SEQ, :] = grad[:SEQ]

    def low(shape):
        return pl.BlockSpec((1, *shape[1:]), lambda i, t: (jnp.minimum(i, half - 1), 0, 0))

    def high(shape):
        return pl.BlockSpec((1, *shape[1:]), lambda i, t: (jnp.maximum(i - half, 0), 0, 0))

    return pl.pallas_call(
        kernel,
        grid_spec=pltpu.PrefetchScalarGridSpec(
            num_scalar_prefetch=1,
            grid=(images,),
            in_specs=[
                low(own.shape),
                high(other.shape),
                pl.BlockSpec((1, *x.shape[1:]), lambda i, t: (i, 0, 0)),
                low(own_grad.shape),
                high(other_grad.shape),
                pl.BlockSpec(gain.shape, lambda i, t: (0, 0)),
            ]
            + [pl.BlockSpec(memory_space=pl.ANY)] * len(after),
            out_specs=pl.BlockSpec((images * SEQ, width), lambda i, t: (0, 0)),
        ),
        out_shape=jax.ShapeDtypeStruct((images * SEQ, width), jnp.float32),
        compiler_params=pltpu.CompilerParams(vmem_limit_bytes=VMEM),
        cost_estimate=cost(15),
        name="input_back",
    )(turn, own, other, x, own_grad, other_grad, gain, *after)


def to_core(value):
    return lax.ppermute(value, "tensor", pairs(lax.axis_size("tensor"), 1))


def across(value):
    return lax.ppermute(value, "tensor", pairs(lax.axis_size("tensor"), 2))


def core_sum(own, other, zero):
    got = to_core(other)
    return (own.astype(jnp.float32) + got.astype(jnp.float32) + zero).astype(jnp.bfloat16)


def zero_of(value):
    return value[(0,) * value.ndim].astype(jnp.float32) * 0.0


def ring_owner(way, step):
    index = lax.axis_index("dp")
    place = jnp.where(index % 2 == 0, index // 2, 7 - index // 2)
    place = (place - way * (step + 1)) % 8
    return jnp.where(place < 4, 2 * place, 15 - 2 * place).astype(jnp.int32)


def ring_hop(value, way):
    path = [(RING[i], RING[(i + way) % len(RING)]) for i in range(len(RING))]
    return lax.ppermute(value, "dp", path)


def ring_add(got, sources, steps, kinds, after, carry=()):
    groups, came = len(sources), got[0].shape[0]
    many, total, cols = sources[0][0].shape
    rows, part = total // 8, 2
    owners = jnp.stack([ring_owner(way, step) for step in steps for way in (1, -1)])
    joint = all(kind == kinds[0] for kind in kinds)

    def kernel(owners_ref, *refs):
        held, locals_ = refs[:2], refs[2 : 2 + 2 * groups]
        outs = refs[2 + 2 * groups + len(after) + len(carry) :]
        for g in range(groups):
            for d in range(2):
                value = locals_[2 * g + d][...]
                if g < came:
                    value = value.astype(jnp.float32) + held[d][g].astype(jnp.float32)
                if joint:
                    outs[d][g] = value.astype(kinds[g])
                else:
                    outs[2 * g + d][0] = value.astype(kinds[g])

    def source(slot):
        return pl.BlockSpec((part, rows, cols), lambda i, own: (i, own[slot], 0))

    def stack(count):
        return pl.BlockSpec((count, part, rows, cols), lambda i, own: (0, i, 0, 0))

    if joint:
        outs = [((groups, many, rows, cols), kinds[0])] * 2
    else:
        outs = [((1, many, rows, cols), kind) for kind in kinds for _ in range(2)]
    return pl.pallas_call(
        kernel,
        grid_spec=pltpu.PrefetchScalarGridSpec(
            num_scalar_prefetch=1,
            grid=(many // part,),
            in_specs=[stack(came)] * 2
            + [source(i) for i in range(2 * groups)]
            + [pl.BlockSpec(memory_space=pl.ANY)] * (len(after) + len(carry)),
            out_specs=[stack(dims[0]) for dims, _ in outs]
            + [pl.BlockSpec(memory_space=pl.ANY)] * len(carry),
        ),
        out_shape=[jax.ShapeDtypeStruct(dims, kind) for dims, kind in outs]
        + [jax.ShapeDtypeStruct(value.shape, value.dtype) for value in carry],
        input_output_aliases={
            3 + 2 * groups + len(after) + i: len(outs) + i for i in range(len(carry))
        },
        compiler_params=pltpu.CompilerParams(vmem_limit_bytes=VMEM),
        cost_estimate=cost(5),
        name="ring_add",
    )(owners, *got, *[piece for pair in sources for piece in pair], *after, *carry)


def on_device(
    embedded,
    attn_gain,
    attn_shift,
    qkv_weight,
    qv_bias,
    out_weight,
    out_bias,
    moe_gain,
    moe_shift,
    router_weight,
    up_weight,
    up_bias,
    down_weight,
    down_bias,
    routes,
    cotangent,
):
    tok_rows, width = embedded.shape
    images = tok_rows // SEQ
    half = images // 2
    head_width = qkv_weight.shape[2]
    expert_count = up_weight.shape[0]
    core = lax.axis_index("tensor") % 2
    f32 = jnp.float32

    def own_first(value, fill):
        value = value.reshape(images, SEQ, value.shape[1])
        value = jnp.pad(value, ((0, 0), (0, ROWS - SEQ), (0, 0)), constant_values=fill)
        return jnp.where(core == 0, value, jnp.roll(value, half, axis=0))

    def in_order(own, other):
        low = jnp.where(core == 0, own, other)
        high = jnp.where(core == 0, other, own)
        return jnp.concatenate([low, high])[:, :SEQ].reshape(tok_rows, width)

    def row(value):
        return value.astype(f32)[None]

    def imaged(value):
        return value.reshape(-1, ROWS, value.shape[1])

    turn = (half * core).astype(jnp.int32)[None]
    bias_rows = jnp.stack([qv_bias[0], jnp.zeros_like(qv_bias[0]), qv_bias[1]]).astype(f32)
    images_in = embedded.reshape(images, SEQ, width)
    own, other, x, normed, queries, keys, values, mixed = attention_forward(
        images_in, turn // PAIR, row(attn_gain), row(attn_shift), qkv_weight, bias_rows, out_weight
    )
    near = core_sum(own, other, 0.0)
    far = across(near)

    near_zero = zero_of(near)
    chosen = own_first(routes + near_zero.astype(jnp.int32), -1).reshape(images * ROWS, 2)
    rows, columns, plan, tiles = route_plan(chosen, expert_count)
    upstream = own_first(cotangent, 0) + near_zero.astype(jnp.bfloat16)
    grad_buffers = spread(upstream.reshape(images * ROWS, width), rows, plan, expert_count)

    extra = 128
    router_twice = jnp.pad(
        jnp.concatenate([router_weight, router_weight], axis=1),
        ((0, 0), (0, extra - 2 * expert_count)),
    )
    bias_twice = jnp.pad(
        jnp.concatenate([down_bias, down_bias]), ((0, extra - 2 * expert_count), (0, 0))
    )
    middle, own_normed = middle_norm(
        near, far, x, row(out_bias), row(moe_gain), row(moe_shift),
        (grad_buffers, router_twice, bias_twice, tiles),
    )
    own_rows = half * ROWS
    buffers, gates, mix_pair = gated_spread(
        own_normed.reshape(own_rows, width), to_core(own_normed).reshape(own_rows, width),
        rows, plan, chosen, router_twice, expert_count, extra,
    )
    gates, mix_pair, chosen = imaged(gates), imaged(mix_pair), imaged(chosen)
    group = expert_count // GROUPS

    def experts_of(i, after):
        return expert_pass(
            buffers, grad_buffers, up_weight, up_bias, down_weight, tiles, i * group, group, after
        )

    ringed = lax.axis_size("dp") == len(RING)
    low = jnp.bfloat16
    y_first, back_first, *first, bias_first = experts_of(0, ())
    moving = ()
    if ringed:
        rows_each = width // 8
        moving = [
            lax.dynamic_slice_in_dim(grad, ring_owner(way, 0) * rows_each, rows_each, 1)[None]
            for grad, way in zip(first, (1, -1))
        ]
    y_second, back_second, *second, bias_second = experts_of(1, tuple(moving))

    def round_trip(step, kinds, after=(), carry=()):
        if not ringed:
            return carry
        got = [ring_hop(value, way) for value, way in zip(moving, (1, -1))]
        if step < 8:
            return ring_add(got, [first, second], [step, step - 1], kinds, after, carry)
        return ring_add(got, [second], [step - 1], kinds, after, carry)

    moving = round_trip(1, [low, low])
    own, other, dots = collect((back_first, back_second), columns, plan, width, tuple(moving))
    *moving, own, other = round_trip(2, [low, low], (), (own, other))
    back_near = core_sum(imaged(own), imaged(other), 0.0)
    back_far = across(back_near)
    dots = dots[:, : 2 * expert_count].T + zero_of(own)
    dots = dots[:expert_count] + dots[expert_count:]
    dots = dots[:, :own_rows] + to_core(dots[:, own_rows:])
    dots = (dots + across(dots)).T.reshape(half, ROWS, expert_count)
    own_y, other_y = collect((y_first, y_second), columns, plan, width, (back_near, *moving))
    moving = round_trip(3, [low, low], (other_y,))
    middle_grad, own_da, moe_sums, router_sums, bias_sums = middle_back(
        back_near, back_far, dots, gates, chosen, mix_pair, own_normed, router_weight,
        down_bias, middle, upstream, row(moe_gain), tuple(moving),
    )
    *moving, own_da = round_trip(4, [low, low], (), (own_da,))
    other_da, other_grad = to_core(own_da), to_core(middle_grad)
    y_near = core_sum(imaged(own_y), imaged(other_y), zero_of(own_da))
    y_far = across(y_near)
    own, other, grad_qkv, grad_out, grad_qv_bias, sums = attention_backward(
        own_da, other_da, x, normed, queries, keys, values, mixed, qkv_weight, out_weight,
        (y_near, *moving),
    )
    *moving, own, other = round_trip(5, [low, low], (y_far,), (own, other))
    last_near = core_sum(own, other, 0.0)
    last_far = across(last_near)

    def after_round(value):
        return value + zero_of(moving[1]).astype(value.dtype) if ringed else value

    def meet(value, axis, bit):
        return value + lax.ppermute(value, axis, pairs(lax.axis_size(axis), bit))

    def halve(values, bit, axis):
        mine = (lax.axis_index("dp") >> bit) % 2
        keep = lax.dynamic_index_in_dim(values, mine, axis, keepdims=True)
        give = lax.dynamic_index_in_dim(values, 1 - mine, axis, keepdims=True).astype(low)
        return keep, lax.ppermute(give, "dp", pairs(8, 1 << bit))

    moving = round_trip(6, [low, low], (last_near,))
    own_out = finish(y_near, y_far, middle, mix_pair, bias_twice, tuple(moving))
    layer_out = in_order(own_out, to_core(own_out))
    router_bias = [router_sums, bias_sums[:expert_count] + bias_sums[expert_count : 2 * expert_count]]
    packed = jnp.concatenate(
        [
            sums[:2],
            0.5 * moe_sums,
            *[0.5 * part for part in router_bias],
            sums[2:],
            jnp.pad(grad_qv_bias, ((0, 0), (0, width - head_width))),
            bias_first[:, 0],
            bias_second[:, 0],
        ]
    )
    slim = jnp.concatenate([grad_qkv, grad_out])
    base = 4 + 2 * expert_count
    last = (last_near.astype(f32) + last_far.astype(f32)).astype(low)
    other_last = to_core(last)

    def input_grad():
        return input_back(
            last, other_last, x, middle_grad, other_grad, row(attn_gain), turn, tuple(moving)
        )

    if ringed:
        slim = slim.reshape(4, 2, 2, 2, width // 8, head_width)
        packed = after_round(packed)
        for step, bit, axis in ((7, 0, 3), (8, 1, 2), (9, 2, 1)):
            keep, got = halve(after_round(slim), bit, axis)
            sent = lax.ppermute(packed, "dp", pairs(8, 1 << bit))
            if step == 7:
                up_first, down_first, *moving = round_trip(7, [f32, low], (layer_out,))
            elif step == 8:
                moving = round_trip(8, [f32])
            slim = keep.astype(f32) + got.astype(f32)
            packed = after_round(packed + sent)
        grad_embedded = input_grad()
        up_second, down_second = moving
        slim = slim.reshape(4, width // 8, head_width)
    else:
        grad_embedded = input_grad()
        packed = lax.psum(packed, "dp")
        slim = lax.psum_scatter(slim, "dp", scatter_dimension=1, tiled=True)
        up_first, down_first, up_second, down_second = [
            lax.psum_scatter(grad, "dp", scatter_dimension=1, tiled=True).astype(f32)[None]
            for grad in (*first, *second)
        ]
    grad_up = jnp.concatenate([up_first[0], up_second[0]])
    grad_down = jnp.concatenate([down_first[0], down_second[0]]).transpose(0, 2, 1)
    tensor_parts = meet(meet(packed[:base], "tensor", 1), "tensor", 2)
    packed = jnp.concatenate([tensor_parts, packed[base:]])
    return (
        layer_out,
        grad_embedded,
        packed[0],
        packed[1],
        slim[:3],
        packed[base + 1 : base + 3, :head_width],
        slim[3].T,
        packed[base],
        packed[2],
        packed[3],
        packed[4 : 4 + expert_count].T,
        grad_up,
        packed[base + 3 :],
        grad_down,
        packed[4 + expert_count : base],
    )


def solution(mesh):
    return jax.shard_map(
        on_device,
        mesh=mesh,
        in_specs=(
            P("dp", None),
            P(),
            P(),
            P(None, None, "tensor"),
            P(None, "tensor"),
            P("tensor", None),
            P(),
            P(),
            P(),
            P(),
            P(None, None, "tensor"),
            P(None, "tensor"),
            P(None, "tensor", None),
            P(),
            P("dp", None),
            P("dp", None),
        ),
        out_specs=(
            P("dp", None),
            P("dp", None),
            P(),
            P(),
            P(None, "dp", "tensor"),
            P(None, "tensor"),
            P("tensor", "dp"),
            P(),
            P(),
            P(),
            P(),
            P(None, "dp", "tensor"),
            P(None, "tensor"),
            P(None, "tensor", "dp"),
            P(),
        ),
        check_vma=False,
    )
```
